32 devices in a mesh: dp: 8 (over y, x, core), tm: 4 (over z).
Axes of the slice: x: 2, y: 2, z: 4, core: 2. Of those that a mesh axis runs over, the one named last changes fastest.
Arguments:
- video: bfloat16 [24, 8, 16, 16, 2048], P('dp', 'tm'), may hold values from -6 to 6
- lengths: int32 [24], replicated, may hold values from 4 to 8, as said below
- mid_norms: float32 [4, 2, 512], replicated
- wide_norms: float32 [3, 2, 2048], replicated
- taps: float32 [3, 3, 128], replicated, may hold values from -2.5 to 2.5
- me_reduce: float32 [512, 32], replicated, may hold values from -0.25 to 0.25
- me_conv: float32 [3, 3, 32, 32], replicated, may hold values from -0.375 to 0.375
- me_expand: float32 [32, 512], replicated, may hold values from -6 to 6
- me_bias: float32 [512], replicated, may hold values from -3 to 3
- w_in1: float32 [2048, 512], P('dp', 'tm'), may hold values from -0.125 to 0.125
- w_mta: float32 [128, 3456], P('dp', 'tm'), may hold values from -0.1875 to 0.1875
- w_out1: float32 [512, 2048], P('dp', 'tm'), may hold values from -0.25 to 0.25
- w_in2: float32 [2048, 512], P('dp', 'tm'), may hold values from -0.125 to 0.125
- w_mid2: float32 [512, 4608], P('dp', 'tm'), may hold values from -0.09375 to 0.09375
- w_out2: float32 [512, 2048], P('dp', 'tm'), may hold values from -0.25 to 0.25
- w_proj: float32 [2048, 2048], P('dp', 'tm'), may hold values from -0.125 to 0.125
- grad_out: bfloat16 [24, 8, 8, 8, 2048], P('dp', 'tm'), may hold values from -6 to 6
Outputs:
- output: bfloat16 [24, 8, 8, 8, 2048], P('dp', 'tm')
- grad_video: bfloat16 [24, 8, 16, 16, 2048], P('dp', 'tm')
- grad_mid_norms: float32 [4, 2, 512], replicated
- grad_wide_norms: float32 [3, 2, 2048], replicated
- grad_taps: float32 [3, 3, 128], replicated
- grad_me_reduce: float32 [512, 32], replicated
- grad_me_conv: float32 [3, 3, 32, 32], replicated
- grad_me_expand: float32 [32, 512], replicated
- grad_me_bias: float32 [512], replicated
- grad_w_in1: float32 [2048, 512], P('dp', 'tm')
- grad_w_mta: float32 [128, 3456], P('dp', 'tm')
- grad_w_out1: float32 [512, 2048], P('dp', 'tm')
- grad_w_in2: float32 [2048, 512], P('dp', 'tm')
- grad_w_mid2: float32 [512, 4608], P('dp', 'tm')
- grad_w_out2: float32 [512, 2048], P('dp', 'tm')
- grad_w_proj: float32 [2048, 2048], P('dp', 'tm')
- rms: float32 [5], replicated
The draws below stay inside these ranges and needn't reach their ends.
Inputs may be any that keep to these rules, and one draw needn't show every extreme that they name: `lengths`: in each aligned block of 3 clips exactly one holds all 8 frames; the others hold 4 to 7.
All inputs are finite; a program needn't handle non-finite values.
Results may differ from the reference program's by a relative error of at most 0.034.
Values may be sent and summed in bfloat16 or wider, within the bound.
A program may use at most 256 MiB of HBM per device.

```python
import jax
import jax.numpy as jnp
from jax import lax

C = 2048
M = 512
R = 32
GW = 128
HW = 16
CLIPS_DEV = 3
FRAMES = 8
CLIPS = 24


def draw_lengths(key, part):
    key = jax.random.fold_in(key, 11)
    shorter = jax.random.randint(jax.random.fold_in(key, 1), (CLIPS,), FRAMES // 2, FRAMES)
    chosen = jax.random.randint(jax.random.fold_in(key, 2), (CLIPS // CLIPS_DEV,), 0, CLIPS_DEV)
    places = jnp.arange(CLIPS, dtype=jnp.int32)
    forced = places % CLIPS_DEV == jnp.repeat(chosen, CLIPS_DEV)
    return jnp.where(forced, FRAMES, shorter).astype(jnp.int32)


def norm_pairs(key, layers, channels):
    gains = jnp.exp(jax.random.uniform(jax.random.fold_in(key, 1), (layers, 1, channels), jnp.float32, -0.6, 0.6))
    biases = 0.5 * jax.random.normal(jax.random.fold_in(key, 2), (layers, 1, channels), jnp.float32)
    return jnp.concatenate([gains, biases], axis=1)


def draw_mid_norms(key, part):
    key = jax.random.fold_in(key, 21)
    return norm_pairs(key, 4, M)


def draw_wide_norms(key, part):
    key = jax.random.fold_in(key, 31)
    return norm_pairs(key, 3, C)


def level_of(rng, dims, split, least, top_value):
    gain = 1.0
    for position, shards_of in split:
        draws = jax.random.uniform(jax.random.fold_in(jax.random.fold_in(rng, 6), position), (shards_of,), jnp.float32, least / len(split), top_value / len(split))
        gain = gain * jnp.repeat(jnp.exp(draws), dims[position] // shards_of).reshape((-1,) + (1,) * (len(dims) - 1 - position))
    return gain


def gaussian(key, extent, scale, reach, split=(), kind=jnp.bfloat16):
    loudness = level_of(key, extent, split, -0.22, 0.18) if split else 1.0
    result = jax.random.normal(key, extent, jnp.float32) * scale * loudness
    return jnp.minimum(jnp.maximum(result, -reach), reach).astype(kind)


def setup_inputs(seed: int = 0) -> dict:
    key_list = jax.random.split(jax.random.key(seed), 18)
    return {
        "video": gaussian(key_list[0], (CLIPS, FRAMES, HW, HW, C), 1.0, 6.0, ((0, 8), (1, 4))),
        "lengths": draw_lengths(jax.random.fold_in(key_list[17], 71), 0),
        "mid_norms": draw_mid_norms(jax.random.fold_in(key_list[17], 71), 0),
        "wide_norms": draw_wide_norms(jax.random.fold_in(key_list[17], 71), 0),
        "taps": gaussian(key_list[4], (3, 3, GW), 0.6, 2.5, (), jnp.float32),
        "me_reduce": gaussian(key_list[5], (M, R), M ** -0.5, 0.25, (), jnp.float32),
        "me_conv": gaussian(key_list[6], (3, 3, R, R), (9 * R) ** -0.5, 0.375, (), jnp.float32),
        "me_expand": gaussian(key_list[7], (R, M), 1.0, 6.0, (), jnp.float32),
        "me_bias": gaussian(key_list[8], (M,), 0.5, 3.0, (), jnp.float32),
        "w_in1": gaussian(key_list[9], (C, M), C ** -0.5, 0.125, ((0, 8), (1, 4)), jnp.float32),
        "w_mta": gaussian(key_list[10], (GW, 27 * GW), (9 * GW) ** -0.5, 0.1875, ((0, 8), (1, 4)), jnp.float32),
        "w_out1": gaussian(key_list[11], (M, C), M ** -0.5, 0.25, ((0, 8), (1, 4)), jnp.float32),
        "w_in2": gaussian(key_list[12], (C, M), C ** -0.5, 0.125, ((0, 8), (1, 4)), jnp.float32),
        "w_mid2": gaussian(key_list[13], (M, 9 * M), (9 * M) ** -0.5, 0.09375, ((0, 8), (1, 4)), jnp.float32),
        "w_out2": gaussian(key_list[14], (M, C), M ** -0.5, 0.25, ((0, 8), (1, 4)), jnp.float32),
        "w_proj": gaussian(key_list[15], (C, C), C ** -0.5, 0.125, ((0, 8), (1, 4)), jnp.float32),
        "grad_out": gaussian(key_list[16], (CLIPS, FRAMES, HW // 2, HW // 2, C), 1.0, 6.0, ((0, 8), (1, 4))),
    }


EPSILON = 1e-05
HIGHEST = lax.Precision.HIGHEST

@jax.custom_vjp
def low(v):
    return lax.optimization_barrier(v.astype(jnp.bfloat16)).astype(jnp.float32)

@jax.custom_vjp
def low_back(v):
    return v

def low_keep(v):
    return (low(v), None)

def low_pass(kept, grad):
    return (grad,)

def back_keep(v):
    return (v, None)

def back_low(kept, grad):
    return (low(grad),)
low.defvjp(low_keep, low_pass)
low_back.defvjp(back_keep, back_low)

def convolve(source, kernel, stride):
    leading = source.shape[:2]
    flattened = source.reshape((-1,) + source.shape[2:])
    convolved = lax.conv_general_dilated(flattened, kernel, (stride, stride), ((1, 1), (1, 1)), dimension_numbers=('NHWC', 'HWIO', 'NHWC'), precision=HIGHEST)
    return convolved.reshape(leading + convolved.shape[1:])

def normalize(values, weight, count, gain_row, bias_row):
    means = lax.optimization_barrier(jnp.sum(weight * values, axis=(0, 1, 2, 3))) / count
    spread = lax.optimization_barrier(jnp.sum(weight * jnp.square(values - means), axis=(0, 1, 2, 3))) / count
    return (values - means) * lax.rsqrt(spread + EPSILON) * gain_row + bias_row

def matmul(left, right):
    return jnp.dot(left, right, precision=HIGHEST)

def forward(source, mid_norms, wide_norms, taps, me_reduce, me_conv, me_expand, me_bias, w_in1, w_mta, w_out1, w_in2, w_mid2, w_out2, w_proj, mask, count_full, count_half):
    weight = mask[:, :, None, None, None]
    mask_next = jnp.concatenate([mask[:, 1:], jnp.zeros_like(mask[:, :1])], axis=1)
    weight_next = mask_next[:, :, None, None, None]
    pre_one = low_back(matmul(source, low(w_in1)))
    hidden_one = jax.nn.silu(normalize(pre_one, weight, count_full, mid_norms[0, 0], mid_norms[0, 1]))
    motion = low(low_back(matmul(low(hidden_one), low(me_reduce))))
    following = jnp.concatenate([motion[:, 1:], jnp.zeros_like(motion[:, :1])], axis=1)
    moved = low_back(convolve(following, low(me_conv), 1))
    change = weight_next * (moved - motion)
    pooled = lax.optimization_barrier(jnp.mean(change, axis=(2, 3)))
    excite = matmul(pooled, me_expand) + me_bias
    mixed = hidden_one * (1.0 + jax.nn.sigmoid(excite))[:, :, None, None, :]
    kernels = low(w_mta).reshape(GW, 3, 3, 3, GW)
    outputs = [mixed[..., :GW]]
    previous = None
    for branch in range(3):
        piece = mixed[..., (branch + 1) * GW:(branch + 2) * GW]
        if branch > 0:
            piece = piece + previous
        masked = weight * piece
        padded = jnp.pad(masked, ((0, 0), (1, 1), (0, 0), (0, 0), (0, 0)))
        blended = taps[branch, 0] * padded[:, :-2] + taps[branch, 1] * padded[:, 1:-1] + taps[branch, 2] * padded[:, 2:]
        kernel = jnp.transpose(kernels[:, branch], (1, 2, 0, 3))
        previous = low_back(convolve(low(blended), kernel, 1))
        outputs.append(previous)
    aggregated = jnp.concatenate(outputs, axis=-1)
    hidden_two = jax.nn.silu(normalize(aggregated, weight, count_full, mid_norms[1, 0], mid_norms[1, 1]))
    pre_three = low_back(matmul(low(hidden_two), low(w_out1)))
    branch_one = normalize(pre_three, weight, count_full, wide_norms[0, 0], wide_norms[0, 1])
    out_one = jax.nn.silu(source + branch_one)
    out_low = low(out_one)
    first_two = low_back(matmul(out_low, low(w_in2)))
    hidden_a = jax.nn.silu(normalize(first_two, weight, count_full, mid_norms[2, 0], mid_norms[2, 1]))
    mid_kernel = jnp.transpose(low(w_mid2).reshape(M, 3, 3, M), (1, 2, 0, 3))
    second_two = low_back(convolve(low(hidden_a), mid_kernel, 2))
    hidden_b = jax.nn.silu(normalize(second_two, weight, count_half, mid_norms[3, 0], mid_norms[3, 1]))
    third_two = low_back(matmul(low(hidden_b), low(w_out2)))
    branch_two = normalize(third_two, weight, count_half, wide_norms[1, 0], wide_norms[1, 1])
    short_two = low_back(matmul(out_low[:, :, ::2, ::2], low(w_proj)))
    shortcut = normalize(short_two, weight, count_half, wide_norms[2, 0], wide_norms[2, 1])
    out_two = weight * jax.nn.silu(branch_two + shortcut)
    squares = jnp.stack([jnp.sum(weight * source * source), jnp.sum(weight * branch_one * branch_one), jnp.sum(weight * out_one * out_one), jnp.sum(weight * branch_two * branch_two), jnp.sum(weight * out_two * out_two)])
    counts = jnp.stack([count_full, count_full, count_full, count_half, count_half]) * C
    return (out_two, jnp.sqrt(squares / counts))

def reference(video, lengths, mid_norms, wide_norms, taps, me_reduce, me_conv, me_expand, me_bias, w_in1, w_mta, w_out1, w_in2, w_mid2, w_out2, w_proj, grad_out):
    stamps = jnp.arange(FRAMES, dtype=jnp.int32)
    mask = (stamps[None, :] < lengths[:, None]).astype(jnp.float32)
    count_full = jnp.sum(mask) * (HW * HW)
    count_half = jnp.sum(mask) * (HW // 2 * (HW // 2))
    weight = mask[:, :, None, None, None]
    source = video.astype(jnp.float32) * weight

    def closed(source, mid_norms, wide_norms, taps, me_reduce, me_conv, me_expand, me_bias, w_in1, w_mta, w_out1, w_in2, w_mid2, w_out2, w_proj):
        return forward(source, mid_norms, wide_norms, taps, me_reduce, me_conv, me_expand, me_bias, w_in1, w_mta, w_out1, w_in2, w_mid2, w_out2, w_proj, mask, count_full, count_half)
    out_two, pull, rms = jax.vjp(closed, source, mid_norms, wide_norms, taps, me_reduce, me_conv, me_expand, me_bias, w_in1, w_mta, w_out1, w_in2, w_mid2, w_out2, w_proj, has_aux=True)
    grads = pull(grad_out.astype(jnp.float32))
    grad_video = (weight * grads[0]).astype(jnp.bfloat16)
    return (out_two.astype(jnp.bfloat16), grad_video, grads[1], grads[2], grads[3], grads[4], grads[5], grads[6], grads[7], grads[8], grads[9], grads[10], grads[11], grads[12], grads[13], grads[14], rms)
```

```python
import functools

import jax
import jax.numpy as jnp
import numpy as np
from jax import lax
from jax.experimental import pallas as pl
from jax.experimental.pallas import tpu as pltpu
from jax.sharding import PartitionSpec as P

C = 2048
M = 512
R = 32
GW = 128
HW = 16
PIX = HW * HW
QUARTER = PIX // 4
CLIPS = 3
SPAN = 2
T = CLIPS * SPAN
ROWS = T * PIX
HALF_ROWS = T * QUARTER
WIDE_TILE = 512
WIDE_STEPS = C // WIDE_TILE

EPSILON = 1e-05
HIGHEST = lax.Precision.HIGHEST
F32 = jnp.float32
BF16 = jnp.bfloat16
MESH = pl.DeviceIdType.MESH
VMEM = pltpu.VMEM
DMA = pltpu.SemaphoreType.DMA
LIMIT = 60 * 1024 * 1024

WHOLE = pl.BlockSpec(memory_space=pltpu.VMEM)
SCALARS = pl.BlockSpec(memory_space=pltpu.SMEM)
ANY = pl.BlockSpec(memory_space=pl.ANY)


def shaped(shape, dtype=F32):
    return jax.ShapeDtypeStruct(shape, dtype)


def fixed(shape):
    return pl.BlockSpec(shape, lambda i: (0,) * len(shape))


def at_first(shape):
    return pl.BlockSpec(shape, lambda i: (i,) + (0,) * (len(shape) - 1))


def at_last(shape):
    return pl.BlockSpec(shape, lambda i: (0,) * (len(shape) - 1) + (i,))


def remote_call(name, body, ident, in_specs, out_specs, out_shape, scratch, cost, *operands):
    return pl.pallas_call(
        body,
        name=name,
        in_specs=in_specs,
        out_specs=out_specs,
        out_shape=out_shape,
        scratch_shapes=scratch,
        cost_estimate=pl.CostEstimate(flops=1024, bytes_accessed=1024, transcendentals=0),
        compiler_params=pltpu.CompilerParams(
            vmem_limit_bytes=LIMIT, collective_id=ident, has_side_effects=True
        ),
    )(*operands)


def sigmoid(z):
    return 0.5 * jnp.tanh(0.5 * z) + 0.5


def nn(left, right):
    return jnp.dot(left, right, preferred_element_type=F32)


def nt(left, right):
    return lax.dot_general(left, right, (((1,), (1,)), ((), ())), preferred_element_type=F32)


def tn(left, right):
    return lax.dot_general(left, right, (((0,), (0,)), ((), ())), preferred_element_type=F32)


def nn_exact(left, right):
    return jnp.dot(left, right, precision=HIGHEST, preferred_element_type=F32)


def nt_exact(left, right):
    return lax.dot_general(
        left, right, (((1,), (1,)), ((), ())), precision=HIGHEST, preferred_element_type=F32
    )


def tn_exact(left, right):
    return lax.dot_general(
        left, right, (((0,), (0,)), ((), ())), precision=HIGHEST, preferred_element_type=F32
    )


def down(values):
    return jnp.sum(values, axis=0, keepdims=True)


def merge(stats, values, tab, i):
    rows = values.shape[0]
    mean = down(values) * (1.0 / rows)
    spread = down(jnp.square(values - mean))
    delta = mean - stats[0:1]
    stats[0:1] += delta * tab[1, i]
    stats[1:2] += spread * tab[0, i] + jnp.square(delta) * (tab[2, i] * rows)


def whole_stats(parts, masks, inv_count):
    mean = sum(down(part) * mask for part, mask in zip(parts, masks)) * inv_count
    spread = sum(down(jnp.square(part - mean)) * mask for part, mask in zip(parts, masks))
    return (mean, spread)


def unit(values, stats):
    return (values - stats[0:1]) * stats[1:2]


def norm_back(grads, centred, stats, pair, totals, mask, inv_count):
    total, cross = (totals[0:1] * inv_count, totals[1:2] * inv_count)
    return (pair[0:1] * stats[1:2]) * (grads - mask * (total + centred * cross))


def peers_of(ndp, ntm):
    d, t = (lax.axis_index("dp"), lax.axis_index("tm"))
    along = [(lax.rem(d + k, ndp), t) for k in range(1, ndp)]
    return along, [(d, lax.rem(t + k, ntm)) for k in range(1, ntm)]


def greet(ndp, ntm):
    along, across = peers_of(ndp, ntm)
    for peer in along + across:
        pl.semaphore_signal(
            pltpu.get_barrier_semaphore(), inc=1, device_id=peer, device_id_type=MESH
        )


def met(ndp, ntm):
    pl.semaphore_wait(pltpu.get_barrier_semaphore(), ndp + ntm - 2)


def sent(source, target, out_sem, in_sem, peer):
    return pltpu.make_async_remote_copy(source, target, out_sem, in_sem, peer, MESH)


def start_all(copies):
    for copy in copies:
        copy.start()


def wait_all(copies):
    for copy in copies:
        copy.wait()


def plain_gather(parts, row, tab):
    return sum(parts[1:], parts[0])


def plain_last(value, tab):
    return value


def spread_gather(scale, parts, row, tab):
    outputs = []
    for k in range(0, parts[0].shape[0], 2):
        means = [part[k : k + 1] for part in parts]
        mean = sum(value * tab[row, s] for s, value in enumerate(means))
        spread = sum(
            part[k + 1 : k + 2] + jnp.square(value - mean) * (tab[row + 1, s] * scale)
            for s, (part, value) in enumerate(zip(parts, means))
        )
        outputs.extend([mean, spread])
    return jnp.concatenate(outputs, axis=0)


def spread_last(scale, value, tab):
    outputs = []
    for k in range(0, value.shape[0], 2):
        outputs.append(value[k : k + 1])
        outputs.append(lax.rsqrt(value[k + 1 : k + 2] * (tab[4, 0] * (1.0 / scale)) + EPSILON))
    return jnp.concatenate(outputs, axis=0)


def swap_scratch(ndp, ntm, shape):
    return [
        VMEM(shape, F32), VMEM((ndp,) + shape, F32), VMEM((ntm,) + shape, F32),
        DMA((4, max(ndp, ntm))),
    ]


def swap_steps(ndp, ntm, scale, tab, out, source, first, second, sems):
    d, t = (lax.axis_index("dp"), lax.axis_index("tm"))
    along, across = peers_of(ndp, ntm)
    if scale is None:
        gather, last = (plain_gather, plain_last)
    else:
        gather = functools.partial(spread_gather, scale)
        last = functools.partial(spread_last, scale)

    def copies(buffer, peers, k):
        return [
            sent(buffer.at[0], buffer.at[j], sems.at[2 * k, j], sems.at[2 * k + 1, j], peer)
            for j, peer in enumerate(peers, 1)
        ]

    one, two = (copies(first, along, 0), copies(second, across, 1))

    def begin():
        first[0] = source[...]
        start_all(one)

    def middle():
        wait_all(one)
        second[0] = gather([first[lax.rem(d - s + ndp, ndp)] for s in range(ndp)], 0, tab)
        start_all(two)

    def end():
        wait_all(two)
        out[...] = last(
            gather([second[lax.rem(t - s + ntm, ntm)] for s in range(ntm)], 2, tab), tab
        )

    return (begin, middle, end)


def all_sums_scratch(ndp, ntm, rows):
    return [
        VMEM((ndp, rows // ndp, GW), F32), VMEM((ntm, rows // ndp // ntm, GW), F32),
        DMA((8, max(ndp, ntm))),
    ]


def all_sums_steps(ndp, ntm, source, out, first, second, sems):
    d, t = (lax.axis_index("dp"), lax.axis_index("tm"))
    large = source.shape[0] // ndp
    small = large // ntm
    along, across = peers_of(ndp, ntm)

    def rows(group, size):
        return pl.ds(pl.multiple_of(group * size, size), size)

    def copies(pieces, peers, k):
        return [
            sent(left, right, sems.at[2 * k, j], sems.at[2 * k + 1, j], peer)
            for j, ((left, right), peer) in enumerate(zip(pieces, peers), 1)
        ]

    own = out.at[pl.ds(pl.multiple_of(d * large + t * small, small), small)]
    block = out.at[rows(d, large)]
    one = copies(
        [(source.at[rows(peer[0], large)], first.at[k]) for k, peer in enumerate(along, 1)],
        along, 0,
    )
    two = copies(
        [(first.at[0, rows(peer[1], small)], second.at[k]) for k, peer in enumerate(across, 1)],
        across, 1,
    )
    three = copies([(own, own)] * (ntm - 1), across, 2)
    four = copies([(block, block)] * (ndp - 1), along, 3)

    def begin():
        start_all(one)

    def second_step():
        wait_all(one)
        first[0] = source[rows(d, large)]
        total = first[lax.rem(d, ndp)]
        for s in range(1, ndp):
            total = total + first[lax.rem(d - s + ndp, ndp)]
        first[0] = total
        start_all(two)

    def third_step():
        wait_all(two)
        second[0] = first[0, rows(t, small)]
        total = second[lax.rem(t, ntm)]
        for s in range(1, ntm):
            total = total + second[lax.rem(t - s + ntm, ntm)]
        own[...] = total
        start_all(three)

    def fourth_step():
        wait_all(three)
        start_all(four)

    def end():
        wait_all(four)

    return [begin, second_step, third_step, fourth_step, end]


def cube(ndp, ntm):
    d, t = (lax.axis_index("dp"), lax.axis_index("tm"))
    core, x, y = (lax.rem(d, 2), lax.rem(d // 2, 2), d // 4)
    peers = ((d + 1 - 2 * core, t), (d + 2 - 4 * x, t), (d + 4 - 8 * y, t))
    return (t, core, x, y, peers)


def lanes(group, width):
    return pl.ds(pl.multiple_of(group * width, GW), width)


def over_z(ntm, low, target, sems):
    d, t = (lax.axis_index("dp"), lax.axis_index("tm"))
    slot = target.at[:, lanes(t, low.shape[1])]
    copies = [pltpu.make_async_copy(low, slot, sems.at[2, 0])]
    for k in range(1, ntm):
        copies.append(sent(low, slot, sems.at[0, k], sems.at[1, k], (d, lax.rem(t + k, ntm))))
    return copies


def gather_steps(ndp, ntm, low, full, rows, z_sems, sems):
    t, core, x, y, (to_core, to_x, to_y) = cube(ndp, ntm)
    own = full.at[2 * y + x, core]
    if low.shape[1] == full.shape[3]:
        zs = [pltpu.make_async_copy(low, own, z_sems.at[0, 0])]
    else:
        zs = over_z(ntm, low, own, z_sems)
    one, two, three = ([], [], [])
    for k, (start, size) in enumerate(rows):
        part = pl.ds(start, size)
        first, second = (to_x, to_y) if k % 2 == 0 else (to_y, to_x)
        other = (y, 1 - x) if k % 2 == 0 else (1 - y, x)
        block = full.at[2 * y + x, core, part]
        one.append([sent(block, block, sems.at[0, k, 0], sems.at[0, k, 1], first)])
        pair = []
        for j, (row, col) in enumerate(((y, x), other), 1):
            block = full.at[2 * row + col, core, part]
            pair.append(sent(block, block, sems.at[j, k, 0], sems.at[j, k, 1], second))
        two.append(pair)
        block = full.at[:, core, part]
        three.append([sent(block, block, sems.at[3, k, 0], sems.at[3, k, 1], to_core)])
    count = len(rows)
    steps = [[functools.partial(start_all, zs)]]

    def after(waits, starts):
        wait_all(waits)
        for group in starts:
            start_all(group)

    steps.append([functools.partial(after, zs, one)])
    steps.append([functools.partial(after, one[k], [two[k]]) for k in range(count)])
    steps.append([functools.partial(after, two[k], [three[k]]) for k in range(count)])
    steps.append([functools.partial(after, three[k], []) for k in range(count)])
    return steps


def run_steps(steps):
    for step in steps:
        step()


def lane_row(values):
    lane = lax.broadcasted_iota(jnp.int32, (1, GW), 1)
    row = jnp.zeros((1, GW), F32)
    for k, value in enumerate(values):
        row = jnp.where(lane == k, value, row)
    return row


def fill_tables(ndp, ntm, lengths, tab, swap, later):
    d, t = (lax.axis_index("dp"), lax.axis_index("tm"))
    held = [lengths[k] for k in range(ndp * CLIPS)]
    counts = [
        [
            sum(jnp.clip(held[i * CLIPS + c] - j * SPAN, 0, SPAN) for c in range(CLIPS))
            for i in range(ndp)
        ]
        for j in range(ntm)
    ]
    sums = [sum(column) for column in counts]
    total = sum(sums).astype(F32)
    column = [
        sum(jnp.where(t == j, counts[j][i], 0) for j in range(ntm)).astype(F32) for i in range(ndp)
    ]
    mask, after = ([], [])
    for c in range(CLIPS):
        own = lengths[d * CLIPS + c]
        for k in range(SPAN):
            mask.append(jnp.where(t * SPAN + k < own, 1.0, 0.0))
            after.append(jnp.where(t * SPAN + k + 1 < own, 1.0, 0.0))
    before = [sum(mask[:k], jnp.float32(0.0)) for k in range(T)]
    mask_row, before_row = (lane_row(mask), lane_row(before))
    share = 1.0 / jnp.maximum(before_row + mask_row, 1.0)
    tab[...] = jnp.zeros_like(tab)
    tab[0:1] = mask_row
    tab[1:2] = mask_row * share
    tab[2:3] = before_row * mask_row * share
    local = jnp.maximum(sum(mask), 1.0)
    ones = jnp.full((1, GW), 1.0, F32)
    rates = lane_row([1.0 / PIX, 1.0 / QUARTER, 1.0 / PIX, 1.0 / QUARTER, 1.0, 1.0])
    bases = lane_row([local, local, total, total, 1.0, 1.0])
    tab[3:4] = rates / jnp.maximum(bases, ones)
    swap[...] = jnp.zeros_like(swap)
    here = jnp.maximum(sum(column), 1.0)
    swap[0:1] = lane_row(column) / (here * ones)
    swap[1:2] = lane_row(column)
    swap[2:3] = lane_row([value.astype(F32) for value in sums]) / (total * ones)
    swap[3:4] = lane_row([value.astype(F32) for value in sums])
    swap[4:5] = ones / (total * ones)
    swap[5:6] = total * ones
    row = lax.broadcasted_iota(jnp.int32, (8, GW), 0)
    values = jnp.zeros((8, GW), F32)
    for k, value in enumerate(after):
        values = jnp.where(row == k, value, values)
    later[...] = values


def first_gather(
    ndp, ntm, lengths, in_shard, mta_shard, out_shard, mid_shard, reduce, conv, expand,
    full_in, full_mta, out_rows, mid_rows, tab, swap, later, reduce_low, conv_low,
    expand_wide,
    low_in, low_mta, low_out, low_mid, z_sems, sems,
):
    greet(ndp, ntm)
    low_in[...] = in_shard[...].astype(BF16)
    low_mta[...] = jnp.zeros_like(low_mta)
    low_mta[:, : mta_shard.shape[1]] = mta_shard[...].astype(BF16)
    low_out[...] = out_shard[...].astype(BF16)
    low_mid[...] = mid_shard[...].astype(BF16)
    one = gather_steps(
        ndp, ntm, low_in, full_in, ((0, 128), (128, 128)), z_sems.at[0], sems.at[0]
    )
    two = gather_steps(ndp, ntm, low_mta, full_mta, ((0, 16),), z_sems.at[1], sems.at[1])
    copies = over_z(ntm, low_out, out_rows, z_sems.at[2])
    copies += over_z(ntm, low_mid, mid_rows, z_sems.at[3])
    met(ndp, ntm)
    run_steps(one[0])
    run_steps(two[0])
    start_all(copies)
    fill_tables(ndp, ntm, lengths, tab, swap, later)
    reduce_low[...] = jnp.zeros_like(reduce_low)
    reduce_low[:, 0:R] = reduce[...].astype(BF16)
    conv_low[...] = jnp.zeros_like(conv_low)
    conv_low[:, 0:R, 0:R] = conv[...].astype(BF16).astype(F32)
    expand_wide[...] = jnp.zeros_like(expand_wide)
    expand_wide[0:R] = expand[...]
    for k in range(1, 5):
        run_steps(one[k])
        run_steps(two[k])
    wait_all(copies)


def scatter_chunks(items):
    chunks = []
    for item, (base, rows, cols, parts) in enumerate(items):
        size = rows // parts
        for part in range(parts):
            chunks.append((item, base + part * size, part * size, size, cols))
    return chunks


def scatter_scratch(items, ntm):
    chunks = scatter_chunks(items)
    scratch = []
    for _, _, _, rows, cols in chunks:
        scratch += [
            VMEM((2, 2, rows, cols), BF16), VMEM((2, 2, rows, cols), BF16),
            VMEM((2, rows, cols), BF16), VMEM((rows, cols), BF16),
            VMEM((ntm, rows, cols // ntm), BF16),
        ]
    return scratch + [DMA((len(chunks), 7)), DMA((len(chunks), 2, ntm))]


def z_scratch(shapes, ntm):
    return [VMEM((ntm, rows, cols // ntm), BF16) for rows, cols in shapes] + [
        DMA((len(shapes), 2, ntm))
    ]


def z_steps(ntm, sources, outs, scratch):
    t = lax.axis_index("tm")
    _, across = peers_of(1, ntm)
    d = lax.axis_index("dp")
    sems = scratch[-1]
    begins, ends = ([], [])
    for i, (source, out) in enumerate(zip(sources, outs)):
        held = scratch[i]
        width = source.shape[1] // ntm
        copies = [
            sent(
                source.at[:, lanes(peer[1], width)], held.at[k], sems.at[i, 0, k], sems.at[i, 1, k],
                (d, peer[1]),
            )
            for k, peer in enumerate(across, 1)
        ]
        copies.append(
            pltpu.make_async_copy(source.at[:, lanes(t, width)], held.at[0], sems.at[i, 0, 0])
        )

        def end(copies=copies, held=held, out=out):
            wait_all(copies)
            total = held[0].astype(F32)
            for k in range(1, ntm):
                total = total + held[k].astype(F32)
            out[...] = total

        begins.append(functools.partial(start_all, copies))
        ends.append(end)
    return [begins, ends]


def scatter_steps(ndp, ntm, items, sources, outs, scratch, partial=False):
    t, core, x, y, (to_core, to_x, to_y) = cube(ndp, ntm)
    _, across = peers_of(ndp, ntm)
    chunks = scatter_chunks(items)
    sems, z_sems = scratch[-2:]
    steps = [[], [], [], [], []]
    for i, (item, start, place, size, cols) in enumerate(chunks):
        own, first, second, third, fourth = scratch[5 * i : 5 * i + 5]
        by_x = i % 2 == 0
        part = pl.ds(start, size)
        width = cols // ntm
        source = sources[item]
        one = [
            pltpu.make_async_copy(source.at[:, :, core, part], own, sems.at[i, 0]),
            sent(source.at[:, :, 1 - core, part], first, sems.at[i, 1], sems.at[i, 2], to_core),
        ]
        if by_x:
            two = [sent(own.at[:, 1 - x], second, sems.at[i, 3], sems.at[i, 4], to_x)]
            three = [sent(second.at[1 - y], third, sems.at[i, 5], sems.at[i, 6], to_y)]
        else:
            two = [sent(own.at[1 - y], second, sems.at[i, 3], sems.at[i, 4], to_y)]
            three = [sent(second.at[1 - x], third, sems.at[i, 5], sems.at[i, 6], to_x)]
        four = [
            sent(
                third.at[:, lanes(peer[1], width)], fourth.at[k], z_sems.at[i, 0, k],
                z_sems.at[i, 1, k], peer,
            )
            for k, peer in enumerate(across, 1)
        ]
        four.append(
            pltpu.make_async_copy(third.at[:, lanes(t, width)], fourth.at[0], z_sems.at[i, 0, 0])
        )

        def add_core(one=one, two=two, own=own, first=first):
            wait_all(one)

            def add(k, carry):
                for j in range(2):
                    own[k, j] += first[k, j]
                return carry

            lax.fori_loop(0, 2, add, 0)
            start_all(two)

        def add_first(two=two, three=three, own=own, second=second, by_x=by_x):
            wait_all(two)
            for k in range(2):
                second[k] += own[k, x] if by_x else own[y, k]
            start_all(three)

        def add_second(
            three=three, four=four, second=second, third=third, by_x=by_x, out=outs[item],
            place=place, size=size,
        ):
            wait_all(three)
            if partial:
                out[place : place + size] = third[...] + second[y if by_x else x]
                return
            third[...] += second[y if by_x else x]
            start_all(four)

        def add_last(four=four, fourth=fourth, out=outs[item], place=place, size=size):
            wait_all(four)
            total = fourth[0].astype(F32)
            for k in range(1, ntm):
                total = total + fourth[k].astype(F32)
            out[place : place + size] = total

        steps[0].append(functools.partial(start_all, one))
        adds = (add_core, add_first, add_second) + (() if partial else (add_last,))
        for k, step in enumerate(adds):
            steps[k + 1].append(step)
    return steps


def cubed(grad):
    return grad.reshape((2, 2, 2, grad.shape[0] // 8, grad.shape[1]))


LOCAL = "local"


def staged_kernel(ndp, ntm, steps, body, counts, marks, scale, items, at, *refs):
    n_in, n_source, n_carry, n_out, n_scratch, swaps = counts

    def take(count):
        nonlocal refs
        taken, refs = (refs[:count], refs[count:])
        return taken

    swap_tab = take(swaps)
    ins, sources, shards = (take(n_in), take(n_source), take(n_carry))
    outs = list(take(n_out))
    totals = take(swaps)
    scattered, gathered = (take(len(items)), take(n_carry))
    scratch = take(n_scratch)
    swap_refs = take(4 * swaps)
    lows, carry_sems = (take(n_carry), take(1 if n_carry else 0))
    scatter_refs = refs
    i = pl.program_id(0)
    last = steps - 1
    copies = []
    for k, (low, target) in enumerate(zip(lows, gathered)):
        copies += over_z(ntm, low, target, carry_sems[0].at[k])
    if marks is not None:
        outs.insert(marks, swap_refs[0])

    @pl.when(i == 0)
    def _():
        greet(ndp, ntm)

    tail = body(*ins, *outs, *scratch) or []
    groups = [[], [], [], [], []]
    if items:
        groups = scatter_steps(ndp, ntm, items, sources, scattered, scatter_refs)
    swap = [lambda: None] * 3
    if swaps:
        swap = swap_steps(ndp, ntm, scale, swap_tab[0], totals[0], *swap_refs)

    @pl.when(i == 0)
    def _():
        for shard, low in zip(shards, lows):
            low[...] = shard[...].astype(BF16)
        met(ndp, ntm)
        start_all(copies)
        run_steps(groups[0])

    for k in range(1, 4):
        if items and isinstance(at[k], int) and at[k] < last:

            @pl.when(i == at[k])
            def _(k=k):
                run_steps(groups[k])

    @pl.when(i == last)
    def _():
        for k in range(1, 4):
            if items and at[k] == last:
                run_steps(groups[k])
        for k, name in enumerate("abc"):
            swap[k]()
            if k < len(tail):
                tail[k]()
            for j in range(1, 5):
                if items and at[j] == name:
                    run_steps(groups[j])
        wait_all(copies)


def plain_kernel(steps, body, *refs):
    tail = body(*refs) or []

    @pl.when(pl.program_id(0) == steps - 1)
    def _():
        run_steps(tail)


def staged(
    name, ident, *, ndp, ntm, steps, body, ins, outs, scratch, cost, swap=None, items=(),
    sources=(), at=(0, 1, 2, 3, "c"), carry=(),
):
    arrays, specs = ([], [])
    if swap is not None:
        arrays.append(swap[0])
        specs.append(SCALARS)
    arrays += [array for array, _ in ins] + list(sources) + list(carry)
    specs += [spec for _, spec in ins] + [ANY] * len(sources)
    specs += [fixed(shard.shape) for shard in carry]
    marks = outs.index(LOCAL) if LOCAL in outs else None
    real = [out for out in outs if out is not LOCAL]
    out_shapes, out_specs = ([shape for shape, _ in real], [spec for _, spec in real])
    extra = []
    swaps, scale = (0, None)
    if swap is not None:
        swaps, scale = (1, swap[1])
        out_shapes.append(shaped(swap[2]))
        out_specs.append(fixed(swap[2]))
        extra += swap_scratch(ndp, ntm, swap[2])
    for _, rows, cols, _ in items:
        out_shapes.append(shaped((rows, cols // ntm)))
        out_specs.append(fixed((rows, cols // ntm)))
    for shard in carry:
        out_shapes.append(shaped((shard.shape[0], shard.shape[1] * ntm), BF16))
        out_specs.append(ANY)
        extra.append(VMEM(shard.shape, BF16))
    if carry:
        extra.append(DMA((len(carry), 3, ntm)))
    if items:
        extra += scatter_scratch(items, ntm)
    if not (swaps or items or carry):
        return pl.pallas_call(
            functools.partial(plain_kernel, steps, body),
            name=name,
            grid=(steps,),
            in_specs=specs,
            out_specs=out_specs,
            out_shape=out_shapes,
            scratch_shapes=list(scratch),
            cost_estimate=pl.CostEstimate(flops=1024, bytes_accessed=1024, transcendentals=0),
            compiler_params=pltpu.CompilerParams(vmem_limit_bytes=LIMIT),
        )(*arrays)
    counts = (len(ins), len(sources), len(carry), len(real), len(scratch), swaps)
    return pl.pallas_call(
        functools.partial(
            staged_kernel, ndp, ntm, steps, body, counts, marks, scale, tuple(items), at
        ),
        name=name,
        grid=(steps,),
        in_specs=specs,
        out_specs=out_specs,
        out_shape=out_shapes,
        scratch_shapes=list(scratch) + extra,
        cost_estimate=pl.CostEstimate(flops=1024, bytes_accessed=1024, transcendentals=0),
        compiler_params=pltpu.CompilerParams(
            vmem_limit_bytes=LIMIT, collective_id=ident, has_side_effects=True
        ),
    )(*arrays)


def in_one(tab, video, weight, pre, squares, stats):
    i = pl.program_id(0)

    @pl.when(i == 0)
    def _():
        stats[...] = jnp.zeros_like(stats)
        squares[...] = jnp.zeros_like(squares)

    source = video[0]
    value = nn(source, weight[...]) * tab[0, i]
    pre[0] = value
    merge(stats, value, tab, i)
    squares[...] += down(jnp.square(source.astype(F32))) * tab[0, i]


def column(shape):
    return lax.rem(lax.broadcasted_iota(jnp.int32, shape, 0), HW)


def spread_taps(store, low):
    value = low.astype(F32)
    place = column(value.shape)
    zeros = jnp.zeros((HW, 3 * GW), BF16)
    store[0:HW] = zeros
    store[HW + PIX : PIX + 2 * HW] = zeros
    before = jnp.where(place == 0, 0.0, pltpu.roll(value, 1, 0))
    after = jnp.where(place == HW - 1, 0.0, pltpu.roll(value, PIX - 1, 0))
    store[HW : HW + PIX, 0:GW] = before.astype(BF16)
    store[HW : HW + PIX, GW : 2 * GW] = low
    store[HW : HW + PIX, 2 * GW : 3 * GW] = after.astype(BF16)


def window(store, row):
    return store[row * HW : row * HW + PIX]


def neighbours(ntm):
    d, t = (lax.axis_index("dp"), lax.axis_index("tm"))
    return (t > 0, t < ntm - 1, (d, jnp.maximum(t - 1, 0)), (d, jnp.minimum(t + 1, ntm - 1)))


def rows_of(pieces):
    place = lax.broadcasted_iota(jnp.int32, (8, pieces[0].shape[1]), 0)
    result = jnp.zeros(place.shape, F32)
    for i, piece in enumerate(pieces):
        result = jnp.where(place == i, piece, result)
    return result


def chosen(rows, cols, shift, start, count):
    row = lax.broadcasted_iota(jnp.int32, (rows, cols), 0)
    col = lax.broadcasted_iota(jnp.int32, (rows, cols), 1)
    inside = (col >= start) & (col < start + count) & (row - col == shift)
    return jnp.where(inside, 1.0, 0.0).astype(BF16)


def tile_from_edges(weight, tile, edge, edge_wide):
    total, col = (None, 0)
    while col < GW:
        block, offset = divmod(tile * GW + col, edge)
        count = min(GW - col, edge - offset)
        base, shift = (block * edge_wide + offset // GW * GW, offset % GW)
        width = GW if shift + count <= GW else 2 * GW
        part = nn(weight[:, base : base + width], chosen(width, GW, shift - col, col, count))
        total = part if total is None else total + part
        col += count
    return total.astype(BF16)


def edge_from_tiles(tiles, place, edge, edge_wide):
    block, at = divmod(place * GW, edge_wide)
    total, col = (None, 0)
    while col < GW and at + col < edge:
        tile, shift = divmod(block * edge + at + col, GW)
        count = min(GW - col, edge - at - col, GW - shift)
        part = nn(tiles[tile], chosen(GW, GW, shift - col, col, count))
        total = part if total is None else total + part
        col += count
    return total.astype(BF16)


def mta_forward(
    ndp, ntm, fast, edge, swap_tab, tab, pre, stats, pair, reduce_low, conv_low, expand, bias,
    weight, taps, windows, later, *refs,
):
    carried = 1 if fast else 0
    shards, refs = (refs[: 2 * carried], refs[2 * carried :])
    agg, stats_out, ext_out, blended, sigma, snext, pooled, kernels = refs[:8]
    gathered, refs = (refs[8 : 8 + 2 * carried], refs[8 + 2 * carried :])
    hidden, store, ext, kept, gates, s_own, s_send, s_recv, ssems, rsems = refs[:10]
    swap_refs, refs = (refs[10:14], refs[14:])
    stats_two = swap_refs[0]
    has_prev, has_next, prev, following = neighbours(ntm)
    greet(ndp, ntm)
    pieces, dp_steps = ([], [[], [], [], [], []])
    if fast:
        low, piece_sems, z_sems, dp_sems = refs
        size = low.shape[0] // 8
        for k in range(8):
            part = pl.ds(k * size, size)
            pieces.append(over_z(ntm, low.at[part], gathered[0].at[part], piece_sems.at[k]))
        dp_steps = gather_steps(
            ndp, ntm, shards[1], gathered[1], ((0, 128), (128, 128)), z_sems, dp_sems
        )
        low[...] = shards[0][...].astype(BF16)

    def bulk(first, last):
        for piece in pieces[first:last]:
            start_all(piece)

    swap = swap_steps(ndp, ntm, PIX, swap_tab, stats_out, *swap_refs)
    for tile in range(27):
        row, col = divmod(tile % 9, 3)
        if fast:
            value = tile_from_edges(weight, tile, edge, weight.shape[1] // ntm)
        else:
            value = weight[tile]
        kernels[tile // 9, row, col * GW : (col + 1) * GW] = value
    met(ndp, ntm)
    run_steps(dp_steps[0])
    bulk(0, 2)

    def first(f, carry):
        z = unit(pre[f], stats) * pair[0:1] + pair[1:2]
        value = z * sigmoid(z)
        hidden[f] = value
        motion = nn(value.astype(BF16), reduce_low[...]).astype(BF16)
        s_own[f] = nn(windows[...], motion)
        return carry

    lax.fori_loop(0, T, first, 0)
    for clip in range(CLIPS):
        s_send[clip] = s_own[clip * SPAN]
    back = sent(s_send, s_recv, ssems.at[9, 0], rsems.at[9, 0], prev)

    @pl.when(has_prev)
    def _():
        back.start()

    run_steps(dp_steps[1])

    @pl.when(has_prev)
    def _():
        back.wait_send()

    @pl.when(has_next)
    def _():
        back.wait_recv()

    @pl.when(jnp.logical_not(has_next))
    def _():
        s_recv[...] = jnp.zeros_like(s_recv)

    bulk(2, 3)
    for clip in range(CLIPS):
        snext[clip * SPAN] = s_own[clip * SPAN + 1]
        snext[clip * SPAN + 1] = s_recv[clip]
    total = -rows_of([s_own[f, 4:5] for f in range(T)])
    for tap in range(9):
        rows = rows_of([snext[f, tap : tap + 1] for f in range(T)])
        total = total + nn_exact(rows, conv_low[tap])
    mean = total * (later[...] * (1.0 / PIX))
    pooled[...] = mean
    level = sigmoid(nn_exact(mean, expand[...]) + bias[...])
    sigma[...] = level
    for f in range(T):
        gates[f] = 1.0 + level[f : f + 1]

    @pl.when(jnp.logical_not(has_prev))
    def _():
        for group in range(3):
            ext[group, :, 0] = jnp.zeros((CLIPS, PIX, GW), BF16)

    @pl.when(jnp.logical_not(has_next))
    def _():
        for group in range(3):
            ext[group, :, 3] = jnp.zeros((CLIPS, PIX, GW), BF16)

    def edges(group, clip):
        k = group * CLIPS + clip
        left = sent(ext.at[group, clip, 1], ext.at[group, clip, 3], ssems.at[k, 0], rsems.at[k, 0], prev)
        right = sent(
            ext.at[group, clip, 2], ext.at[group, clip, 0], ssems.at[k, 1], rsems.at[k, 1],
            following,
        )
        return left, right

    def offer(group, clip):
        low, high = ((group + 1) * GW, (group + 2) * GW)

        def piece(step, carry):
            f = clip * SPAN + step
            value = hidden[f, :, low:high] * gates[f, :, low:high]
            if group > 0:
                value = value + agg[f, :, low - GW : low]
            value = value * tab[0, f]
            kept[group % 2, clip, step] = value
            ext[group, clip, step + 1] = value.astype(BF16)
            return carry

        lax.fori_loop(0, SPAN, piece, 0)
        left, right = edges(group, clip)

        @pl.when(has_prev)
        def _():
            left.start()

        @pl.when(has_next)
        def _():
            right.start()

    def taken(group, clip):
        left, right = edges(group, clip)

        @pl.when(has_prev)
        def _():
            left.wait_send()
            right.wait_recv()

        @pl.when(has_next)
        def _():
            right.wait_send()
            left.wait_recv()

    def convolve(group, clip):
        low, high = ((group + 1) * GW, (group + 2) * GW)
        row = [taps[group * 3 + k : group * 3 + k + 1] for k in range(3)]

        def mix(step, carry):
            f = clip * SPAN + step
            own = [kept[group % 2, clip, k] for k in range(SPAN)]
            line = [ext[group, clip, 0].astype(F32)] + own + [ext[group, clip, 3].astype(F32)]
            here = [jnp.where(step == 0, line[k], line[k + 1]) for k in range(3)]
            mixed = row[0] * here[0] + row[1] * here[1] + row[2] * here[2]
            value = mixed.astype(BF16)
            blended[group, f] = value
            spread_taps(store.at[step], value)
            result = nn(window(store.at[step], 0), kernels[group, 0])
            result += nn(window(store.at[step], 1), kernels[group, 1])
            result += nn(window(store.at[step], 2), kernels[group, 2])
            agg[f, :, low:high] = result
            return carry

        lax.fori_loop(0, SPAN, mix, 0)

    for clip in range(CLIPS):
        offer(0, clip)

    def base(f, carry):
        agg[f, :, 0:GW] = hidden[f, :, 0:GW] * gates[f, :, 0:GW]
        return carry

    lax.fori_loop(0, T, base, 0)
    pieces_at = {(0, 0): (3, 4), (0, 2): (4, 5), (1, 2): (5, 8)}
    for group in range(3):
        for clip in range(CLIPS):
            taken(group, clip)
            convolve(group, clip)
            if group < 2:
                offer(group + 1, clip)
                bulk(*(pieces_at.get((group, clip), (0, 0))))
        run_steps(dp_steps[2 + group])
    ext_out[...] = ext[...]
    masks = [tab[0, f] for f in range(T)]
    mean, spread = whole_stats([agg[f] for f in range(T)], masks, tab[3, 0])
    stats_two[0:1] = mean
    stats_two[1:2] = spread
    run_steps(swap)
    for piece in pieces:
        wait_all(piece)


def out_one(tab, agg, stats, pair, order, weight, hidden, pre, sums):
    i = pl.program_id(0)

    @pl.when(i == 0)
    def _():
        sums[...] = jnp.zeros_like(sums)

    z = unit(agg[0], stats) * pair[0:1] + pair[1:2]
    value = nn(order[...], (z * sigmoid(z)).astype(BF16)).astype(BF16)
    hidden[0] = value
    result = nn(value, weight[...])
    pre[0] = result
    merge(sums, result, tab, i)


def in_two(
    tab, video, pre, stats, pair, order, weight, out_low, centred, slope, first, squares, sums
):
    i = pl.program_id(0)

    @pl.when(i == 0)
    def _():
        sums[...] = jnp.zeros_like(sums)
        squares[...] = jnp.zeros_like(squares)

    mask = tab[0, i]
    source = nn(order[...], video[0]) * mask
    scaled = unit(pre[0], stats)
    branch = scaled * pair[0:1] + pair[1:2]
    before = source + branch
    gate = sigmoid(before)
    value = before * gate
    low = value.astype(BF16)
    out_low[0] = low
    centred[0] = scaled.astype(BF16)
    slope[0] = (gate + value * (1.0 - gate)).astype(BF16)
    squares[0:1] += down(jnp.square(branch)) * mask
    squares[1:2] += down(jnp.square(value)) * mask
    result = nn(low, weight[...])
    first[0] = result
    merge(sums, result, tab, i)


def shifted(piece, tap, backward=False):
    rows, cols = (tap // 3 == 0, tap % 3 == 0)
    side = HW // 2
    place = lax.broadcasted_iota(jnp.int32, piece.shape, 0)
    if rows:
        if backward:
            piece = jnp.where(place < QUARTER - side, pltpu.roll(piece, QUARTER - side, 0), 0.0)
        else:
            piece = jnp.where(place >= side, pltpu.roll(piece, side, 0), 0.0)
    if cols:
        col = lax.rem(place, side)
        if backward:
            piece = jnp.where(col < side - 1, pltpu.roll(piece, QUARTER - 1, 0), 0.0)
        else:
            piece = jnp.where(col > 0, pltpu.roll(piece, 1, 0), 0.0)
    return piece


def plane(tap):
    return (0 if tap // 3 == 1 else 2) + (0 if tap % 3 == 1 else 1)


def mid_two(tab, first, stats, pair, weight, taps_out, second, sums, store):
    t = pl.program_id(0)

    @pl.when(t == 0)
    def _():
        def frame(f, carry):
            z = unit(first[f], stats) * pair[0:1] + pair[1:2]
            value = z * sigmoid(z)
            for tap in range(9):
                at = plane(tap) * QUARTER
                piece = shifted(value[at : at + QUARTER], tap)
                store[tap, pl.ds(pl.multiple_of(f * QUARTER, QUARTER), QUARTER)] = piece.astype(BF16)
            return carry

        lax.fori_loop(0, T, frame, 0)

    left = store[t]
    taps_out[0] = left
    part = nn(left, weight[...])

    @pl.when(t == 0)
    def _():
        second[...] = part

    @pl.when(t > 0)
    def _():
        second[...] += part

    @pl.when(t == 8)
    def _():
        parts = [second[f * QUARTER : (f + 1) * QUARTER] for f in range(T)]
        mean, spread = whole_stats(parts, [tab[0, f] for f in range(T)], tab[3, 1])
        sums[0:1] = mean
        sums[1:2] = spread


def last_two(
    tab, second, stats, pair, weight, even, projection, hidden, third, short, sums, store
):
    t = pl.program_id(0)

    @pl.when(t == 0)
    def _():
        z = unit(second[...], stats) * pair[0:1] + pair[1:2]
        value = (z * sigmoid(z)).astype(BF16)
        store[...] = value
        hidden[...] = value

    masks = [tab[0, f] for f in range(T)]
    here = lanes(t, WIDE_TILE)
    for k, (out, result) in enumerate(
        (
            (third, nn(store[...], weight[...].reshape(M, WIDE_TILE))),
            (
                short,
                nn(even[...].reshape(HALF_ROWS, C), projection[...].reshape(C, WIDE_TILE)),
            ),
        )
    ):
        out[...] = result
        parts = [result[f * QUARTER : (f + 1) * QUARTER] for f in range(T)]
        mean, spread = whole_stats(parts, masks, tab[3, 1])
        sums[2 * k : 2 * k + 1, here] = mean
        sums[2 * k + 1 : 2 * k + 2, here] = spread


def finish(tab, third, short, stats, pairs, cotangent, result, grads, squares, sums):
    total = [jnp.zeros((1, WIDE_TILE), F32) for _ in range(5)]
    for f in range(T):
        rows = slice(f * QUARTER, (f + 1) * QUARTER)
        mask = tab[0, f]
        main = unit(third[rows], stats[0:2])
        side = unit(short[rows], stats[2:4])
        branch = main * pairs[0:1] + pairs[1:2]
        before = branch + (side * pairs[2:3] + pairs[3:4])
        gate = sigmoid(before)
        value = before * gate
        masked = value * mask
        result[rows] = masked.astype(BF16)
        grad = (gate + value * (1.0 - gate)) * (cotangent[rows].astype(F32) * mask)
        grads[rows] = grad
        for k, part in enumerate(
            (grad, grad * main, grad * side, jnp.square(branch) * mask, jnp.square(masked))
        ):
            total[k] = total[k] + down(part)
    here = lanes(pl.program_id(0), WIDE_TILE)
    for k in range(3):
        sums[k : k + 1, here] = total[k]
    sums[3:4, here] = jnp.zeros((1, WIDE_TILE), F32)
    for k in range(2):
        squares[k : k + 1] = total[3 + k]


def back_last(
    tab, grads, third, short, stats, pairs, totals, hidden, second, stats_mid, pair_mid, weight,
    even, projection,
    grad_joined, grad_even, grad_mid, sums, even_sum, hidden_sum, mains_all,
    sides_all, weight_store, projection_store, sems,
):
    t = pl.program_id(0)
    mains, sides = ([], [])
    for f in range(T):
        rows = slice(f * QUARTER, (f + 1) * QUARTER)
        mask = tab[0, f]
        main = unit(third[rows], stats[0:2])
        side = unit(short[rows], stats[2:4])
        grad = grads[rows]
        mains.append(
            norm_back(grad, main, stats[0:2], pairs[0:2], totals[0:2], mask, tab[3, 3]).astype(BF16)
        )
        side_totals = jnp.concatenate([totals[0:1], totals[2:3]], axis=0)
        sides.append(
            norm_back(grad, side, stats[2:4], pairs[2:4], side_totals, mask, tab[3, 3]).astype(BF16)
        )
    main = jnp.concatenate(mains, axis=0)
    side = jnp.concatenate(sides, axis=0)
    mains_all[t] = main
    sides_all[t] = side
    hidden_part = nt(main, weight[...].reshape(M, WIDE_TILE))
    even_part = nt(side, projection[...].reshape(C, WIDE_TILE))

    @pl.when(t == 0)
    def _():
        hidden_sum[...] = hidden_part
        even_sum[...] = even_part

    @pl.when(t > 0)
    def _():
        hidden_sum[...] += hidden_part
        even_sum[...] += even_part

    @pl.when(t == WIDE_STEPS - 1)
    def _():
        grad_even[...] = even_sum[...]
        centred = unit(second[...], stats_mid)
        z = centred * pair_mid[0:1] + pair_mid[1:2]
        gate = sigmoid(z)
        grad = hidden_sum[...] * (gate + z * gate * (1.0 - gate))
        grad_mid[...] = grad
        sums[0:1] = down(grad)
        sums[1:2] = down(grad * centred)

    copies = []
    for k in range(WIDE_STEPS):
        part = pl.ds(k * WIDE_TILE, WIDE_TILE)
        join = C // 8
        copies.append(
            (
                pltpu.make_async_copy(
                    projection_store.at[k], grad_joined.at[:, 0:join, part], sems.at[0, k]
                ),
                pltpu.make_async_copy(
                    weight_store.at[k], grad_joined.at[:, join : join + M // 8, part],
                    sems.at[1, k],
                ),
            )
        )

    def products(steps):
        def run():
            for k in steps:
                source = even[...].reshape(HALF_ROWS, C)
                projection_store[k] = tn(source, sides_all[k]).astype(BF16).reshape(8, C // 8, WIDE_TILE)
                copies[k][0].start()
                weight_store[k] = tn(hidden[...], mains_all[k]).astype(BF16).reshape(8, M // 8, WIDE_TILE)
                copies[k][1].start()

        return run

    def ended():
        for pair in copies:
            wait_all(pair)

    half = WIDE_STEPS // 2
    return [products(range(half)), products(range(half, WIDE_STEPS)), ended]


def back_mid(
    tab, grads, second, stats, pair, totals, taps_in, weight, first, stats_a, pair_a,
    grad_weight, grad_first, sums, low, store, held, sem,
):
    t = pl.program_id(0)
    load = pltpu.make_async_copy(taps_in, held, sem)

    @pl.when(t == 0)
    def _():
        load.start()
        for f in range(T):
            rows = slice(f * QUARTER, (f + 1) * QUARTER)
            centred = unit(second[rows], stats)
            grad = norm_back(grads[rows], centred, stats, pair, totals, tab[0, f], tab[3, 3])
            low[rows] = grad.astype(BF16)
        store[...] = jnp.zeros_like(store)

    part = nt(low[...], weight[...])
    for tap in range(9):

        @pl.when(t == tap)
        def _(tap=tap):
            at = plane(tap) * QUARTER
            for f in range(T):
                piece = shifted(part[f * QUARTER : (f + 1) * QUARTER], tap, True)
                store[f, at : at + QUARTER] += piece

    @pl.when(t == 8)
    def _():
        sums[...] = jnp.zeros_like(sums)

        def frame(f, carry):
            centred = unit(first[f], stats_a)
            z = centred * pair_a[0:1] + pair_a[1:2]
            gate = sigmoid(z)
            grad = store[f] * (gate + z * gate * (1.0 - gate))
            grad_first[f] = grad
            sums[0:1] += down(grad)
            sums[1:2] += down(grad * centred)
            return carry

        lax.fori_loop(0, T, frame, 0)

    def products(steps):
        def run():
            if steps[0] == 0:
                load.wait()
            for tap in steps:
                value = tn(held[tap], low[...])
                grad_weight[:, tap * M : (tap + 1) * M] = value.astype(BF16)

        return run

    return [products(range(5)), products(range(5, 9))]


def back_in_two(
    tab, grads, first, stats, pair, totals, out_low, weight, even, slope, centred,
    grad_weight, grad_before, sums, lows, held, sem,
):
    i = pl.program_id(0)
    load = pltpu.make_async_copy(out_low, held, sem)
    scaled = unit(first[0], stats)
    low = norm_back(grads[0], scaled, stats, pair, totals, tab[0, i], tab[3, 2]).astype(BF16)
    grad = nt(low, weight[...])
    lows[i] = low

    @pl.when(i == 0)
    def _():
        load.start()
        sums[...] = jnp.zeros_like(sums)

    grad = jnp.concatenate([grad[0:QUARTER] + even[...], grad[QUARTER:]], axis=0)
    grad = grad * slope[0].astype(F32)
    grad_before[0] = grad.astype(BF16)
    sums[0:1] += down(grad)
    sums[1:2] += down(grad * centred[0].astype(F32))

    def products(steps):
        def run():
            if steps[0] == 0:
                load.wait()
            for k in steps:
                part = slice(k * WIDE_TILE, (k + 1) * WIDE_TILE)
                source = held[:, :, part].reshape(ROWS, WIDE_TILE)
                grad_weight[part] = tn(source, lows[...].reshape(ROWS, M)).astype(BF16)

        return run

    half = WIDE_STEPS // 2
    return [products(range(half)), products(range(half, WIDE_STEPS))]


def back_out_one(
    tab, grads, centred, stats, pair, totals, hidden, weight, order, agg, stats_two, pair_two,
    grad_weight, grad_two, sums, lows, held, sem,
):
    i = pl.program_id(0)
    load = pltpu.make_async_copy(hidden, held, sem)
    low = norm_back(
        grads[0].astype(F32), centred[0].astype(F32), stats, pair, totals, tab[0, i], tab[3, 2]
    ).astype(BF16)
    grad = nt(low, weight[...])
    lows[i] = low

    @pl.when(i == 0)
    def _():
        load.start()
        sums[...] = jnp.zeros_like(sums)

    high = grad.astype(BF16)
    rest = (grad - high.astype(F32)).astype(BF16)
    grad = tn(order[...], high) + tn(order[...], rest)
    scaled = unit(agg[0], stats_two)
    z = scaled * pair_two[0:1] + pair_two[1:2]
    gate = sigmoid(z)
    grad = grad * (gate + z * gate * (1.0 - gate))
    grad_two[0] = grad
    sums[0:1] += down(grad)
    sums[1:2] += down(grad * scaled)

    def products(steps):
        def run():
            if steps[0] == 0:
                load.wait()
            for k in steps:
                part = slice(k * WIDE_TILE, (k + 1) * WIDE_TILE)
                source = lows[:, :, part].reshape(ROWS, WIDE_TILE)
                grad_weight[:, part] = tn(held[...].reshape(ROWS, M), source).astype(BF16)

        return run

    half = WIDE_STEPS // 2
    return [products(range(half)), products(range(half, WIDE_STEPS))]


def mta_backward(
    ndp, ntm, items, edge, tab, grads, agg, stats_two, pair_two, totals, pre, stats, pair, sigma,
    ext, blended, kernels, taps, reduce_low, conv_low, expand, windows, later, snext, pooled, *refs,
):
    count = len(items)
    sources, refs = (refs[:count], refs[count:])
    grad_one, totals_out, grad_mta, grad_reduce, grad_conv, grad_expand, grad_bias = refs[:7]
    grad_taps, refs = (refs[7], refs[8:])
    outs, refs = (refs[:count], refs[count:])
    mixed, low_store, store, back, parts, edge_send, edge_recv, mta_sum = refs[:8]
    k_store, k_send, k_recv, gate_sum, ssems, rsems, tiles = refs[8:15]
    swap_refs, refs = (refs[15:19], refs[19:])
    sums = swap_refs[0]
    has_prev, has_next, prev, following = neighbours(ntm)
    greet(ndp, ntm)
    swap = swap_steps(ndp, ntm, None, None, totals_out, *swap_refs)
    steps = [[], [], [], [], []]
    if count:
        steps = scatter_steps(ndp, ntm, items, sources, outs, refs, True)

    def start(f, carry):
        centred = unit(agg[f], stats_two)
        mixed[f] = norm_back(
            grads[f], centred, stats_two, pair_two, totals, tab[0, f], tab[3, 2]
        )
        return carry

    met(ndp, ntm)
    run_steps(steps[0])
    lax.fori_loop(0, T, start, 0)

    @pl.when(jnp.logical_not(has_prev))
    def _():
        edge_recv[:, :, 0] = jnp.zeros((3, CLIPS, PIX, GW), BF16)

    @pl.when(jnp.logical_not(has_next))
    def _():
        edge_recv[:, :, 1] = jnp.zeros((3, CLIPS, PIX, GW), BF16)

    grad_taps[...] = jnp.zeros_like(grad_taps)

    def edges(group, clip):
        k = group * CLIPS + clip
        left = sent(
            edge_send.at[group, clip, 0], edge_recv.at[group, clip, 1], ssems.at[k, 0],
            rsems.at[k, 0], prev,
        )
        right = sent(
            edge_send.at[group, clip, 1], edge_recv.at[group, clip, 0], ssems.at[k, 1],
            rsems.at[k, 1], following,
        )
        return left, right

    def convolve(group, clip):
        low, high = ((group + 1) * GW, (group + 2) * GW)
        row = [taps[group * 3 + k : group * 3 + k + 1] for k in range(3)]

        def part(step, carry):
            f = clip * SPAN + step
            value = mixed[f, :, low:high]
            if group < 2:
                value = value + mixed[f, :, low + GW : high + GW]
            value = value.astype(BF16)
            low_store[f] = value
            spread_taps(store.at[step], value)
            result = jnp.zeros((PIX, GW), F32)
            for tap in range(9):
                other = 8 - tap
                patch = store[
                    step,
                    (tap // 3) * HW : (tap // 3) * HW + PIX,
                    (tap % 3) * GW : (tap % 3 + 1) * GW,
                ]
                at = other % 3 * GW
                result += nt(patch, kernels[group, other // 3, at : at + GW])
            for k in range(3):
                source = ext[group, clip, step + k].astype(F32)
                at = group * 3 + k
                grad_taps[at : at + 1] += down(result * source)
            parts[step] = result
            return carry

        lax.fori_loop(0, SPAN, part, 0)
        edge_send[group, clip, 0] = (row[0] * parts[0]).astype(BF16)
        edge_send[group, clip, 1] = (row[2] * parts[1]).astype(BF16)
        left, right = edges(group, clip)

        @pl.when(has_prev)
        def _():
            left.start()

        @pl.when(has_next)
        def _():
            right.start()

        back[clip, 0] = row[1] * parts[0] + row[0] * parts[1]
        back[clip, 1] = row[2] * parts[0] + row[1] * parts[1]

    def products(group, clip):
        def product(step, carry):
            f = clip * SPAN + step
            spread_taps(store.at[step], blended[group, f])
            for k in range(3):
                mta_sum[k] += tn(window(store.at[step], k), low_store[f])
            return carry

        lax.fori_loop(0, SPAN, product, 0)

    def collect(group, clip):
        low, high = ((group + 1) * GW, (group + 2) * GW)
        left, right = edges(group, clip)

        @pl.when(has_prev)
        def _():
            left.wait_send()
            right.wait_recv()

        @pl.when(has_next)
        def _():
            right.wait_send()
            left.wait_recv()

        def put(step, carry):
            f = clip * SPAN + step
            total = back[clip, step] + edge_recv[group, clip, step].astype(F32)
            mixed[f, :, low:high] = total * tab[0, f]
            return carry

        lax.fori_loop(0, SPAN, put, 0)

    for group in (2, 1, 0):
        mta_sum[...] = jnp.zeros_like(mta_sum)
        for clip in range(CLIPS):
            if group < 2:
                collect(group + 1, clip)
            convolve(group, clip)
            products(group, clip)
        for tap in range(9):
            at = tap % 3 * GW
            tiles[group * 9 + tap] = mta_sum[tap // 3, at : at + GW].astype(BF16)
        run_steps(steps[3 - group])
    for clip in range(CLIPS):
        collect(0, clip)

    def gates(f, carry):
        z = unit(pre[f], stats) * pair[0:1] + pair[1:2]
        gate_sum[f] = down(mixed[f] * (z * sigmoid(z)))
        return carry

    lax.fori_loop(0, T, gates, 0)
    gate = sigma[...]
    excite = rows_of([gate_sum[f] for f in range(T)]) * gate * (1.0 - gate)
    grad_bias[...] = down(excite)
    grad_expand[...] = tn_exact(pooled[...], excite)
    change = nt_exact(excite, expand[...]) * (later[...] * (1.0 / PIX))
    change_low = change.astype(BF16)
    change_wide = change_low.astype(F32)
    for tap in range(9):
        rows = rows_of([snext[f, tap : tap + 1] for f in range(T)])
        grad_conv[tap] = tn_exact(rows, change_wide)[0:R]
        k_store[tap] = nt(change_low, conv_low[tap].astype(BF16))
    index = lax.broadcasted_iota(jnp.int32, (16, GW), 0)

    def stacked(f):
        result = jnp.zeros((16, GW), F32)
        for tap in range(9):
            result = jnp.where(index == tap, k_store[tap, f : f + 1], result)
        return result

    for clip in range(CLIPS):
        k_send[clip] = stacked(clip * SPAN + 1)
    onward = sent(k_send, k_recv, ssems.at[9, 0], rsems.at[9, 0], following)

    @pl.when(has_next)
    def _():
        onward.start()
        onward.wait_send()

    @pl.when(has_prev)
    def _():
        onward.wait_recv()

    @pl.when(jnp.logical_not(has_prev))
    def _():
        k_recv[...] = jnp.zeros_like(k_recv)

    sums[...] = jnp.zeros_like(sums)
    grad_reduce[...] = jnp.zeros_like(grad_reduce)
    for f in range(T):
        spread = k_recv[f // SPAN] if f % SPAN == 0 else stacked(f - 1)
        motion = tn_exact(windows[...].astype(F32), spread) - change[f : f + 1]
        motion_low = motion.astype(BF16)
        centred = unit(pre[f], stats)
        z = centred * pair[0:1] + pair[1:2]
        gate = sigmoid(z)
        hidden = z * gate
        grad_reduce[...] += tn(motion_low, hidden.astype(BF16))[0:R]
        grad = mixed[f] * (1.0 + sigma[f : f + 1]) + nt(motion_low, reduce_low[...])
        grad = grad * (gate + hidden * (1.0 - gate))
        grad_one[f] = grad
        sums[0:1] += down(grad)
        sums[1:2] += down(grad * centred)
    swap[0]()
    if edge:
        for place in range(grad_mta.shape[1] // GW):
            grad_mta[:, place * GW : (place + 1) * GW] = edge_from_tiles(
                tiles, place, edge, grad_mta.shape[1] // ntm
            )
    else:
        grad_mta[...] = tiles[...]
    swap[1]()
    swap[2]()


def back_in_one(
    tab, grads, pre, stats, pair, totals, video, weight, order, grad_before,
    grad_weight, grad_video, lows, held, sem,
):
    i = pl.program_id(0)
    load = pltpu.make_async_copy(video, held, sem)
    centred = unit(pre[0], stats)
    low = norm_back(grads[0], centred, stats, pair, totals, tab[0, i], tab[3, 2]).astype(BF16)
    lows[i] = low

    @pl.when(i == 0)
    def _():
        load.start()

    grad = nt(low, weight[...]) + tn(order[...], grad_before[0])
    grad_video[0] = (grad * tab[0, i]).astype(BF16)

    def products(steps):
        def run():
            if steps[0] == 0:
                load.wait()
            for k in steps:
                part = slice(k * WIDE_TILE, (k + 1) * WIDE_TILE)
                source = held[:, :, part].reshape(ROWS, WIDE_TILE)
                grad_weight[part] = tn(source, lows[...].reshape(ROWS, M)).astype(BF16)

        return run

    half = WIDE_STEPS // 2
    return [products(range(half)), products(range(half, WIDE_STEPS))]


def final_sums(
    ndp, ntm, items, z_count, reduce, expand, conv, bias, taps, source_squares, one_squares, last_squares,
    *refs,
):
    count = len(items)
    sources, refs = (refs[:count], refs[count:])
    z_sources, refs = (refs[:z_count], refs[z_count:])
    reduce_out, expand_out, conv_out, bias_out, taps_out, squares_out = refs[:6]
    outs, refs = (refs[6 : 6 + count], refs[6 + count :])
    z_outs, refs = (refs[:z_count], refs[z_count:])
    packed, summed, first, second, sems = refs[:5]
    greet(ndp, ntm)
    large, over = ([[], [], [], [], []], [[], []])
    if count:
        over = z_steps(ntm, z_sources, z_outs, refs[5 : 6 + z_count])
        large = scatter_steps(ndp, ntm, items, sources, outs, refs[6 + z_count :])
    small = all_sums_steps(ndp, ntm, packed, summed, first, second, sems)
    packed[...] = jnp.zeros_like(packed)
    for k in range(M // GW):
        part = slice(k * GW, (k + 1) * GW)
        packed[k * R : (k + 1) * R] = reduce[:, part]
        packed[128 + k * R : 128 + (k + 1) * R] = expand[0:R, part]
        packed[544 + k : 545 + k] = bias[:, part]
    for tap in range(9):
        packed[256 + tap * R : 256 + (tap + 1) * R] = conv[tap]
    packed[552:561] = taps[...]
    lane = lax.broadcasted_iota(jnp.int32, (1, GW), 1)
    row = jnp.zeros((1, GW), F32)
    values = [source_squares[0:1], one_squares[0:1], one_squares[1:2]]
    values += [last_squares[0:1], last_squares[1:2]]
    for k, value in enumerate(values):
        row = jnp.where(lane == k, jnp.sum(value, axis=1, keepdims=True), row)
    packed[568:569] = row
    met(ndp, ntm)
    run_steps(large[0])
    small[0]()
    for k in range(1, 5):
        if k == 2:
            run_steps(over[0])
        small[k]()
        run_steps(large[k])
    run_steps(over[1])
    for k in range(M // GW):
        part = slice(k * GW, (k + 1) * GW)
        reduce_out[:, part] = summed[k * R : (k + 1) * R]
        expand_out[:, part] = summed[128 + k * R : 128 + (k + 1) * R]
        bias_out[:, part] = summed[544 + k : 545 + k]
    for tap in range(9):
        conv_out[tap] = summed[256 + tap * R : 256 + (tap + 1) * R]
    taps_out[...] = summed[552:561]
    squares_out[...] = summed[568:576]


def parity_order():
    order = np.zeros((PIX, PIX), np.float32)
    for y in range(HW):
        for x in range(HW):
            row = ((y % 2) * 2 + x % 2) * QUARTER + (y // 2) * (HW // 2) + x // 2
            order[row, y * HW + x] = 1.0
    return order


def window_rows():
    rows = np.zeros((16, PIX), np.float32)
    for tap in range(9):
        for y in range(HW):
            for x in range(HW):
                inside = 0 <= y - (tap // 3 - 1) < HW and 0 <= x - (tap % 3 - 1) < HW
                rows[tap, y * HW + x] = float(inside)
    return rows


def fetch(shard):
    partly = lax.all_gather(shard.astype(BF16), "tm", axis=1, tiled=True)
    return lax.all_gather(partly, "dp", axis=0, tiled=True)


def deliver(gradient):
    partly = lax.psum_scatter(gradient, "dp", scatter_dimension=0, tiled=True)
    return lax.psum_scatter(partly, "tm", scatter_dimension=1, tiled=True).astype(F32)


def padded(values, rows, cols):
    return jnp.pad(values, ((0, rows - values.shape[0]), (0, cols - values.shape[1])))


def tables(lengths, ndp, ntm):
    d, t = (lax.axis_index("dp"), lax.axis_index("tm"))
    grouped = lengths.reshape(ndp, CLIPS)
    starts = jnp.arange(ntm, dtype=jnp.int32) * SPAN
    counts = jnp.sum(jnp.clip(grouped[:, :, None] - starts, 0, SPAN), axis=1).astype(F32)
    own = lax.dynamic_slice_in_dim(lengths, d * CLIPS, CLIPS)
    stamps = t * SPAN + jnp.arange(SPAN, dtype=jnp.int32)
    mask = (stamps[None, :] < own[:, None]).astype(F32).reshape(T)
    later = (stamps[None, :] + 1 < own[:, None]).astype(F32).reshape(T)
    total = jnp.sum(lengths).astype(F32)
    before = jnp.cumsum(mask) - mask
    held = jnp.maximum(before + mask, 1.0)
    local = jnp.maximum(jnp.sum(mask), 1.0)
    full, half = (1.0 / PIX, 1.0 / QUARTER)
    last = jnp.stack([full / local, half / local, full / total, half / total, total, total])
    tab = jnp.stack([mask, mask / held, before * mask / held, last])
    width = max(ndp, ntm)
    column = lax.dynamic_slice_in_dim(counts, t, 1, axis=1)[:, 0]
    sums = jnp.sum(counts, axis=0)

    def row(values):
        return jnp.pad(values, (0, width - values.shape[0]))

    swap = jnp.stack(
        [
            row(column / jnp.maximum(jnp.sum(column), 1.0)),
            row(column),
            row(sums / total),
            row(sums),
            jnp.broadcast_to(1.0 / total, (width,)),
        ]
    )
    return (tab, swap, later, total)


def local(
    video, lengths, mid_norms, wide_norms, taps, me_reduce, me_conv, me_expand, me_bias,
    w_in1, w_mta, w_out1, w_in2, w_mid2, w_out2, w_proj, grad_out,
):
    ndp, ntm = (lax.axis_size("dp"), lax.axis_size("tm"))
    fast = ndp == 8 and ntm == 4
    order = jnp.asarray(parity_order(), BF16)
    windows = jnp.asarray(window_rows(), BF16)
    frames = video.reshape(T, PIX, C)
    cotangent = grad_out.reshape(HALF_ROWS, C)
    bias = me_bias.reshape(1, M)
    tap_rows = taps.reshape(9, GW)
    main_pairs = jnp.concatenate([wide_norms[1], wide_norms[2]], axis=0)
    stage = functools.partial(staged, ndp=ndp, ntm=ntm)

    def gathered(rows):
        return lax.all_gather(rows, "dp", axis=0, tiled=True)

    edge = w_mta.shape[1]
    edge_wide = -(-edge // GW) * GW
    small = (8, GW)
    if fast:
        shard_rows = [w_in1.shape, (w_mta.shape[0], edge_wide), w_out1.shape, w_mid2.shape]
        wide_rows = [(rows, cols * ntm) for rows, cols in shard_rows]
        (
            full_in1, full_mta, rows_out1, rows_mid2, tab, swap, later, reduce_low,
            conv_low, expand,
        ) = remote_call(
            "first_gather", functools.partial(first_gather, ndp, ntm), 1,
            [SCALARS] + [WHOLE] * 7, [WHOLE] * 10,
            [shaped((4, 2) + shape, BF16) for shape in wide_rows[:2]]
            + [shaped(shape, BF16) for shape in wide_rows[2:]]
            + [
                shaped(small), shaped(small), shaped(small), shaped((M, GW), BF16),
                shaped((9, GW, GW)), shaped((GW, M)),
            ],
            [VMEM(shape, BF16) for shape in shard_rows] + [DMA((4, 3, ntm)), DMA((2, 4, 2, 2))],
            1 << 24,
            lengths, w_in1, w_mta, w_out1, w_mid2, me_reduce, me_conv.reshape(9, R, R),
            me_expand,
        )
        total = swap[5, 0]
        full_in1 = full_in1.reshape(C, M)
        full_mta = full_mta.reshape(GW, ntm * edge_wide)
        full_out1, full_mid2 = (gathered(rows_out1), gathered(rows_mid2))
    else:
        tab, swap, later, total = tables(lengths, ndp, ntm)
        later = jnp.broadcast_to(jnp.pad(later, (0, 2))[:, None], small)
        reduce_low = padded(me_reduce, M, GW).astype(BF16)
        conv_low = jnp.pad(me_conv.reshape(9, R, R), ((0, 0), (0, GW - R), (0, GW - R)))
        conv_low = conv_low.astype(BF16).astype(F32)
        expand = padded(me_expand, GW, M)
        full_in1, full_mta, full_out1, full_in2, full_mid2, full_out2, full_proj = [
            fetch(shard) for shard in (w_in1, w_mta, w_out1, w_in2, w_mid2, w_out2, w_proj)
        ]
        full_mta = jnp.transpose(full_mta.reshape(GW, 27, GW), (1, 0, 2))

    frame_wide, frame_mid = (at_first((1, PIX, C)), at_first((1, PIX, M)))
    pair_mid, pair_wide = (fixed((2, M)), fixed((2, C)))
    wide_low, mid_wide = (shaped((T, PIX, C), BF16), shaped((T, PIX, M)))
    rows_wide = at_last((HALF_ROWS, WIDE_TILE))
    even_spec = fixed((T, QUARTER, C))
    order_spec = fixed((PIX, PIX))
    half_mid = fixed((HALF_ROWS, M))
    four = at_last((4, WIDE_TILE))
    ins_tab = (tab, SCALARS)
    mids = [(mid_norms[k], pair_mid) for k in range(4)]
    order_in = (order, order_spec)

    pre, squares_source, stats_one, *rows = stage(
        "in_one", 2, steps=T, body=in_one,
        ins=[ins_tab, (frames, frame_wide), (full_in1, fixed((C, M)))],
        outs=[(mid_wide, frame_mid), (shaped((1, C)), fixed((1, C))), LOCAL],
        scratch=[], cost=2 * ROWS * C * M, swap=(swap, PIX, (2, M)),
        carry=(w_out2, w_in2) if fast else (),
    )
    rows_out2, rows_in2 = rows if fast else (None, None)

    frame_low = (T, PIX, GW)
    carried = [w_proj, rows_in2] if fast else []
    agg, stats_two, ext, blended, sigma, snext, pooled, kernels, *rows = remote_call(
        "mta_forward", functools.partial(mta_forward, ndp, ntm, fast, edge), 3,
        [SCALARS] * 2 + [WHOLE] * (11 + len(carried)),
        [WHOLE] * (8 + len(carried)),
        [
            mid_wide, shaped((2, M)), shaped((3, CLIPS, 4, PIX, GW), BF16),
            shaped((3,) + frame_low, BF16), shaped((8, M)), shaped((T, 16, GW)), shaped((8, GW)),
            shaped((3, 3, 3 * GW, GW), BF16),
        ]
        + ([shaped((w_proj.shape[0], C), BF16), shaped((4, 2, C // 8, M), BF16)] if fast else []),
        [
            VMEM((T, PIX, M), F32), VMEM((SPAN, PIX + 2 * HW, 3 * GW), BF16),
            VMEM((3, CLIPS, 4, PIX, GW), BF16), VMEM((2, CLIPS, SPAN, PIX, GW), F32),
            VMEM((T, 1, M), F32), VMEM((T, 16, GW), F32), VMEM((CLIPS, 16, GW), F32),
            VMEM((CLIPS, 16, GW), F32), DMA((10, 2)), DMA((10, 2)),
        ]
        + swap_scratch(ndp, ntm, (2, M))
        + (
            [VMEM(w_proj.shape, BF16), DMA((8, 3, ntm)), DMA((1, 1)), DMA((4, 2, 2))]
            if fast
            else []
        ),
        2 * ROWS * 9 * GW * GW * 3,
        swap, tab, pre, stats_one, mid_norms[0], reduce_low, conv_low, expand, bias, full_mta,
        tap_rows, windows, later, *carried,
    )
    join = C // 8
    wide_tile = (8, join, WIDE_TILE)
    if fast:
        full_in2 = rows[1].reshape(C, M)
        joined = gathered(jnp.concatenate([rows[0], rows_out2], axis=0))
        joined = joined.reshape(8, join + M // 8, C)
        proj_in = (joined, pl.BlockSpec(wide_tile, lambda i: (0, 0, i)))
        out2_in = (
            joined, pl.BlockSpec((8, M // 8, WIDE_TILE), lambda i: (0, C // M, i)),
        )
    else:
        proj_in = (full_proj.reshape(8, join, C), pl.BlockSpec(wide_tile, lambda i: (0, 0, i)))
        out2_in = (
            full_out2.reshape(8, M // 8, C),
            pl.BlockSpec((8, M // 8, WIDE_TILE), lambda i: (0, 0, i)),
        )

    hidden_two, pre_three, stats_three = stage(
        "out_one", 4, steps=T, body=out_one,
        ins=[
            ins_tab, (agg, frame_mid), (stats_two, pair_mid), mids[1], order_in,
            (full_out1, fixed((M, C))),
        ],
        outs=[(shaped((T, PIX, M), BF16), frame_mid), (shaped((T, PIX, C)), frame_wide), LOCAL],
        scratch=[], cost=2 * ROWS * C * M, swap=(swap, PIX, (2, C)),
    )

    out_low, centred_three, slope, first_two, squares_one, stats_alpha = stage(
        "in_two", 5, steps=T, body=in_two,
        ins=[
            ins_tab, (frames, frame_wide), (pre_three, frame_wide), (stats_three, pair_wide),
            (wide_norms[0], pair_wide), order_in, (full_in2, fixed((C, M))),
        ],
        outs=[
            (wide_low, frame_wide), (wide_low, frame_wide), (wide_low, frame_wide),
            (mid_wide, frame_mid), (shaped((2, C)), pair_wide), LOCAL,
        ],
        scratch=[], cost=2 * ROWS * C * M, swap=(swap, PIX, (2, M)),
    )

    stride_taps, second_two, stats_beta = stage(
        "mid_two", 6, steps=9, body=mid_two,
        ins=[
            ins_tab, (first_two, fixed((T, PIX, M))), (stats_alpha, pair_mid), mids[2],
            (full_mid2, at_last((M, M))),
        ],
        outs=[
            (shaped((9, HALF_ROWS, M), BF16), at_first((1, HALF_ROWS, M))),
            (shaped((HALF_ROWS, M)), half_mid), LOCAL,
        ],
        scratch=[VMEM((9, HALF_ROWS, M), BF16)], cost=2 * HALF_ROWS * 9 * M * M,
        swap=(swap, QUARTER, (2, M)),
    )

    hidden_beta, third_two, short_two, stats_last = stage(
        "last_two", 7, steps=WIDE_STEPS, body=last_two,
        ins=[
            ins_tab, (second_two, half_mid), (stats_beta, pair_mid), mids[3],
            out2_in, (out_low, even_spec), proj_in,
        ],
        outs=[
            (shaped((HALF_ROWS, M), BF16), half_mid), (shaped((HALF_ROWS, C)), rows_wide),
            (shaped((HALF_ROWS, C)), rows_wide), LOCAL,
        ],
        scratch=[VMEM((HALF_ROWS, M), BF16)], cost=2 * HALF_ROWS * C * (M + C),
        swap=(swap, QUARTER, (4, C)),
    )

    result, grad_before_two, squares_last, totals_last = stage(
        "finish", 8, steps=WIDE_STEPS, body=finish,
        ins=[
            ins_tab, (third_two, rows_wide), (short_two, rows_wide), (stats_last, four),
            (main_pairs, four), (cotangent, rows_wide),
        ],
        outs=[
            (shaped((HALF_ROWS, C), BF16), rows_wide), (shaped((HALF_ROWS, C)), rows_wide),
            (shaped((2, C)), at_last((2, WIDE_TILE))), LOCAL,
        ],
        scratch=[], cost=1 << 28, swap=(swap, None, (4, C)),
    )

    wide_store = VMEM((WIDE_STEPS, HALF_ROWS, WIDE_TILE), BF16)
    grad_joined, grad_even, grad_beta, totals_beta = stage(
        "back_last", 9, steps=WIDE_STEPS, body=back_last,
        ins=[
            ins_tab, (grad_before_two, rows_wide), (third_two, rows_wide), (short_two, rows_wide),
            (stats_last, four), (main_pairs, four), (totals_last, four), (hidden_beta, half_mid),
            (second_two, half_mid), (stats_beta, pair_mid), mids[3],
            out2_in, (out_low, even_spec), proj_in,
        ],
        outs=[
            (shaped((8, join + M // 8, C), BF16), ANY),
            (shaped((HALF_ROWS, C)), fixed((HALF_ROWS, C))), (shaped((HALF_ROWS, M)), half_mid),
            LOCAL,
        ],
        scratch=[
            VMEM((HALF_ROWS, C), F32), VMEM((HALF_ROWS, M), F32), wide_store, wide_store,
            VMEM((WIDE_STEPS, 8, M // 8, WIDE_TILE), BF16),
            VMEM((WIDE_STEPS, 8, join, WIDE_TILE), BF16),
            DMA((2, WIDE_STEPS)),
        ],
        cost=4 * HALF_ROWS * C * (M + C), swap=(swap, None, (2, M)),
    )

    if fast:
        joined_part = grad_joined.reshape(8 * (join + M // 8), C)
        joined_part = lax.psum_scatter(joined_part, "dp", scatter_dimension=0, tiled=True)

    def scattered(*pairs):
        if not fast:
            return {}
        return {"items": [item for item, _ in pairs], "sources": [source for _, source in pairs]}

    grad_w_mid2, grad_alpha, totals_alpha = stage(
        "back_mid", 10, steps=9, body=back_mid,
        ins=[
            ins_tab, (grad_beta, half_mid), (second_two, half_mid), (stats_beta, pair_mid),
            mids[3], (totals_beta, pair_mid), (stride_taps, ANY), (full_mid2, at_last((M, M))),
            (first_two, fixed((T, PIX, M))), (stats_alpha, pair_mid), mids[2],
        ],
        outs=[
            (shaped((M, 9 * M), BF16), fixed((M, 9 * M))), (mid_wide, fixed((T, PIX, M))), LOCAL,
        ],
        scratch=[
            VMEM((HALF_ROWS, M), BF16), VMEM((T, PIX, M), F32), VMEM((9, HALF_ROWS, M), BF16),
            DMA,
        ],
        cost=4 * HALF_ROWS * 9 * M * M, swap=(swap, None, (2, M)),
    )
    cube_mid2 = cubed(grad_w_mid2) if fast else None

    grad_w_in2, grad_before_one, totals_three = stage(
        "back_in_two", 11, steps=T, body=back_in_two,
        ins=[
            ins_tab, (grad_alpha, frame_mid), (first_two, frame_mid), (stats_alpha, pair_mid),
            mids[2], (totals_alpha, pair_mid), (out_low, ANY), (full_in2, fixed((C, M))),
            (grad_even, at_first((QUARTER, C))), (slope, frame_wide), (centred_three, frame_wide),
        ],
        outs=[(shaped((C, M), BF16), fixed((C, M))), (wide_low, frame_wide), LOCAL],
        scratch=[VMEM((T, PIX, M), BF16), VMEM((T, PIX, C), BF16), DMA],
        cost=4 * ROWS * C * M, swap=(swap, None, (2, C)),
    )
    cube_in2 = cubed(grad_w_in2) if fast else None

    grad_w_out1, grad_two, totals_two = stage(
        "back_out_one", 12, steps=T, body=back_out_one,
        ins=[
            ins_tab, (grad_before_one, frame_wide), (centred_three, frame_wide),
            (stats_three, pair_wide), (wide_norms[0], pair_wide), (totals_three, pair_wide),
            (hidden_two, ANY), (full_out1, fixed((M, C))), order_in, (agg, frame_mid),
            (stats_two, pair_mid), mids[1],
        ],
        outs=[(shaped((M, C), BF16), fixed((M, C))), (mid_wide, frame_mid), LOCAL],
        scratch=[VMEM((T, PIX, C), BF16), VMEM((T, PIX, M), BF16), DMA],
        cost=4 * ROWS * C * M, swap=(swap, None, (2, M)),
    )
    cube_out1 = cubed(grad_w_out1) if fast else None

    if fast:
        totals_two, joined_part = lax.optimization_barrier((totals_two, joined_part))
        sent_joined = lax.psum_scatter(joined_part, "tm", scatter_dimension=1, tiled=True)
    early = scattered(((0, 64, 9 * M, 2), cube_mid2), ((0, 256, M, 2), cube_in2))
    items = early.get("items", [])
    mta_shape = (GW, ntm * edge_wide) if fast else (27, GW, GW)
    (
        grad_one, totals_one, grad_w_mta, grad_reduce, grad_conv, grad_expand, grad_bias, grad_taps,
        *sent_d,
    ) = remote_call(
        "mta_backward",
        functools.partial(mta_backward, ndp, ntm, items, edge if fast else None), 13,
        [SCALARS] + [WHOLE] * 20 + [ANY] * len(items),
        [WHOLE] * (8 + len(items)),
        [
            mid_wide, shaped((2, M)), shaped(mta_shape, BF16), shaped((R, M)),
            shaped((9, R, GW)), shaped((GW, M)), shaped((1, M)), shaped((9, GW)),
        ]
        + [shaped((rows, cols), BF16) for _, rows, cols, _ in items],
        [
            VMEM((T, PIX, M), F32), VMEM(frame_low, BF16),
            VMEM((SPAN, PIX + 2 * HW, 3 * GW), BF16), VMEM((CLIPS, SPAN, PIX, GW), F32),
            VMEM((SPAN, PIX, GW), F32),
            VMEM((3, CLIPS, 2, PIX, GW), BF16), VMEM((3, CLIPS, 2, PIX, GW), BF16),
            VMEM((3, 3 * GW, GW), F32), VMEM((9, 8, GW), F32), VMEM((CLIPS, 16, GW), F32),
            VMEM((CLIPS, 16, GW), F32), VMEM((T, 1, M), F32), DMA((10, 2)), DMA((10, 2)),
            VMEM((27, GW, GW), BF16),
        ]
        + swap_scratch(ndp, ntm, (2, M))
        + (scatter_scratch(items, ntm) if items else []),
        4 * ROWS * 9 * GW * GW * 3,
        tab, grad_two, agg, stats_two, mid_norms[1], totals_two, pre, stats_one, mid_norms[0],
        sigma, ext, blended, kernels, tap_rows, reduce_low, conv_low, expand, windows, later,
        snext, pooled, *early.get("sources", []),
    )

    if fast:
        totals_one, sent_joined = lax.optimization_barrier((totals_one, sent_joined))
    grad_w_in1, grad_frames = stage(
        "back_in_one", 14, steps=T, body=back_in_one,
        ins=[
            ins_tab, (grad_one, frame_mid), (pre, frame_mid), (stats_one, pair_mid), mids[0],
            (totals_one, pair_mid), (frames, ANY), (full_in1, fixed((C, M))), order_in,
            (grad_before_one, frame_wide),
        ],
        outs=[(shaped((C, M), BF16), fixed((C, M))), (wide_low, frame_wide)],
        scratch=[VMEM((T, PIX, M), BF16), VMEM((T, PIX, C), BF16), DMA],
        cost=4 * ROWS * C * M,
    )

    late = scattered(
        ((0, 64, C, 2), cube_out1),
        ((0, 16, ntm * edge_wide, 1), cubed(grad_w_mta) if fast else None),
        ((0, 256, M, 2), cubed(grad_w_in1) if fast else None),
    )
    items = late.get("items", [])
    z_shapes = [part.shape for part in sent_d]
    unit_rows = 8 * ndp * ntm
    rows = -(-576 // unit_rows) * unit_rows
    sum_reduce, sum_expand, sum_conv, sum_bias, sum_taps, squares, *sent_f = remote_call(
        "final_sums", functools.partial(final_sums, ndp, ntm, items, len(z_shapes)), 15,
        [WHOLE] * 8 + [ANY] * len(items) + [WHOLE] * len(z_shapes),
        [WHOLE] * (6 + len(items) + len(z_shapes)),
        [
            shaped((R, M)), shaped((R, M)), shaped((9, R, GW)), shaped((1, M)), shaped((9, GW)),
            shaped((8, GW)),
        ]
        + [shaped((rows_, cols // ntm)) for _, rows_, cols, _ in items]
        + [shaped((rows_, cols // ntm)) for rows_, cols in z_shapes],
        [VMEM((rows, GW), F32), VMEM((rows, GW), F32)]
        + all_sums_scratch(ndp, ntm, rows)
        + (z_scratch(z_shapes, ntm) + scatter_scratch(items, ntm) if items else []),
        1 << 26,
        grad_reduce, grad_expand, grad_conv, grad_bias, grad_taps, squares_source, squares_one,
        squares_last, *late.get("sources", []), *sent_d,
    )
    if fast:
        sent_out1, sent_mta, sent_in1, sent_mid2, sent_in2 = sent_f
        sent_mta = sent_mta[:, :edge]
        sent_proj = sent_joined[:join].astype(F32)
        sent_out2 = sent_joined[join:].astype(F32)
    else:
        grad_w_mta = jnp.transpose(grad_w_mta, (1, 0, 2)).reshape(GW, 27 * GW)
        grad_w_proj = grad_joined[:, :join].reshape(C, C)
        grad_w_out2 = grad_joined[:, join:].reshape(M, C)
        sent_in1, sent_mta, sent_out1, sent_in2, sent_mid2, sent_out2, sent_proj = [
            deliver(g)
            for g in (
                grad_w_in1, grad_w_mta, grad_w_out1, grad_w_in2, grad_w_mid2, grad_w_out2,
                grad_w_proj,
            )
        ]
    counts = jnp.stack([total * PIX] * 3 + [total * QUARTER] * 2) * C
    rms = jnp.sqrt(squares[0, :5] / counts)

    def pair(totals):
        return jnp.stack([totals[1], totals[0]])

    grad_mid_norms = jnp.stack(
        [pair(value) for value in (totals_one, totals_two, totals_alpha, totals_beta)]
    )
    grad_wide_norms = jnp.stack(
        [
            pair(totals_three),
            jnp.stack([totals_last[1], totals_last[0]]),
            jnp.stack([totals_last[2], totals_last[0]]),
        ]
    )
    return (
        result.reshape(grad_out.shape),
        grad_frames.reshape(video.shape),
        grad_mid_norms,
        grad_wide_norms,
        sum_taps.reshape(3, 3, GW),
        sum_reduce.T,
        sum_conv.reshape(3, 3, R, GW)[..., :R],
        sum_expand,
        sum_bias.reshape(M),
        sent_in1,
        sent_mta,
        sent_out1,
        sent_in2,
        sent_mid2,
        sent_out2,
        sent_proj,
        rms,
    )


def solution(mesh):
    clip_spec = P("dp", "tm", None, None, None)
    return jax.shard_map(
        local,
        mesh=mesh,
        in_specs=(clip_spec,) + (P(),) * 8 + (P("dp", "tm"),) * 7 + (clip_spec,),
        out_specs=(clip_spec,) * 2 + (P(),) * 7 + (P("dp", "tm"),) * 7 + (P(),),
        check_vma=False,
    )
```

```python
import functools

import jax
import jax.numpy as jnp
import numpy as np
from jax import lax
from jax.experimental import pallas as pl
from jax.experimental.pallas import tpu as pltpu
from jax.sharding import PartitionSpec as P

C = 2048
M = 512
R = 32
GW = 128
HW = 16
PIX = HW * HW
QUARTER = PIX // 4
CLIPS = 3
SPAN = 2
T = CLIPS * SPAN
ROWS = T * PIX
HALF_ROWS = T * QUARTER
WIDE_TILE = 512
WIDE_STEPS = C // WIDE_TILE

EPSILON = 1e-05
HIGHEST = lax.Precision.HIGHEST
F32 = jnp.float32
BF16 = jnp.bfloat16
MESH = pl.DeviceIdType.MESH
VMEM = pltpu.VMEM
DMA = pltpu.SemaphoreType.DMA
LIMIT = 60 * 1024 * 1024

WHOLE = pl.BlockSpec(memory_space=pltpu.VMEM)
SCALARS = pl.BlockSpec(memory_space=pltpu.SMEM)
ANY = pl.BlockSpec(memory_space=pl.ANY)


def shaped(shape, dtype=F32):
    return jax.ShapeDtypeStruct(shape, dtype)


def fixed(shape):
    return pl.BlockSpec(shape, lambda i: (0,) * len(shape))


def at_first(shape):
    return pl.BlockSpec(shape, lambda i: (i,) + (0,) * (len(shape) - 1))


def at_last(shape):
    return pl.BlockSpec(shape, lambda i: (0,) * (len(shape) - 1) + (i,))


def remote_call(name, body, ident, in_specs, out_specs, out_shape, scratch, cost, *operands):
    return pl.pallas_call(
        body,
        name=name,
        in_specs=in_specs,
        out_specs=out_specs,
        out_shape=out_shape,
        scratch_shapes=scratch,
        cost_estimate=pl.CostEstimate(flops=1024, bytes_accessed=1024, transcendentals=0),
        compiler_params=pltpu.CompilerParams(
            vmem_limit_bytes=LIMIT, collective_id=ident, has_side_effects=True
        ),
    )(*operands)


def sigmoid(z):
    return 0.5 * jnp.tanh(0.5 * z) + 0.5


def nn(left, right):
    return jnp.dot(left, right, preferred_element_type=F32)


def nt(left, right):
    return lax.dot_general(left, right, (((1,), (1,)), ((), ())), preferred_element_type=F32)


def tn(left, right):
    return lax.dot_general(left, right, (((0,), (0,)), ((), ())), preferred_element_type=F32)


def nn_exact(left, right):
    return jnp.dot(left, right, precision=HIGHEST, preferred_element_type=F32)


def nt_exact(left, right):
    return lax.dot_general(
        left, right, (((1,), (1,)), ((), ())), precision=HIGHEST, preferred_element_type=F32
    )


def tn_exact(left, right):
    return lax.dot_general(
        left, right, (((0,), (0,)), ((), ())), precision=HIGHEST, preferred_element_type=F32
    )


def down(values):
    return jnp.sum(values, axis=0, keepdims=True)


def merge(stats, values, tab, i):
    rows = values.shape[0]
    mean = down(values) * (1.0 / rows)
    spread = down(jnp.square(values - mean))
    delta = mean - stats[0:1]
    stats[0:1] += delta * tab[1, i]
    stats[1:2] += spread * tab[0, i] + jnp.square(delta) * (tab[2, i] * rows)


def whole_stats(parts, masks, inv_count):
    mean = sum(down(part) * mask for part, mask in zip(parts, masks)) * inv_count
    spread = sum(down(jnp.square(part - mean)) * mask for part, mask in zip(parts, masks))
    return (mean, spread)


def unit(values, stats):
    return (values - stats[0:1]) * stats[1:2]


def norm_back(grads, centred, stats, pair, totals, mask, inv_count):
    total, cross = (totals[0:1] * inv_count, totals[1:2] * inv_count)
    return (pair[0:1] * stats[1:2]) * (grads - mask * (total + centred * cross))


def peers_of(ndp, ntm):
    d, t = (lax.axis_index("dp"), lax.axis_index("tm"))
    along = [(lax.rem(d + k, ndp), t) for k in range(1, ndp)]
    return along, [(d, lax.rem(t + k, ntm)) for k in range(1, ntm)]


def greet(ndp, ntm):
    along, across = peers_of(ndp, ntm)
    for peer in along + across:
        pl.semaphore_signal(
            pltpu.get_barrier_semaphore(), inc=1, device_id=peer, device_id_type=MESH
        )


def met(ndp, ntm):
    pl.semaphore_wait(pltpu.get_barrier_semaphore(), ndp + ntm - 2)


def sent(source, target, out_sem, in_sem, peer):
    return pltpu.make_async_remote_copy(source, target, out_sem, in_sem, peer, MESH)


def start_all(copies):
    for copy in copies:
        copy.start()


def wait_all(copies):
    for copy in copies:
        copy.wait()


def plain_gather(parts, row, tab):
    return sum(parts[1:], parts[0])


def plain_last(value, tab):
    return value


def spread_gather(scale, parts, row, tab):
    outputs = []
    for k in range(0, parts[0].shape[0], 2):
        means = [part[k : k + 1] for part in parts]
        mean = sum(value * tab[row, s] for s, value in enumerate(means))
        spread = sum(
            part[k + 1 : k + 2] + jnp.square(value - mean) * (tab[row + 1, s] * scale)
            for s, (part, value) in enumerate(zip(parts, means))
        )
        outputs.extend([mean, spread])
    return jnp.concatenate(outputs, axis=0)


def spread_last(scale, value, tab):
    outputs = []
    for k in range(0, value.shape[0], 2):
        outputs.append(value[k : k + 1])
        outputs.append(lax.rsqrt(value[k + 1 : k + 2] * (tab[4, 0] * (1.0 / scale)) + EPSILON))
    return jnp.concatenate(outputs, axis=0)


def swap_scratch(ndp, ntm, shape):
    return [
        VMEM(shape, F32), VMEM((ndp,) + shape, F32), VMEM((ntm,) + shape, F32),
        DMA((4, max(ndp, ntm))),
    ]


def swap_steps(ndp, ntm, scale, tab, out, source, first, second, sems):
    d, t = (lax.axis_index("dp"), lax.axis_index("tm"))
    along, across = peers_of(ndp, ntm)
    if scale is None:
        gather, last = (plain_gather, plain_last)
    else:
        gather = functools.partial(spread_gather, scale)
        last = functools.partial(spread_last, scale)

    def copies(buffer, peers, k):
        return [
            sent(buffer.at[0], buffer.at[j], sems.at[2 * k, j], sems.at[2 * k + 1, j], peer)
            for j, peer in enumerate(peers, 1)
        ]

    one, two = (copies(first, along, 0), copies(second, across, 1))

    def begin():
        first[0] = source[...]
        start_all(one)

    def middle():
        wait_all(one)
        second[0] = gather([first[lax.rem(d - s + ndp, ndp)] for s in range(ndp)], 0, tab)
        start_all(two)

    def end():
        wait_all(two)
        out[...] = last(
            gather([second[lax.rem(t - s + ntm, ntm)] for s in range(ntm)], 2, tab), tab
        )

    return (begin, middle, end)


def all_sums_scratch(ndp, ntm, rows):
    return [
        VMEM((ndp, rows // ndp, GW), F32), VMEM((ntm, rows // ndp // ntm, GW), F32),
        DMA((8, max(ndp, ntm))),
    ]


def all_sums_steps(ndp, ntm, source, out, first, second, sems):
    d, t = (lax.axis_index("dp"), lax.axis_index("tm"))
    large = source.shape[0] // ndp
    small = large // ntm
    along, across = peers_of(ndp, ntm)

    def rows(group, size):
        return pl.ds(pl.multiple_of(group * size, size), size)

    def copies(pieces, peers, k):
        return [
            sent(left, right, sems.at[2 * k, j], sems.at[2 * k + 1, j], peer)
            for j, ((left, right), peer) in enumerate(zip(pieces, peers), 1)
        ]

    own = out.at[pl.ds(pl.multiple_of(d * large + t * small, small), small)]
    block = out.at[rows(d, large)]
    one = copies(
        [(source.at[rows(peer[0], large)], first.at[k]) for k, peer in enumerate(along, 1)],
        along, 0,
    )
    two = copies(
        [(first.at[0, rows(peer[1], small)], second.at[k]) for k, peer in enumerate(across, 1)],
        across, 1,
    )
    three = copies([(own, own)] * (ntm - 1), across, 2)
    four = copies([(block, block)] * (ndp - 1), along, 3)

    def begin():
        start_all(one)

    def second_step():
        wait_all(one)
        first[0] = source[rows(d, large)]
        total = first[lax.rem(d, ndp)]
        for s in range(1, ndp):
            total = total + first[lax.rem(d - s + ndp, ndp)]
        first[0] = total
        start_all(two)

    def third_step():
        wait_all(two)
        second[0] = first[0, rows(t, small)]
        total = second[lax.rem(t, ntm)]
        for s in range(1, ntm):
            total = total + second[lax.rem(t - s + ntm, ntm)]
        own[...] = total
        start_all(three)

    def fourth_step():
        wait_all(three)
        start_all(four)

    def end():
        wait_all(four)

    return [begin, second_step, third_step, fourth_step, end]


def cube(ndp, ntm):
    d, t = (lax.axis_index("dp"), lax.axis_index("tm"))
    core, x, y = (lax.rem(d, 2), lax.rem(d // 2, 2), d // 4)
    peers = ((d + 1 - 2 * core, t), (d + 2 - 4 * x, t), (d + 4 - 8 * y, t))
    return (t, core, x, y, peers)


def lanes(group, width):
    return pl.ds(pl.multiple_of(group * width, GW), width)


def over_z(ntm, low, target, sems):
    d, t = (lax.axis_index("dp"), lax.axis_index("tm"))
    slot = target.at[:, lanes(t, low.shape[1])]
    copies = [pltpu.make_async_copy(low, slot, sems.at[2, 0])]
    for k in range(1, ntm):
        copies.append(sent(low, slot, sems.at[0, k], sems.at[1, k], (d, lax.rem(t + k, ntm))))
    return copies


def gather_steps(ndp, ntm, low, full, rows, z_sems, sems):
    t, core, x, y, (to_core, to_x, to_y) = cube(ndp, ntm)
    own = full.at[2 * y + x, core]
    zs, one, two, three = ([], [], [], [])
    for k, (start, size) in enumerate(rows):
        part = pl.ds(start, size)
        if low.shape[1] == full.shape[3]:
            zs.append([pltpu.make_async_copy(low.at[part], own.at[part], z_sems.at[k, 0, 0])])
        else:
            zs.append(over_z(ntm, low.at[part], own.at[part], z_sems.at[k]))
        first, second = (to_x, to_y) if k % 2 == 0 else (to_y, to_x)
        other = (y, 1 - x) if k % 2 == 0 else (1 - y, x)
        block = full.at[2 * y + x, core, part]
        one.append([sent(block, block, sems.at[0, k, 0], sems.at[0, k, 1], first)])
        pair = []
        for j, (row, col) in enumerate(((y, x), other), 1):
            block = full.at[2 * row + col, core, part]
            pair.append(sent(block, block, sems.at[j, k, 0], sems.at[j, k, 1], second))
        two.append(pair)
        block = full.at[:, core, part]
        three.append([sent(block, block, sems.at[3, k, 0], sems.at[3, k, 1], to_core)])
    count = len(rows)

    def after(waits, starts):
        wait_all(waits)
        start_all(starts)

    return [
        [functools.partial(start_all, zs[k]) for k in range(count)],
        [functools.partial(after, zs[k], one[k]) for k in range(count)],
        [functools.partial(after, one[k], two[k]) for k in range(count)],
        [functools.partial(after, two[k], three[k]) for k in range(count)],
        [functools.partial(after, three[k], []) for k in range(count)],
    ]


def each(start, stop, body):
    def step(k, carry):
        body(k)
        return carry

    lax.fori_loop(start, stop, step, 0)


def rows_at(group, size):
    return pl.ds(pl.multiple_of(group * size, size), size)


def run_steps(steps):
    for step in steps:
        step()


def lane_row(values):
    lane = lax.broadcasted_iota(jnp.int32, (1, GW), 1)
    row = jnp.zeros((1, GW), F32)
    for k, value in enumerate(values):
        row = jnp.where(lane == k, value, row)
    return row


def fill_tables(ndp, ntm, lengths, tab, swap, later):
    d, t = (lax.axis_index("dp"), lax.axis_index("tm"))
    held = [lengths[k] for k in range(ndp * CLIPS)]
    counts = [
        [
            sum(jnp.clip(held[i * CLIPS + c] - j * SPAN, 0, SPAN) for c in range(CLIPS))
            for i in range(ndp)
        ]
        for j in range(ntm)
    ]
    sums = [sum(column) for column in counts]
    total = sum(sums).astype(F32)
    column = [
        sum(jnp.where(t == j, counts[j][i], 0) for j in range(ntm)).astype(F32) for i in range(ndp)
    ]
    mask, after = ([], [])
    for c in range(CLIPS):
        own = lengths[d * CLIPS + c]
        for k in range(SPAN):
            mask.append(jnp.where(t * SPAN + k < own, 1.0, 0.0))
            after.append(jnp.where(t * SPAN + k + 1 < own, 1.0, 0.0))
    before = [sum(mask[:k], jnp.float32(0.0)) for k in range(T)]
    mask_row, before_row = (lane_row(mask), lane_row(before))
    share = 1.0 / jnp.maximum(before_row + mask_row, 1.0)
    tab[...] = jnp.zeros_like(tab)
    tab[0:1] = mask_row
    tab[1:2] = mask_row * share
    tab[2:3] = before_row * mask_row * share
    local = jnp.maximum(sum(mask), 1.0)
    ones = jnp.full((1, GW), 1.0, F32)
    rates = lane_row([1.0 / PIX, 1.0 / QUARTER, 1.0 / PIX, 1.0 / QUARTER, 1.0, 1.0])
    bases = lane_row([local, local, total, total, 1.0, 1.0])
    tab[3:4] = rates / jnp.maximum(bases, ones)
    swap[...] = jnp.zeros_like(swap)
    here = jnp.maximum(sum(column), 1.0)
    swap[0:1] = lane_row(column) / (here * ones)
    swap[1:2] = lane_row(column)
    swap[2:3] = lane_row([value.astype(F32) for value in sums]) / (total * ones)
    swap[3:4] = lane_row([value.astype(F32) for value in sums])
    swap[4:5] = ones / (total * ones)
    swap[5:6] = total * ones
    row = lax.broadcasted_iota(jnp.int32, (8, GW), 0)
    values = jnp.zeros((8, GW), F32)
    for k, value in enumerate(after):
        values = jnp.where(row == k, value, values)
    later[...] = values


def first_gather(
    ndp, ntm, lengths, in_shard, mta_shard, out_shard, mid_shard, proj_shard, last_shard, reduce,
    conv, expand, full_in, full_mta, out_rows, mid_rows, pair, tab, swap, later, reduce_low,
    conv_low, expand_wide,
    low_in, low_mta, low_out, low_mid, z_sems, sems,
):
    greet(ndp, ntm)
    low_in[...] = in_shard[...].astype(BF16)
    low_mta[...] = jnp.zeros_like(low_mta)
    low_mta[:, : mta_shard.shape[1]] = mta_shard[...].astype(BF16)
    low_out[...] = out_shard[...].astype(BF16)
    low_mid[...] = mid_shard[...].astype(BF16)
    chunks = [(k * 128, 128) for k in range(2)]
    one = gather_steps(ndp, ntm, low_in, full_in, chunks, z_sems.at[0], sems.at[0])
    two = gather_steps(ndp, ntm, low_mta, full_mta, ((0, 16),), z_sems.at[1], sems.at[1])
    copies = over_z(ntm, low_out, out_rows, z_sems.at[2, 0])
    copies += over_z(ntm, low_mid, mid_rows, z_sems.at[3, 0])
    met(ndp, ntm)
    run_steps(one[0])
    run_steps(two[0])
    start_all(copies)
    fill_tables(ndp, ntm, lengths, tab, swap, later)
    reduce_low[...] = jnp.zeros_like(reduce_low)
    reduce_low[:, 0:R] = reduce[...].T.astype(BF16)
    conv_low[...] = jnp.zeros_like(conv_low)
    conv_low[:, 0:R, 0:R] = conv[...].astype(BF16).astype(F32)
    expand_wide[...] = jnp.zeros_like(expand_wide)
    expand_wide[0:R] = expand[...]
    pair[0 : C // 8] = proj_shard[...].astype(BF16)
    pair[C // 8 :] = last_shard[...].astype(BF16)
    for k in range(1, 5):
        run_steps(one[k])
        run_steps(two[k])
    wait_all(copies)


def scatter_chunks(items):
    chunks = []
    for item, (base, rows, cols, parts) in enumerate(items):
        size = rows // parts
        for part in range(parts):
            chunks.append((item, base + part * size, part * size, size, cols))
    return chunks


def scatter_scratch(items, ntm):
    chunks = scatter_chunks(items)
    scratch = []
    for _, _, _, rows, cols in chunks:
        scratch += [
            VMEM((2, 2, rows, cols), BF16), VMEM((2, 2, rows, cols), BF16),
            VMEM((2, rows, cols), BF16), VMEM((rows, cols), BF16),
            VMEM((ntm, rows, cols // ntm), BF16),
        ]
    return scratch + [DMA((len(chunks), 7)), DMA((len(chunks), 2, ntm))]


def scatter_steps(ndp, ntm, items, sources, outs, scratch, partial=False):
    t, core, x, y, (to_core, to_x, to_y) = cube(ndp, ntm)
    _, across = peers_of(ndp, ntm)
    chunks = scatter_chunks(items)
    sems, z_sems = scratch[-2:]
    steps = [[], [], [], [], []]
    for i, (item, start, place, size, cols) in enumerate(chunks):
        own, first, second, third, fourth = scratch[5 * i : 5 * i + 5]
        by_x = i % 2 == 0
        part = pl.ds(start, size)
        width = cols // ntm
        source = sources[item]
        one = [
            pltpu.make_async_copy(source.at[:, :, core, part], own, sems.at[i, 0]),
            sent(source.at[:, :, 1 - core, part], first, sems.at[i, 1], sems.at[i, 2], to_core),
        ]
        if by_x:
            two = [sent(own.at[:, 1 - x], second, sems.at[i, 3], sems.at[i, 4], to_x)]
            three = [sent(second.at[1 - y], third, sems.at[i, 5], sems.at[i, 6], to_y)]
        else:
            two = [sent(own.at[1 - y], second, sems.at[i, 3], sems.at[i, 4], to_y)]
            three = [sent(second.at[1 - x], third, sems.at[i, 5], sems.at[i, 6], to_x)]
        four = [
            sent(
                third.at[:, lanes(peer[1], width)], fourth.at[k], z_sems.at[i, 0, k],
                z_sems.at[i, 1, k], peer,
            )
            for k, peer in enumerate(across, 1)
        ]
        four.append(
            pltpu.make_async_copy(third.at[:, lanes(t, width)], fourth.at[0], z_sems.at[i, 0, 0])
        )

        def add_core(one=one, two=two, own=own, first=first):
            wait_all(one)

            def add(k):
                own[k // 2, lax.rem(k, 2)] += first[k // 2, lax.rem(k, 2)]

            each(0, 4, add)
            start_all(two)

        def add_first(two=two, three=three, own=own, second=second, by_x=by_x):
            wait_all(two)

            def add(k):
                second[k] += own[k, x] if by_x else own[y, k]

            each(0, 2, add)
            start_all(three)

        def add_second(
            three=three, four=four, second=second, third=third, by_x=by_x, out=outs[item],
            place=place, size=size,
        ):
            wait_all(three)
            if partial:
                target, base, rows = out
                value = third[...] + second[y if by_x else x]
                tiles = value.shape[1] // ntm // GW
                for k in range(ntm):
                    for j in range(tiles):
                        at, lane = (base + j * rows + place, (k * tiles + j) * GW)
                        target[k, at : at + size] = value[:, lane : lane + GW]
                return
            third[...] += second[y if by_x else x]
            start_all(four)

        def add_last(four=four, fourth=fourth, out=outs[item], place=place, size=size):
            wait_all(four)
            total = fourth[0].astype(F32)
            for k in range(1, ntm):
                total = total + fourth[k].astype(F32)
            out[place : place + size] = total

        steps[0].append(functools.partial(start_all, one))
        adds = (add_core, add_first, add_second) + (() if partial else (add_last,))
        for k, step in enumerate(adds):
            steps[k + 1].append(step)
    return steps


def cubed(grad):
    return grad.reshape((2, 2, 2, grad.shape[0] // 8, grad.shape[1]))


LOCAL = "local"


def staged_kernel(ndp, ntm, steps, body, counts, marks, scale, items, at, *refs):
    n_in, n_source, n_carry, n_out, n_scratch, swaps = counts

    def take(count):
        nonlocal refs
        taken, refs = (refs[:count], refs[count:])
        return taken

    swap_tab = take(swaps)
    ins, sources, shards = (take(n_in), take(n_source), take(n_carry))
    outs = list(take(n_out))
    totals = take(swaps)
    scattered, gathered = (take(len(items)), take(n_carry))
    scratch = take(n_scratch)
    swap_refs = take(4 * swaps)
    lows, carry_sems = (take(n_carry), take(1 if n_carry else 0))
    scatter_refs = refs
    i = pl.program_id(0)
    last = steps - 1
    copies = []
    for k, (low, target) in enumerate(zip(lows, gathered)):
        copies += over_z(ntm, low, target, carry_sems[0].at[k])
    if marks is not None:
        outs.insert(marks, swap_refs[0])

    @pl.when(i == 0)
    def _():
        greet(ndp, ntm)

    tail = body(*ins, *outs, *scratch) or []
    groups = [[], [], [], [], []]
    if items:
        groups = scatter_steps(ndp, ntm, items, sources, scattered, scatter_refs)
    swap = [lambda: None] * 3
    if swaps:
        swap = swap_steps(ndp, ntm, scale, swap_tab[0], totals[0], *swap_refs)

    @pl.when(i == 0)
    def _():
        for shard, low in zip(shards, lows):
            low[...] = shard[...].astype(BF16)
        met(ndp, ntm)
        start_all(copies)
        run_steps(groups[0])

    for k in range(1, 4):
        if items and isinstance(at[k], int) and at[k] < last:

            @pl.when(i == at[k])
            def _(k=k):
                run_steps(groups[k])

    @pl.when(i == last)
    def _():
        for k in range(1, 4):
            if items and at[k] == last:
                run_steps(groups[k])
        for k, name in enumerate("abc"):
            swap[k]()
            if k < len(tail):
                tail[k]()
            for j in range(1, 5):
                if items and at[j] == name:
                    run_steps(groups[j])
        wait_all(copies)


def plain_kernel(steps, body, *refs):
    tail = body(*refs) or []

    @pl.when(pl.program_id(0) == steps - 1)
    def _():
        run_steps(tail)


def staged(
    name, ident, *, ndp, ntm, steps, body, ins, outs, scratch, cost, swap=None, items=(),
    sources=(), at=(0, 1, 2, 3, "c"), carry=(),
):
    arrays, specs = ([], [])
    if swap is not None:
        arrays.append(swap[0])
        specs.append(SCALARS)
    arrays += [array for array, _ in ins] + list(sources) + list(carry)
    specs += [spec for _, spec in ins] + [ANY] * len(sources)
    specs += [fixed(shard.shape) for shard in carry]
    marks = outs.index(LOCAL) if LOCAL in outs else None
    real = [out for out in outs if out is not LOCAL]
    out_shapes, out_specs = ([shape for shape, _ in real], [spec for _, spec in real])
    extra = []
    swaps, scale = (0, None)
    if swap is not None:
        swaps, scale = (1, swap[1])
        out_shapes.append(shaped(swap[2]))
        out_specs.append(fixed(swap[2]))
        extra += swap_scratch(ndp, ntm, swap[2])
    for _, rows, cols, _ in items:
        out_shapes.append(shaped((rows, cols // ntm)))
        out_specs.append(fixed((rows, cols // ntm)))
    for shard in carry:
        out_shapes.append(shaped((shard.shape[0], shard.shape[1] * ntm), BF16))
        out_specs.append(ANY)
        extra.append(VMEM(shard.shape, BF16))
    if carry:
        extra.append(DMA((len(carry), 3, ntm)))
    if items:
        extra += scatter_scratch(items, ntm)
    if not (swaps or items or carry):
        return pl.pallas_call(
            functools.partial(plain_kernel, steps, body),
            name=name,
            grid=(steps,),
            in_specs=specs,
            out_specs=out_specs,
            out_shape=out_shapes,
            scratch_shapes=list(scratch),
            cost_estimate=pl.CostEstimate(flops=1024, bytes_accessed=1024, transcendentals=0),
            compiler_params=pltpu.CompilerParams(vmem_limit_bytes=LIMIT),
        )(*arrays)
    counts = (len(ins), len(sources), len(carry), len(real), len(scratch), swaps)
    return pl.pallas_call(
        functools.partial(
            staged_kernel, ndp, ntm, steps, body, counts, marks, scale, tuple(items), at
        ),
        name=name,
        grid=(steps,),
        in_specs=specs,
        out_specs=out_specs,
        out_shape=out_shapes,
        scratch_shapes=list(scratch) + extra,
        cost_estimate=pl.CostEstimate(flops=1024, bytes_accessed=1024, transcendentals=0),
        compiler_params=pltpu.CompilerParams(
            vmem_limit_bytes=LIMIT, collective_id=ident, has_side_effects=True
        ),
    )(*arrays)


def in_one(tab, video, weight, pre, squares, stats):
    i = pl.program_id(0)

    @pl.when(i == 0)
    def _():
        stats[...] = jnp.zeros_like(stats)
        squares[...] = jnp.zeros_like(squares)

    source = video[0]
    value = nn(source, weight[...]) * tab[0, i]
    pre[0] = value
    merge(stats, value, tab, i)
    squares[...] += down(jnp.square(source.astype(F32))) * tab[0, i]


def column(shape):
    return lax.rem(lax.broadcasted_iota(jnp.int32, shape, 0), HW)


def spread_taps(store, low):
    value = low.astype(F32)
    place = column(value.shape)
    zeros = jnp.zeros((HW, 3 * GW), BF16)
    store[0:HW] = zeros
    store[HW + PIX : PIX + 2 * HW] = zeros
    before = jnp.where(place == 0, 0.0, pltpu.roll(value, 1, 0))
    after = jnp.where(place == HW - 1, 0.0, pltpu.roll(value, PIX - 1, 0))
    store[HW : HW + PIX, 0:GW] = before.astype(BF16)
    store[HW : HW + PIX, GW : 2 * GW] = low
    store[HW : HW + PIX, 2 * GW : 3 * GW] = after.astype(BF16)


def window(store, row):
    return store[row * HW : row * HW + PIX]


def neighbours(ntm):
    d, t = (lax.axis_index("dp"), lax.axis_index("tm"))
    return (t > 0, t < ntm - 1, (d, jnp.maximum(t - 1, 0)), (d, jnp.minimum(t + 1, ntm - 1)))


def rows_of(pieces):
    place = lax.broadcasted_iota(jnp.int32, (8, pieces[0].shape[1]), 0)
    result = jnp.zeros(place.shape, F32)
    for i, piece in enumerate(pieces):
        result = jnp.where(place == i, piece, result)
    return result


def chosen(rows, cols, shift, limit, skip):
    row = lax.broadcasted_iota(jnp.int32, (rows, cols), 0)
    source = lax.broadcasted_iota(jnp.int32, (rows, cols), 1) + shift
    source = jnp.where(source < limit, source, source + skip)
    return jnp.where(row == source, 1.0, 0.0).astype(BF16)


def tile_from_edges(weight, tile, edge, edge_wide):
    start = tile * GW
    block = start // edge
    offset = start - block * edge
    base = offset // GW * GW
    window_lanes = pl.ds(pl.multiple_of(block * edge_wide + base, GW), 2 * GW)
    pick = chosen(2 * GW, GW, offset - base, edge - base, edge_wide - edge)
    return nn(weight[:, window_lanes], pick).astype(BF16)


def edge_from_tiles(tiles, place, edge, edge_wide):
    block = place // (edge_wide // GW)
    start = block * edge + (place - block * (edge_wide // GW)) * GW
    tile = start // GW
    shift = start - tile * GW
    left = nn(tiles[tile], chosen(GW, GW, shift, 2 * GW, 0))
    right = nn(tiles[jnp.minimum(tile + 1, 26)], chosen(GW, GW, shift - GW, 2 * GW, 0))
    return (left + right).astype(BF16)


def mta_forward(
    ndp, ntm, fast, edge, swap_tab, tab, pre, stats, pair, reduce_low, conv_low, expand, bias,
    weight, taps, windows, later, *refs,
):
    carried = 2 if fast else 0
    shards, refs = (refs[:carried], refs[carried:])
    agg, stats_out, ext_out, blended, sigma, snext, pooled, kernels = refs[:8]
    gathered, refs = (refs[8 : 8 + carried], refs[8 + carried :])
    hidden, store, ext, kept, gates, s_own, s_send, s_recv, ssems, rsems = refs[:10]
    swap_refs, refs = (refs[10:14], refs[14:])
    stats_two = swap_refs[0]
    has_prev, has_next, prev, following = neighbours(ntm)
    greet(ndp, ntm)
    dp_steps = [[], [], [], [], []]
    if fast:
        z_sems, dp_sems = refs
        for k, size in enumerate((32, 128)):
            part = gather_steps(
                ndp, ntm, shards[k], gathered[k], ((0, size), (size, size)), z_sems.at[k],
                dp_sems.at[k],
            )
            dp_steps = [steps + more for steps, more in zip(dp_steps, part)]
    swap = swap_steps(ndp, ntm, PIX, swap_tab, stats_out, *swap_refs)

    def assemble(tile):
        if fast:
            value = tile_from_edges(weight, tile, edge, weight.shape[1] // ntm)
        else:
            value = weight[tile]
        row = lax.rem(tile, 9) // 3
        kernels[tile // 9, row, rows_at(lax.rem(tile, 3), GW)] = value

    each(0, 27, assemble)
    met(ndp, ntm)
    run_steps(dp_steps[0])

    def first(f, carry):
        z = unit(pre[f], stats) * pair[0:1] + pair[1:2]
        value = z * sigmoid(z)
        hidden[f] = value
        motion = nn(value.astype(BF16), reduce_low[...]).astype(BF16)
        s_own[f] = nn(windows[...], motion)
        return carry

    lax.fori_loop(0, T, first, 0)
    for clip in range(CLIPS):
        s_send[clip] = s_own[clip * SPAN]
    back = sent(s_send, s_recv, ssems.at[9, 0], rsems.at[9, 0], prev)

    @pl.when(has_prev)
    def _():
        back.start()

    run_steps(dp_steps[1])

    @pl.when(has_prev)
    def _():
        back.wait_send()

    @pl.when(has_next)
    def _():
        back.wait_recv()

    @pl.when(jnp.logical_not(has_next))
    def _():
        s_recv[...] = jnp.zeros_like(s_recv)

    for clip in range(CLIPS):
        snext[clip * SPAN] = s_own[clip * SPAN + 1]
        snext[clip * SPAN + 1] = s_recv[clip]
    total = -rows_of([s_own[f, 4:5] for f in range(T)])
    for tap in range(9):
        rows = rows_of([snext[f, tap : tap + 1] for f in range(T)])
        total = total + nn_exact(rows, conv_low[tap])
    mean = total * (later[...] * (1.0 / PIX))
    pooled[...] = mean
    level = sigmoid(nn_exact(mean, expand[...]) + bias[...])
    sigma[...] = level
    for f in range(T):
        gates[f] = 1.0 + level[f : f + 1]

    @pl.when(jnp.logical_not(has_prev))
    def _():
        for group in range(3):
            ext[group, :, 0] = jnp.zeros((CLIPS, PIX, GW), BF16)

    @pl.when(jnp.logical_not(has_next))
    def _():
        for group in range(3):
            ext[group, :, 3] = jnp.zeros((CLIPS, PIX, GW), BF16)

    def edges(group, clip):
        k = group * CLIPS + clip
        left = sent(ext.at[group, clip, 1], ext.at[group, clip, 3], ssems.at[k, 0], rsems.at[k, 0], prev)
        right = sent(
            ext.at[group, clip, 2], ext.at[group, clip, 0], ssems.at[k, 1], rsems.at[k, 1],
            following,
        )
        return left, right

    def offer(group, clip, first):
        here = lanes(group + 1, GW)

        def piece(step):
            f = clip * SPAN + step
            value = hidden[f, :, here] * gates[f, :, here]
            if not first:
                value = value + agg[f, :, lanes(group, GW)]
            value = value * tab[0, f]
            kept[lax.rem(group, 2), clip, step] = value
            ext[group, clip, step + 1] = value.astype(BF16)

        each(0, SPAN, piece)
        left, right = edges(group, clip)

        @pl.when(has_prev)
        def _():
            left.start()

        @pl.when(has_next)
        def _():
            right.start()

    def taken(group, clip):
        left, right = edges(group, clip)

        @pl.when(has_prev)
        def _():
            left.wait_send()
            right.wait_recv()

        @pl.when(has_next)
        def _():
            right.wait_send()
            left.wait_recv()

    def convolve(group, clip):
        row = [taps[group * 3 + k] for k in range(3)]

        def mix(step):
            f = clip * SPAN + step
            own = [kept[lax.rem(group, 2), clip, k] for k in range(SPAN)]
            line = [ext[group, clip, 0].astype(F32)] + own + [ext[group, clip, 3].astype(F32)]
            here = [jnp.where(step == 0, line[k], line[k + 1]) for k in range(3)]
            mixed = row[0] * here[0] + row[1] * here[1] + row[2] * here[2]
            value = mixed.astype(BF16)
            blended[group, f] = value
            spread_taps(store.at[step], value)
            result = nn(window(store.at[step], 0), kernels[group, 0])
            result += nn(window(store.at[step], 1), kernels[group, 1])
            result += nn(window(store.at[step], 2), kernels[group, 2])
            agg[f, :, lanes(group + 1, GW)] = result

        each(0, SPAN, mix)

    each(0, CLIPS, lambda clip: offer(0, clip, True))

    def base(f):
        agg[f, :, 0:GW] = hidden[f, :, 0:GW] * gates[f, :, 0:GW]

    each(0, T, base)

    def turn(n):
        group, clip = (n // CLIPS, lax.rem(n, CLIPS))
        taken(group, clip)
        convolve(group, clip)

        @pl.when(group < 2)
        def _():
            offer(group + 1, clip, False)

        for k in range(3):

            @pl.when(n == 3 * k + 2)
            def _(k=k):
                run_steps(dp_steps[2 + k])

    each(0, 3 * CLIPS, turn)
    ext_out[...] = ext[...]
    stats_two[...] = jnp.zeros_like(stats_two)
    each(0, T, lambda f: merge(stats_two, agg[f], tab, f))
    run_steps(swap)


def out_one(tab, agg, stats, pair, order, weight, hidden, pre, sums):
    i = pl.program_id(0)

    @pl.when(i == 0)
    def _():
        sums[...] = jnp.zeros_like(sums)

    z = unit(agg[0], stats) * pair[0:1] + pair[1:2]
    value = nn(order[...], (z * sigmoid(z)).astype(BF16)).astype(BF16)
    hidden[0] = value
    result = nn(value, weight[...])
    pre[0] = result
    merge(sums, result, tab, i)


def in_two(
    tab, video, pre, stats, pair, order, weight, out_low, centred, slope, first, squares, sums
):
    i = pl.program_id(0)

    @pl.when(i == 0)
    def _():
        sums[...] = jnp.zeros_like(sums)
        squares[...] = jnp.zeros_like(squares)

    mask = tab[0, i]
    source = nn(order[...], video[0]) * mask
    scaled = unit(pre[0], stats)
    branch = scaled * pair[0:1] + pair[1:2]
    before = source + branch
    gate = sigmoid(before)
    value = before * gate
    low = value.astype(BF16)
    out_low[0] = low
    centred[0] = scaled.astype(BF16)
    slope[0] = (gate + value * (1.0 - gate)).astype(BF16)
    squares[0:1] += down(jnp.square(branch)) * mask
    squares[1:2] += down(jnp.square(value)) * mask
    result = nn(low, weight[...])
    first[0] = result
    merge(sums, result, tab, i)


def shifted(piece, tap, backward=False):
    rows, cols = (tap // 3 == 0, tap % 3 == 0)
    side = HW // 2
    place = lax.broadcasted_iota(jnp.int32, piece.shape, 0)
    if rows:
        if backward:
            piece = jnp.where(place < QUARTER - side, pltpu.roll(piece, QUARTER - side, 0), 0.0)
        else:
            piece = jnp.where(place >= side, pltpu.roll(piece, side, 0), 0.0)
    if cols:
        col = lax.rem(place, side)
        if backward:
            piece = jnp.where(col < side - 1, pltpu.roll(piece, QUARTER - 1, 0), 0.0)
        else:
            piece = jnp.where(col > 0, pltpu.roll(piece, 1, 0), 0.0)
    return piece


def plane(tap):
    return (0 if tap // 3 == 1 else 2) + (0 if tap % 3 == 1 else 1)


def mid_two(tab, first, stats, pair, weight, taps_out, second, sums, store):
    t = pl.program_id(0)

    @pl.when(t == 0)
    def _():
        def frame(f, carry):
            z = unit(first[f], stats) * pair[0:1] + pair[1:2]
            value = z * sigmoid(z)
            for tap in range(9):
                at = plane(tap) * QUARTER
                piece = shifted(value[at : at + QUARTER], tap)
                store[tap, pl.ds(pl.multiple_of(f * QUARTER, QUARTER), QUARTER)] = piece.astype(BF16)
            return carry

        lax.fori_loop(0, T, frame, 0)

    left = store[t]
    taps_out[0] = left
    part = nn(left, weight[...])

    @pl.when(t == 0)
    def _():
        second[...] = part

    @pl.when(t > 0)
    def _():
        second[...] += part

    @pl.when(t == 8)
    def _():
        parts = [second[f * QUARTER : (f + 1) * QUARTER] for f in range(T)]
        mean, spread = whole_stats(parts, [tab[0, f] for f in range(T)], tab[3, 1])
        sums[0:1] = mean
        sums[1:2] = spread


def middle(
    ndp, ntm, swap_tab, tab, second, stats_mid, pair_mid, joined, even, pairs, cotangent,
    result, grad_weight, grad_projection, grad_even, grad_mid, squares, totals_out, beta_out,
    hidden, thirds, shorts, grads, stats_all, totals_all, hidden_sum,
    mains_all, sides_all, weight_store, projection_store, held, sems, *swap_refs,
):
    s = pl.program_id(0)
    steps = WIDE_STEPS
    j = lax.rem(s, steps)
    sums = swap_refs[8]
    beta = swap_steps(ndp, ntm, None, None, beta_out, *swap_refs[8:12])

    def one(k):
        refs = [ref.at[k] for ref in swap_refs[0:4]]
        return swap_steps(ndp, ntm, QUARTER, swap_tab, stats_all.at[k], *refs)

    def two(k):
        refs = [ref.at[k] for ref in swap_refs[4:8]]
        return swap_steps(ndp, ntm, None, None, totals_all.at[k], *refs)

    def load(k):
        return pltpu.make_async_copy(joined.at[:, k], held.at[k], sems.at[2, k])

    def projection(k):
        return held[k, :, 0 : C // 8].reshape(C, WIDE_TILE)

    def weight(k):
        return held[k, :, C // 8 :].reshape(M, WIDE_TILE)

    @pl.when(s == 0)
    def _():
        greet(ndp, ntm)
        each(0, steps, lambda k: load(k).start())
        z = unit(second[...], stats_mid) * pair_mid[0:1] + pair_mid[1:2]
        hidden[...] = (z * sigmoid(z)).astype(BF16)

    @pl.when(s < steps)
    def _():
        load(j).wait()
        third = nn(hidden[...], weight(j))
        short = nn(even[...].reshape(HALF_ROWS, C), projection(j))
        thirds[j] = third
        shorts[j] = short
        stats = swap_refs[0].at[j]
        stats[...] = jnp.zeros((4, WIDE_TILE), F32)

        def gather_stats(f):
            merge(stats.at[0:2], thirds[j, rows_at(f, QUARTER)], tab, f)
            merge(stats.at[2:4], shorts[j, rows_at(f, QUARTER)], tab, f)

        each(0, T, gather_stats)

    @pl.when(s == 0)
    def _():
        met(ndp, ntm)

    @pl.when(s < steps)
    def _():
        one(j)[0]()

    @pl.when((s >= steps) & (s < 2 * steps))
    def _():
        one(j)[2]()
        stats = stats_all[j]
        sums_two = swap_refs[4].at[j]
        sums_two[...] = jnp.zeros((4, WIDE_TILE), F32)
        squares[...] = jnp.zeros_like(squares)

        def frame(f):
            rows, mask = (rows_at(f, QUARTER), tab[0, f])
            main = unit(thirds[j, rows], stats[0:2])
            side = unit(shorts[j, rows], stats[2:4])
            branch = main * pairs[0:1] + pairs[1:2]
            before = branch + (side * pairs[2:3] + pairs[3:4])
            gate = sigmoid(before)
            value = before * gate
            masked = value * mask
            result[rows] = masked.astype(BF16)
            grad = (gate + value * (1.0 - gate)) * (cotangent[rows].astype(F32) * mask)
            grads[j, rows] = grad
            for k, part in enumerate((grad, grad * main, grad * side)):
                sums_two[k : k + 1] += down(part)
            squares[0:1] += down(jnp.square(branch) * mask)
            squares[1:2] += down(jnp.square(masked))

        each(0, T, frame)
        two(j)[0]()

    @pl.when(s >= 2 * steps)
    def _():
        two(j)[2]()
        totals = totals_all[j]
        totals_out[:, lanes(j, WIDE_TILE)] = totals
        stats = stats_all[j]
        side_totals = jnp.concatenate([totals[0:1], totals[2:3]], axis=0)

        def frame(f):
            rows, mask = (rows_at(f, QUARTER), tab[0, f])
            grad = grads[j, rows]
            main = unit(thirds[j, rows], stats[0:2])
            main = norm_back(grad, main, stats[0:2], pairs[0:2], totals[0:2], mask, tab[3, 3])
            mains_all[j, rows] = main.astype(BF16)
            side = unit(shorts[j, rows], stats[2:4])
            side = norm_back(grad, side, stats[2:4], pairs[2:4], side_totals, mask, tab[3, 3])
            sides_all[j, rows] = side.astype(BF16)

        each(0, T, frame)
        hidden_part = nt(mains_all[j], weight(j))
        even_part = nt(sides_all[j], projection(j))

        @pl.when(j == 0)
        def _():
            hidden_sum[...] = hidden_part
            grad_even[...] = even_part

        @pl.when(j > 0)
        def _():
            hidden_sum[...] += hidden_part
            grad_even[...] += even_part

    @pl.when((s >= 2) & (s < steps + 2))
    def _():
        one(s - 2)[1]()

    @pl.when((s >= steps + 2) & (s < 2 * steps + 2))
    def _():
        two(s - steps - 2)[1]()

    def stores(k):
        here = lanes(k, WIDE_TILE)
        return [
            pltpu.make_async_copy(
                projection_store.at[k], grad_projection.at[:, here], sems.at[0, k]
            ),
            pltpu.make_async_copy(weight_store.at[k], grad_weight.at[:, here], sems.at[1, k]),
        ]

    def product(k):
        source = even[...].reshape(HALF_ROWS, C)
        projection_store[k] = tn(source, sides_all[k]).astype(BF16)
        weight_store[k] = tn(hidden[...], mains_all[k]).astype(BF16)
        start_all(stores(k))

    @pl.when(s == 3 * steps - 1)
    def _():
        centred = unit(second[...], stats_mid)
        z = centred * pair_mid[0:1] + pair_mid[1:2]
        gate = sigmoid(z)
        grad = hidden_sum[...] * (gate + z * gate * (1.0 - gate))
        grad_mid[...] = grad
        sums[0:1] = down(grad)
        sums[1:2] = down(grad * centred)
        beta[0]()
        each(0, steps // 2, product)
        beta[1]()
        each(steps // 2, steps, product)
        beta[2]()
        each(0, steps, lambda k: wait_all(stores(k)))


def back_mid(
    tab, grads, second, stats, pair, totals, taps_in, weight, first, stats_a, pair_a,
    grad_weight, grad_first, sums, low, store, held, sem, partial_sum,
):
    t = pl.program_id(0)
    load = pltpu.make_async_copy(taps_in, held, sem)

    @pl.when(t == 0)
    def _():
        load.start()

        def normal(f):
            rows = rows_at(f, QUARTER)
            centred = unit(second[rows], stats)
            grad = norm_back(grads[rows], centred, stats, pair, totals, tab[0, f], tab[3, 3])
            low[rows] = grad.astype(BF16)

        each(0, T, normal)
        store[...] = jnp.zeros_like(store)

    partial_sum[...] = nt(low[...], weight[...])
    for tap in range(9):

        @pl.when(t == tap)
        def _(tap=tap):
            at = plane(tap) * QUARTER

            def put(f):
                piece = shifted(partial_sum[rows_at(f, QUARTER)], tap, True)
                store[f, at : at + QUARTER] += piece

            each(0, T, put)

    @pl.when(t == 8)
    def _():
        sums[...] = jnp.zeros_like(sums)

        def frame(f, carry):
            centred = unit(first[f], stats_a)
            z = centred * pair_a[0:1] + pair_a[1:2]
            gate = sigmoid(z)
            grad = store[f] * (gate + z * gate * (1.0 - gate))
            grad_first[f] = grad
            sums[0:1] += down(grad)
            sums[1:2] += down(grad * centred)
            return carry

        lax.fori_loop(0, T, frame, 0)

    def products(steps):
        def run():
            if steps[0] == 0:
                load.wait()

            def product(tap):
                grad_weight[:, lanes(tap, M)] = tn(held[tap], low[...]).astype(BF16)

            each(steps[0], steps[-1] + 1, product)

        return run

    return [products(range(5)), products(range(5, 9))]


def back_in_two(
    tab, grads, first, stats, pair, totals, out_low, weight, even, slope, centred,
    grad_weight, grad_before, sums, lows, held, sem,
):
    i = pl.program_id(0)
    load = pltpu.make_async_copy(out_low, held, sem)
    scaled = unit(first[0], stats)
    low = norm_back(grads[0], scaled, stats, pair, totals, tab[0, i], tab[3, 2]).astype(BF16)
    grad = nt(low, weight[...])
    lows[i] = low

    @pl.when(i == 0)
    def _():
        load.start()
        sums[...] = jnp.zeros_like(sums)

    grad = jnp.concatenate([grad[0:QUARTER] + even[...], grad[QUARTER:]], axis=0)
    grad = grad * slope[0].astype(F32)
    grad_before[0] = grad.astype(BF16)
    sums[0:1] += down(grad)
    sums[1:2] += down(grad * centred[0].astype(F32))

    def products(steps):
        def run():
            if steps[0] == 0:
                load.wait()

            def product(k):
                source = held[:, :, lanes(k, WIDE_TILE)].reshape(ROWS, WIDE_TILE)
                value = tn(source, lows[...].reshape(ROWS, M))
                grad_weight[rows_at(k, WIDE_TILE)] = value.astype(BF16)

            each(steps[0], steps[-1] + 1, product)

        return run

    half = WIDE_STEPS // 2
    return [products(range(half)), products(range(half, WIDE_STEPS))]


def back_out_one(
    tab, grads, centred, stats, pair, totals, hidden, weight, order, agg, stats_two, pair_two,
    grad_weight, grad_two, sums, lows, held, sem,
):
    i = pl.program_id(0)
    load = pltpu.make_async_copy(hidden, held, sem)
    low = norm_back(
        grads[0].astype(F32), centred[0].astype(F32), stats, pair, totals, tab[0, i], tab[3, 2]
    ).astype(BF16)
    grad = nt(low, weight[...])
    lows[i] = low

    @pl.when(i == 0)
    def _():
        load.start()
        sums[...] = jnp.zeros_like(sums)

    high = grad.astype(BF16)
    rest = (grad - high.astype(F32)).astype(BF16)
    grad = tn(order[...], high) + tn(order[...], rest)
    scaled = unit(agg[0], stats_two)
    z = scaled * pair_two[0:1] + pair_two[1:2]
    gate = sigmoid(z)
    grad = grad * (gate + z * gate * (1.0 - gate))
    grad_two[0] = grad
    sums[0:1] += down(grad)
    sums[1:2] += down(grad * scaled)

    def products(steps):
        def run():
            if steps[0] == 0:
                load.wait()

            def product(k):
                here = lanes(k, WIDE_TILE)
                source = lows[:, :, here].reshape(ROWS, WIDE_TILE)
                grad_weight[:, here] = tn(held[...].reshape(ROWS, M), source).astype(BF16)

            each(steps[0], steps[-1] + 1, product)

        return run

    half = WIDE_STEPS // 2
    return [products(range(half)), products(range(half, WIDE_STEPS))]


def mta_backward(
    ndp, ntm, items, edge, tab, grads, agg, stats_two, pair_two, totals, pre, stats, pair, sigma,
    ext, blended, kernels, taps, reduce_low, conv_low, expand, windows, later, snext, pooled, *refs,
):
    count = len(items)
    sources, refs = (refs[:count], refs[count:])
    grad_one, totals_out, grad_mta, grad_reduce, grad_conv, grad_expand, grad_bias = refs[:7]
    grad_taps, refs = (refs[7], refs[8:])
    outs = []
    if count:
        base = 0
        for _, rows, cols, _ in items:
            outs.append((refs[0], base, rows))
            base += rows * (cols // ntm // GW)
        refs = refs[1:]
    mixed, low_store, store, back, parts, edge_send, edge_recv, mta_sum = refs[:8]
    k_store, k_send, k_recv, gate_sum, ssems, rsems, tiles, tap_sum, spreads, changes = refs[8:18]
    swap_refs, refs = (refs[18:22], refs[22:])
    sums = swap_refs[0]
    has_prev, has_next, prev, following = neighbours(ntm)
    greet(ndp, ntm)
    swap = swap_steps(ndp, ntm, None, None, totals_out, *swap_refs)
    steps = [[], [], [], [], []]
    if count:
        steps = scatter_steps(ndp, ntm, items, sources, outs, refs, True)

    def start(f, carry):
        centred = unit(agg[f], stats_two)
        mixed[f] = norm_back(
            grads[f], centred, stats_two, pair_two, totals, tab[0, f], tab[3, 2]
        )
        return carry

    met(ndp, ntm)
    run_steps(steps[0])
    lax.fori_loop(0, T, start, 0)
    run_steps(steps[1][0:2])

    @pl.when(jnp.logical_not(has_prev))
    def _():
        edge_recv[:, :, 0] = jnp.zeros((3, CLIPS, PIX, GW), BF16)

    @pl.when(jnp.logical_not(has_next))
    def _():
        edge_recv[:, :, 1] = jnp.zeros((3, CLIPS, PIX, GW), BF16)

    tap_sum[...] = jnp.zeros_like(tap_sum)

    def edges(group, clip):
        k = group * CLIPS + clip
        left = sent(
            edge_send.at[group, clip, 0], edge_recv.at[group, clip, 1], ssems.at[k, 0],
            rsems.at[k, 0], prev,
        )
        right = sent(
            edge_send.at[group, clip, 1], edge_recv.at[group, clip, 0], ssems.at[k, 1],
            rsems.at[k, 1], following,
        )
        return left, right

    def convolve(group, clip):
        row = [taps[group * 3 + k] for k in range(3)]
        rest = jnp.where(group < 2, 1.0, 0.0)

        def part(step):
            f = clip * SPAN + step
            value = mixed[f, :, lanes(group + 1, GW)]
            value = value + rest * mixed[f, :, lanes(jnp.minimum(group + 2, 3), GW)]
            value = value.astype(BF16)
            low_store[f] = value
            spread_taps(store.at[step], value)
            result = jnp.zeros((PIX, GW), F32)
            for tap in range(9):
                other = 8 - tap
                patch = store[
                    step,
                    (tap // 3) * HW : (tap // 3) * HW + PIX,
                    (tap % 3) * GW : (tap % 3 + 1) * GW,
                ]
                at = other % 3 * GW
                result += nt(patch, kernels[group, other // 3, at : at + GW])
            for k in range(3):
                source = ext[group, clip, step + k].astype(F32)
                tap_sum[group * 3 + k] += down(result * source)
            parts[step] = result

        each(0, SPAN, part)
        edge_send[group, clip, 0] = (row[0] * parts[0]).astype(BF16)
        edge_send[group, clip, 1] = (row[2] * parts[1]).astype(BF16)
        left, right = edges(group, clip)

        @pl.when(has_prev)
        def _():
            left.start()

        @pl.when(has_next)
        def _():
            right.start()

        back[clip, 0] = row[1] * parts[0] + row[0] * parts[1]
        back[clip, 1] = row[2] * parts[0] + row[1] * parts[1]

    def products(group, clip):
        def product(step):
            f = clip * SPAN + step
            spread_taps(store.at[step], blended[group, f])
            for k in range(3):
                mta_sum[k] += tn(window(store.at[step], k), low_store[f])

        each(0, SPAN, product)

    def collect(group, clip):
        left, right = edges(group, clip)

        @pl.when(has_prev)
        def _():
            left.wait_send()
            right.wait_recv()

        @pl.when(has_next)
        def _():
            right.wait_send()
            left.wait_recv()

        def put(step):
            f = clip * SPAN + step
            total = back[clip, step] + edge_recv[group, clip, step].astype(F32)
            mixed[f, :, lanes(group + 1, GW)] = total * tab[0, f]

        each(0, SPAN, put)

    moments = {
        0: steps[1][2:5], 1: steps[1][5:], 4: steps[2][0:2], 6: steps[2][2:5], 7: steps[2][5:],
    }

    def turn(n):
        group, clip = (2 - n // CLIPS, lax.rem(n, CLIPS))

        @pl.when(n >= CLIPS)
        def _():
            collect(group + 1, clip)

        convolve(group, clip)

        @pl.when(clip == 0)
        def _():
            mta_sum[...] = jnp.zeros_like(mta_sum)

        products(group, clip)

        @pl.when(clip == CLIPS - 1)
        def _():
            for tap in range(9):
                at = tap % 3 * GW
                tiles[group * 9 + tap] = mta_sum[tap // 3, at : at + GW].astype(BF16)

        for k, moment in moments.items():
            if moment:

                @pl.when(n == k)
                def _(moment=moment):
                    run_steps(moment)

    each(0, 3 * CLIPS, turn)
    each(0, CLIPS, lambda clip: collect(0, clip))
    for k in range(9):
        grad_taps[k : k + 1] = tap_sum[k]

    def gates(f, carry):
        z = unit(pre[f], stats) * pair[0:1] + pair[1:2]
        gate_sum[f] = down(mixed[f] * (z * sigmoid(z)))
        return carry

    lax.fori_loop(0, T, gates, 0)
    gate = sigma[...]
    excite = rows_of([gate_sum[f] for f in range(T)]) * gate * (1.0 - gate)
    grad_bias[...] = down(excite)
    grad_expand[...] = tn_exact(pooled[...], excite)
    change = nt_exact(excite, expand[...]) * (later[...] * (1.0 / PIX))
    change_low = change.astype(BF16)
    change_wide = change_low.astype(F32)
    for tap in range(9):
        rows = rows_of([snext[f, tap : tap + 1] for f in range(T)])
        grad_conv[tap] = tn_exact(rows, change_wide)[0:R]
        k_store[tap] = nt(change_low, conv_low[tap].astype(BF16))
    index = lax.broadcasted_iota(jnp.int32, (16, GW), 0)

    def stacked(f):
        result = jnp.zeros((16, GW), F32)
        for tap in range(9):
            result = jnp.where(index == tap, k_store[tap, f : f + 1], result)
        return result

    for clip in range(CLIPS):
        k_send[clip] = stacked(clip * SPAN + 1)
    onward = sent(k_send, k_recv, ssems.at[9, 0], rsems.at[9, 0], following)

    @pl.when(has_next)
    def _():
        onward.start()
        onward.wait_send()

    @pl.when(has_prev)
    def _():
        onward.wait_recv()

    @pl.when(jnp.logical_not(has_prev))
    def _():
        k_recv[...] = jnp.zeros_like(k_recv)

    sums[...] = jnp.zeros_like(sums)
    grad_reduce[...] = jnp.zeros_like(grad_reduce)
    for f in range(T):
        spreads[f] = k_recv[f // SPAN] if f % SPAN == 0 else stacked(f - 1)
        changes[f] = change[f : f + 1]
        gate_sum[f] = 1.0 + gate[f : f + 1]

    def finish_frame(f):
        motion = tn_exact(windows[...].astype(F32), spreads[f]) - changes[f]
        motion_low = motion.astype(BF16)
        centred = unit(pre[f], stats)
        z = centred * pair[0:1] + pair[1:2]
        slope = sigmoid(z)
        hidden = z * slope
        grad_reduce[...] += tn(motion_low, hidden.astype(BF16))[0:R]
        grad = mixed[f] * gate_sum[f] + nt(motion_low, reduce_low[...])
        grad = grad * (slope + hidden * (1.0 - slope))
        grad_one[f] = grad
        sums[0:1] += down(grad)
        sums[1:2] += down(grad * centred)

    each(0, T, finish_frame)
    swap[0]()
    if edge:

        def assemble(place):
            grad_mta[:, lanes(place, GW)] = edge_from_tiles(
                tiles, place, edge, grad_mta.shape[1] // ntm
            )

        each(0, grad_mta.shape[1] // GW, assemble)
    else:
        grad_mta[...] = tiles[...]
    swap[1]()
    run_steps(steps[3])
    swap[2]()


def back_in_one(
    tab, grads, pre, stats, pair, totals, video, weight, order, grad_before,
    grad_weight, grad_video, lows, held, sem,
):
    i = pl.program_id(0)
    load = pltpu.make_async_copy(video, held, sem)
    centred = unit(pre[0], stats)
    low = norm_back(grads[0], centred, stats, pair, totals, tab[0, i], tab[3, 2]).astype(BF16)
    lows[i] = low

    @pl.when(i == 0)
    def _():
        load.start()

    grad = nt(low, weight[...]) + tn(order[...], grad_before[0])
    grad_video[0] = (grad * tab[0, i]).astype(BF16)

    def products(steps):
        def run():
            if steps[0] == 0:
                load.wait()

            def product(k):
                source = held[:, :, lanes(k, WIDE_TILE)].reshape(ROWS, WIDE_TILE)
                value = tn(source, lows[...].reshape(ROWS, M))
                grad_weight[rows_at(k, WIDE_TILE)] = value.astype(BF16)

            each(steps[0], steps[-1] + 1, product)

        return run

    half = WIDE_STEPS // 2
    return [products(range(half)), products(range(half, WIDE_STEPS))]


def pack_sums(packed, reduce, expand, conv, bias, taps, source, one, last):
    packed[...] = jnp.zeros_like(packed)
    for k in range(M // GW):
        part = slice(k * GW, (k + 1) * GW)
        packed[k * R : (k + 1) * R] = reduce[:, part]
        packed[128 + k * R : 128 + (k + 1) * R] = expand[0:R, part]
        packed[352 + k : 353 + k] = bias[:, part]
    for group in range(3):
        value = conv[4 * group]
        for k in range(1, min(4, 9 - 4 * group)):
            value = value + pltpu.roll(conv[4 * group + k], k * R, 1)
        packed[256 + group * R : 256 + (group + 1) * R] = value
    packed[360:369] = taps[...]
    lane = lax.broadcasted_iota(jnp.int32, (1, GW), 1)
    row = jnp.zeros((1, GW), F32)
    for k, value in enumerate((source[0:1], one[0:1], one[1:2], last[0:1], last[1:2])):
        row = jnp.where(lane == k, jnp.sum(value, axis=1, keepdims=True), row)
    packed[376:377] = row


def unpack_sums(summed, reduce, expand, conv, bias, taps, squares):
    for k in range(M // GW):
        part = slice(k * GW, (k + 1) * GW)
        reduce[:, part] = summed[k * R : (k + 1) * R]
        expand[:, part] = summed[128 + k * R : 128 + (k + 1) * R]
        bias[:, part] = summed[352 + k : 353 + k]
    for tap in range(9):
        group, k = divmod(tap, 4)
        value = summed[256 + group * R : 256 + (group + 1) * R]
        conv[tap] = value if k == 0 else pltpu.roll(value, GW - k * R, 1)
    taps[...] = summed[360:369]
    squares[...] = summed[376:384]


def final_sums(ndp, ntm, *refs):
    ins, outs = (refs[:8], refs[8:14])
    packed, summed, first, second, sems = refs[14:]
    greet(ndp, ntm)
    pack_sums(packed, *ins)
    met(ndp, ntm)
    run_steps(all_sums_steps(ndp, ntm, packed, summed, first, second, sems))
    unpack_sums(summed, *outs)


def last_part(ndp, ntm, items, own_items, *refs):
    tab, grads, pre, stats, pair, totals, video, weight, order, grad_before = refs[:10]
    small_ins, refs = (refs[10:18], refs[18:])
    sources, refs = (refs[: len(items)], refs[len(items) :])
    grad_video, small_outs, refs = (refs[0], refs[1:7], refs[7:])
    outs, refs = (refs[: len(items)], refs[len(items) :])
    own_out, refs = (refs[0], refs[1:])
    lows, held, sem, grad_weight, packed, summed, first, second, sems = refs[:9]
    count = 5 * len(scatter_chunks(items)) + 2
    i = pl.program_id(0)
    load = pltpu.make_async_copy(video, held, sem)
    large = scatter_steps(ndp, ntm, items, sources, outs, refs[9 : 9 + count])
    own = scatter_steps(ndp, ntm, own_items, [grad_weight], [own_out], refs[9 + count :])
    small = all_sums_steps(ndp, ntm, packed, summed, first, second, sems)

    @pl.when(i == 0)
    def _():
        greet(ndp, ntm)
        load.start()
        pack_sums(packed, *small_ins)
        met(ndp, ntm)
        run_steps(large[0])
        small[0]()

    @pl.when(i < T)
    def _():
        centred = unit(pre[0], stats)
        low = norm_back(grads[0], centred, stats, pair, totals, tab[0, i], tab[3, 2])
        lows[i] = low.astype(BF16)

    @pl.when(i == T - 1)
    def _():
        load.wait()
        small[1]()
        run_steps(large[1])

        def product(k):
            source = held[:, :, lanes(k, WIDE_TILE)].reshape(ROWS, WIDE_TILE)
            value = tn(source, lows[...].reshape(ROWS, M)).astype(BF16)
            grad_weight[k // 2, lax.rem(k, 2)] = value.reshape(2, C // 8, M)

        each(0, WIDE_STEPS, product)
        run_steps(own[0])

    @pl.when(i >= T)
    def _():
        grad = nt(lows[i - T], weight[...]) + tn(order[...], grad_before[0])
        grad_video[0] = (grad * tab[0, i - T]).astype(BF16)

    @pl.when(i == T)
    def _():
        small[2]()

    @pl.when(i == T + 2)
    def _():
        run_steps(own[1])

    @pl.when(i == T + 3)
    def _():
        run_steps(large[2])
        small[3]()

    @pl.when(i == 2 * T - 1)
    def _():
        run_steps(large[3])
        run_steps(own[2])
        small[4]()
        unpack_sums(summed, *small_outs)
        run_steps(large[4])
        run_steps(own[3])
        run_steps(own[4])


def wrap(
    fast, reduce, expand, conv, bias, taps, squares, swap, one, two, alpha, beta, three, last, *refs
):
    ins, refs = (refs[:6], refs[6:]) if fast else ((), refs)
    loads, stores = ([], [])
    if fast:
        *targets, held_one, held_two, sems = refs[-5:]
        refs = refs[:-5]
        for k, (source, target, held) in enumerate(
            zip(ins[4:6], targets, (held_one, held_two))
        ):
            size = source.shape[0] // T
            for j in range(T):
                part = pl.ds(j * size, size)
                loads.append(
                    pltpu.make_async_copy(source.at[part], held.at[part], sems.at[k, 0, j])
                )
                stores.append(
                    pltpu.make_async_copy(held.at[part], target.at[part], sems.at[k, 1, j])
                )
    start_all(loads)
    wrap_small(
        fast, reduce, expand, conv, bias, taps, squares, swap, one, two, alpha, beta, three,
        last, ins, refs,
    )
    for load, store in zip(loads, stores):
        load.wait()
        store.start()
    wait_all(stores)


def wrap_small(
    fast, reduce, expand, conv, bias, taps, squares, swap, one, two, alpha, beta, three, last, ins,
    refs,
):
    mid, wide, taps_out, reduce_out, conv_out, expand_out, bias_out, rms = refs[:8]
    for k, totals in enumerate((one, two, alpha, beta)):
        mid[k, 0:1] = totals[1:2]
        mid[k, 1:2] = totals[0:1]
    for k, (gain, shift) in enumerate(((three[1:2], three[0:1]), (last[1:2], last[0:1]))):
        wide[k, 0:1] = gain
        wide[k, 1:2] = shift
    wide[2, 0:1] = last[2:3]
    wide[2, 1:2] = last[0:1]
    for k in range(3):
        taps_out[k] = taps[3 * k : 3 * k + 3]
    reduce_out[...] = reduce[...]
    conv_out[...] = conv[:, :, 0:R]
    expand_out[...] = expand[...]
    bias_out[...] = bias[...]
    lane = lax.broadcasted_iota(jnp.int32, (1, GW), 1)
    total = swap[5:6]
    counts = jnp.where(lane < 3, total * PIX, total * QUARTER) * C
    rms[...] = jnp.sqrt(squares[0:1] / counts)[:, 0:5]
    if fast:
        mta, in1, projection, over = ins[:4]
        in1_out, mta_out, out1_out, in2_out, mid2_out, out2_out, proj_out = refs[8:15]
        in1_out[...] = in1[...]
        mta_out[...] = mta[:, 0 : mta_out.shape[1]]
        proj_out[...] = projection[...].astype(F32)
        at = 0
        for target in (mid2_out, in2_out, out2_out, out1_out):
            rows = target.shape[0]
            for k in range(target.shape[1] // GW):
                target[:, k * GW : (k + 1) * GW] = over[at : at + rows].astype(F32)
                at += rows


def parity_order():
    order = np.zeros((PIX, PIX), np.float32)
    for y in range(HW):
        for x in range(HW):
            row = ((y % 2) * 2 + x % 2) * QUARTER + (y // 2) * (HW // 2) + x // 2
            order[row, y * HW + x] = 1.0
    return order


def window_rows():
    rows = np.zeros((16, PIX), np.float32)
    for tap in range(9):
        for y in range(HW):
            for x in range(HW):
                inside = 0 <= y - (tap // 3 - 1) < HW and 0 <= x - (tap % 3 - 1) < HW
                rows[tap, y * HW + x] = float(inside)
    return rows


def fetch(shard):
    partly = lax.all_gather(shard.astype(BF16), "tm", axis=1, tiled=True)
    return lax.all_gather(partly, "dp", axis=0, tiled=True)


def deliver(gradient):
    partly = lax.psum_scatter(gradient, "dp", scatter_dimension=0, tiled=True)
    return lax.psum_scatter(partly, "tm", scatter_dimension=1, tiled=True).astype(F32)


def padded(values, rows, cols):
    return jnp.pad(values, ((0, rows - values.shape[0]), (0, cols - values.shape[1])))


def tables(lengths, ndp, ntm):
    d, t = (lax.axis_index("dp"), lax.axis_index("tm"))
    grouped = lengths.reshape(ndp, CLIPS)
    starts = jnp.arange(ntm, dtype=jnp.int32) * SPAN
    counts = jnp.sum(jnp.clip(grouped[:, :, None] - starts, 0, SPAN), axis=1).astype(F32)
    own = lax.dynamic_slice_in_dim(lengths, d * CLIPS, CLIPS)
    stamps = t * SPAN + jnp.arange(SPAN, dtype=jnp.int32)
    mask = (stamps[None, :] < own[:, None]).astype(F32).reshape(T)
    later = (stamps[None, :] + 1 < own[:, None]).astype(F32).reshape(T)
    total = jnp.sum(lengths).astype(F32)
    before = jnp.cumsum(mask) - mask
    held = jnp.maximum(before + mask, 1.0)
    local = jnp.maximum(jnp.sum(mask), 1.0)
    full, half = (1.0 / PIX, 1.0 / QUARTER)
    last = jnp.stack([full / local, half / local, full / total, half / total, total, total])
    tab = jnp.stack([mask, mask / held, before * mask / held, last])
    width = max(ndp, ntm)
    column = lax.dynamic_slice_in_dim(counts, t, 1, axis=1)[:, 0]
    sums = jnp.sum(counts, axis=0)

    def row(values):
        return jnp.pad(values, (0, width - values.shape[0]))

    swap = jnp.stack(
        [
            row(column / jnp.maximum(jnp.sum(column), 1.0)),
            row(column),
            row(sums / total),
            row(sums),
            jnp.broadcast_to(1.0 / total, (width,)),
        ]
    )
    return (tab, swap, later, total)


def local(
    video, lengths, mid_norms, wide_norms, taps, me_reduce, me_conv, me_expand, me_bias,
    w_in1, w_mta, w_out1, w_in2, w_mid2, w_out2, w_proj, grad_out,
):
    ndp, ntm = (lax.axis_size("dp"), lax.axis_size("tm"))
    fast = ndp == 8 and ntm == 4
    order = jnp.asarray(parity_order(), BF16)
    windows = jnp.asarray(window_rows(), BF16)
    frames = video.reshape(T, PIX, C)
    cotangent = grad_out.reshape(HALF_ROWS, C)
    bias = me_bias.reshape(1, M)
    tap_rows = taps.reshape(9, 1, GW)
    main_pairs = jnp.concatenate([wide_norms[1], wide_norms[2]], axis=0)
    stage = functools.partial(staged, ndp=ndp, ntm=ntm)

    def gathered(rows):
        return lax.all_gather(rows, "dp", axis=0, tiled=True)

    edge = w_mta.shape[1]
    edge_wide = -(-edge // GW) * GW
    small = (8, GW)
    if fast:
        shard_rows = [w_in1.shape, (w_mta.shape[0], edge_wide), w_out1.shape, w_mid2.shape]
        wide_rows = [(rows, cols * ntm) for rows, cols in shard_rows]
        (
            full_in1, full_mta, rows_out1, rows_mid2, pair, tab, swap, later, reduce_low,
            conv_low, expand,
        ) = remote_call(
            "first_gather", functools.partial(first_gather, ndp, ntm), 1,
            [SCALARS] + [WHOLE] * 9, [WHOLE] * 11,
            [shaped((4, 2) + shape, BF16) for shape in wide_rows[:2]]
            + [shaped(shape, BF16) for shape in wide_rows[2:]]
            + [
                shaped(((C + M) // 8, WIDE_TILE), BF16), shaped(small), shaped(small), shaped(small), shaped((M, GW), BF16),
                shaped((9, GW, GW)), shaped((GW, M)),
            ],
            [VMEM(shape, BF16) for shape in shard_rows] + [DMA((4, 4, 3, ntm)), DMA((2, 4, 4, 2))],
            1 << 24,
            lengths, w_in1, w_mta, w_out1, w_mid2, w_proj, w_out2, me_reduce.T, me_conv.reshape(9, R, R),
            me_expand,
        )
        full_in1 = full_in1.reshape(C, M)
        full_mta = full_mta.reshape(GW, ntm * edge_wide)
        full_mid2 = gathered(rows_mid2)
        joined = lax.all_gather(pair, ("dp", "tm"), axis=0, tiled=True)
    else:
        tab, swap, later, total = tables(lengths, ndp, ntm)
        later = jnp.broadcast_to(jnp.pad(later, (0, 2))[:, None], small)
        reduce_low = padded(me_reduce, M, GW).astype(BF16)
        conv_low = jnp.pad(me_conv.reshape(9, R, R), ((0, 0), (0, GW - R), (0, GW - R)))
        conv_low = conv_low.astype(BF16).astype(F32)
        expand = padded(me_expand, GW, M)
        full_in1, full_mta, full_out1, full_in2, full_mid2, full_out2, full_proj = [
            fetch(shard) for shard in (w_in1, w_mta, w_out1, w_in2, w_mid2, w_out2, w_proj)
        ]
        full_mta = jnp.transpose(full_mta.reshape(GW, 27, GW), (1, 0, 2))
        halves = [
            jnp.transpose(full.reshape(8, -1, WIDE_STEPS, WIDE_TILE), (0, 2, 1, 3))
            for full in (full_proj, full_out2)
        ]
        joined = jnp.concatenate(halves, axis=2)
    joined = joined.reshape(8, WIDE_STEPS, (C + M) // 8, WIDE_TILE)

    frame_wide, frame_mid = (at_first((1, PIX, C)), at_first((1, PIX, M)))
    pair_mid, pair_wide = (fixed((2, M)), fixed((2, C)))
    wide_low, mid_wide = (shaped((T, PIX, C), BF16), shaped((T, PIX, M)))
    even_spec = fixed((T, QUARTER, C))
    order_spec = fixed((PIX, PIX))
    half_mid = fixed((HALF_ROWS, M))
    ins_tab = (tab, SCALARS)
    mids = [(mid_norms[k], pair_mid) for k in range(4)]
    order_in = (order, order_spec)

    pre, squares_source, stats_one, *rows = stage(
        "in_one", 2, steps=T, body=in_one,
        ins=[ins_tab, (frames, frame_wide), (full_in1, fixed((C, M)))],
        outs=[(mid_wide, frame_mid), (shaped((1, C)), fixed((1, C))), LOCAL],
        scratch=[], cost=2 * ROWS * C * M, swap=(swap, PIX, (2, M)),
        carry=(w_in2,) if fast else (),
    )

    frame_low = (T, PIX, GW)
    carried = [rows_out1, *rows] if fast else []
    agg, stats_two, ext, blended, sigma, snext, pooled, kernels, *rows = remote_call(
        "mta_forward", functools.partial(mta_forward, ndp, ntm, fast, edge), 3,
        [SCALARS] * 2 + [WHOLE] * (11 + len(carried)),
        [WHOLE] * (8 + len(carried)),
        [
            mid_wide, shaped((2, M)), shaped((3, CLIPS, 4, PIX, GW), BF16),
            shaped((3,) + frame_low, BF16), shaped((8, M)), shaped((T, 16, GW)), shaped((8, GW)),
            shaped((3, 3, 3 * GW, GW), BF16),
        ]
        + [shaped((4, 2) + part.shape, BF16) for part in carried],
        [
            VMEM((T, PIX, M), F32), VMEM((SPAN, PIX + 2 * HW, 3 * GW), BF16),
            VMEM((3, CLIPS, 4, PIX, GW), BF16), VMEM((2, CLIPS, SPAN, PIX, GW), F32),
            VMEM((T, 1, M), F32), VMEM((T, 16, GW), F32), VMEM((CLIPS, 16, GW), F32),
            VMEM((CLIPS, 16, GW), F32), DMA((10, 2)), DMA((10, 2)),
        ]
        + swap_scratch(ndp, ntm, (2, M))
        + ([DMA((2, 2, 1, 1)), DMA((2, 4, 2, 2))] if fast else []),
        2 * ROWS * 9 * GW * GW * 3,
        swap, tab, pre, stats_one, mid_norms[0], reduce_low, conv_low, expand, bias, full_mta,
        tap_rows, windows, later, *carried,
    )
    if fast:
        full_out1, full_in2 = (rows[0].reshape(M, C), rows[1].reshape(C, M))

    hidden_two, pre_three, stats_three = stage(
        "out_one", 4, steps=T, body=out_one,
        ins=[
            ins_tab, (agg, frame_mid), (stats_two, pair_mid), mids[1], order_in,
            (full_out1, fixed((M, C))),
        ],
        outs=[(shaped((T, PIX, M), BF16), frame_mid), (shaped((T, PIX, C)), frame_wide), LOCAL],
        scratch=[], cost=2 * ROWS * C * M, swap=(swap, PIX, (2, C)),
    )

    out_low, centred_three, slope, first_two, squares_one, stats_alpha = stage(
        "in_two", 5, steps=T, body=in_two,
        ins=[
            ins_tab, (frames, frame_wide), (pre_three, frame_wide), (stats_three, pair_wide),
            (wide_norms[0], pair_wide), order_in, (full_in2, fixed((C, M))),
        ],
        outs=[
            (wide_low, frame_wide), (wide_low, frame_wide), (wide_low, frame_wide),
            (mid_wide, frame_mid), (shaped((2, C)), pair_wide), LOCAL,
        ],
        scratch=[], cost=2 * ROWS * C * M, swap=(swap, PIX, (2, M)),
    )

    stride_taps, second_two, stats_beta = stage(
        "mid_two", 6, steps=9, body=mid_two,
        ins=[
            ins_tab, (first_two, fixed((T, PIX, M))), (stats_alpha, pair_mid), mids[2],
            (full_mid2, at_last((M, M))),
        ],
        outs=[
            (shaped((9, HALF_ROWS, M), BF16), at_first((1, HALF_ROWS, M))),
            (shaped((HALF_ROWS, M)), half_mid), LOCAL,
        ],
        scratch=[VMEM((9, HALF_ROWS, M), BF16)], cost=2 * HALF_ROWS * 9 * M * M,
        swap=(swap, QUARTER, (2, M)),
    )

    tile = (HALF_ROWS, WIDE_TILE)
    steps = WIDE_STEPS

    def result_at(i):
        return jnp.clip(i - steps, 0, steps - 1)

    def pair_at(i):
        return jnp.where(i < steps, 0, lax.rem(i, steps))

    many = (steps, 4, WIDE_TILE)
    four_sums = [
        VMEM(many, F32), VMEM((steps, ndp, 4, WIDE_TILE), F32),
        VMEM((steps, ntm, 4, WIDE_TILE), F32), DMA((steps, 4, max(ndp, ntm))),
    ]
    result, grad_w_out2, grad_w_proj, grad_even, grad_beta, squares_last, totals_last, totals_beta = (
        pl.pallas_call(
            functools.partial(middle, ndp, ntm),
            name="middle",
            grid=(3 * steps,),
            in_specs=[
                SCALARS, SCALARS, half_mid, pair_mid, pair_mid,
                ANY, even_spec,
                pl.BlockSpec((4, WIDE_TILE), lambda i: (0, pair_at(i))),
                pl.BlockSpec(tile, lambda i: (0, result_at(i))),
            ],
            out_specs=[
                pl.BlockSpec(tile, lambda i: (0, result_at(i))), ANY, ANY, fixed((HALF_ROWS, C)),
                half_mid, pl.BlockSpec((2, WIDE_TILE), lambda i: (0, result_at(i))),
                fixed((4, C)), pair_mid,
            ],
            out_shape=[
                shaped((HALF_ROWS, C), BF16), shaped((M, C), BF16), shaped((C, C), BF16),
                shaped((HALF_ROWS, C)), shaped((HALF_ROWS, M)), shaped((2, C)), shaped((4, C)),
                shaped((2, M)),
            ],
            scratch_shapes=[
                VMEM((HALF_ROWS, M), BF16), VMEM((steps,) + tile, F32), VMEM((steps,) + tile, F32),
                VMEM((steps,) + tile, F32), VMEM(many, F32), VMEM(many, F32),
                VMEM((HALF_ROWS, M), F32), VMEM((steps,) + tile, BF16),
                VMEM((steps,) + tile, BF16), VMEM((steps, M, WIDE_TILE), BF16),
                VMEM((steps, C, WIDE_TILE), BF16), VMEM((steps, 8, (C + M) // 8, WIDE_TILE), BF16),
                DMA((3, steps)),
            ]
            + four_sums * 2
            + swap_scratch(ndp, ntm, (2, M)),
            cost_estimate=pl.CostEstimate(flops=1024, bytes_accessed=1024, transcendentals=0),
            compiler_params=pltpu.CompilerParams(
                vmem_limit_bytes=LIMIT, collective_id=7, has_side_effects=True
            ),
        )(
            swap, tab, second_two, stats_beta, mid_norms[3], joined, out_low, main_pairs, cotangent,
        )
    )
    if fast:
        proj_part = lax.psum_scatter(grad_w_proj, "dp", scatter_dimension=0, tiled=True)
        cube_out2 = cubed(grad_w_out2)

    def scattered(*pairs):
        if not fast:
            return {}
        return {"items": [item for item, _ in pairs], "sources": [source for _, source in pairs]}

    grad_w_mid2, grad_alpha, totals_alpha = stage(
        "back_mid", 10, steps=9, body=back_mid,
        ins=[
            ins_tab, (grad_beta, half_mid), (second_two, half_mid), (stats_beta, pair_mid),
            mids[3], (totals_beta, pair_mid), (stride_taps, ANY), (full_mid2, at_last((M, M))),
            (first_two, fixed((T, PIX, M))), (stats_alpha, pair_mid), mids[2],
        ],
        outs=[
            (shaped((M, 9 * M), BF16), fixed((M, 9 * M))), (mid_wide, fixed((T, PIX, M))), LOCAL,
        ],
        scratch=[
            VMEM((HALF_ROWS, M), BF16), VMEM((T, PIX, M), F32), VMEM((9, HALF_ROWS, M), BF16),
            DMA, VMEM((HALF_ROWS, M), F32),
        ],
        cost=4 * HALF_ROWS * 9 * M * M, swap=(swap, None, (2, M)),
    )
    cube_mid2 = cubed(grad_w_mid2) if fast else None

    grad_w_in2, grad_before_one, totals_three = stage(
        "back_in_two", 11, steps=T, body=back_in_two,
        ins=[
            ins_tab, (grad_alpha, frame_mid), (first_two, frame_mid), (stats_alpha, pair_mid),
            mids[2], (totals_alpha, pair_mid), (out_low, ANY), (full_in2, fixed((C, M))),
            (grad_even, at_first((QUARTER, C))), (slope, frame_wide), (centred_three, frame_wide),
        ],
        outs=[(shaped((C, M), BF16), fixed((C, M))), (wide_low, frame_wide), LOCAL],
        scratch=[VMEM((T, PIX, M), BF16), VMEM((T, PIX, C), BF16), DMA],
        cost=4 * ROWS * C * M, swap=(swap, None, (2, C)),
    )
    cube_in2 = cubed(grad_w_in2) if fast else None

    grad_w_out1, grad_two, totals_two = stage(
        "back_out_one", 12, steps=T, body=back_out_one,
        ins=[
            ins_tab, (grad_before_one, frame_wide), (centred_three, frame_wide),
            (stats_three, pair_wide), (wide_norms[0], pair_wide), (totals_three, pair_wide),
            (hidden_two, ANY), (full_out1, fixed((M, C))), order_in, (agg, frame_mid),
            (stats_two, pair_mid), mids[1],
        ],
        outs=[(shaped((M, C), BF16), fixed((M, C))), (mid_wide, frame_mid), LOCAL],
        scratch=[VMEM((T, PIX, C), BF16), VMEM((T, PIX, M), BF16), DMA],
        cost=4 * ROWS * C * M, swap=(swap, None, (2, M)),
    )
    cube_out1 = cubed(grad_w_out1) if fast else None

    early = {}
    if fast:
        totals_two, proj_part = lax.optimization_barrier((totals_two, proj_part))
        sent_proj = lax.psum_scatter(proj_part, "tm", scatter_dimension=1, tiled=True)
        early = scattered(
            ((0, 64, 9 * M, 2), cube_mid2), ((0, 256, M, 2), cube_in2),
            ((0, 64, C, 2), cube_out2), ((0, 64, C, 2), cube_out1),
        )
    items = early.get("items", [])
    z_rows = sum(rows * (cols // ntm // GW) for _, rows, cols, _ in items)
    mta_shape = (GW, ntm * edge_wide) if fast else (27, GW, GW)
    (
        grad_one, totals_one, grad_w_mta, grad_reduce, grad_conv, grad_expand, grad_bias, grad_taps,
        *sent_d,
    ) = remote_call(
        "mta_backward",
        functools.partial(mta_backward, ndp, ntm, items, edge if fast else None), 13,
        [SCALARS] + [WHOLE] * 20 + [ANY] * len(items),
        [WHOLE] * (9 if items else 8),
        [
            mid_wide, shaped((2, M)), shaped(mta_shape, BF16), shaped((R, M)),
            shaped((9, R, GW)), shaped((GW, M)), shaped((1, M)), shaped((9, GW)),
        ]
        + ([shaped((ntm, z_rows, GW), BF16)] if items else []),
        [
            VMEM((T, PIX, M), F32), VMEM(frame_low, BF16),
            VMEM((SPAN, PIX + 2 * HW, 3 * GW), BF16), VMEM((CLIPS, SPAN, PIX, GW), F32),
            VMEM((SPAN, PIX, GW), F32),
            VMEM((3, CLIPS, 2, PIX, GW), BF16), VMEM((3, CLIPS, 2, PIX, GW), BF16),
            VMEM((3, 3 * GW, GW), F32), VMEM((9, 8, GW), F32), VMEM((CLIPS, 16, GW), F32),
            VMEM((CLIPS, 16, GW), F32), VMEM((T, 1, M), F32), DMA((10, 2)), DMA((10, 2)),
            VMEM((27, GW, GW), BF16), VMEM((9, 1, GW), F32), VMEM((T, 16, GW), F32),
            VMEM((T, 1, GW), F32),
        ]
        + swap_scratch(ndp, ntm, (2, M))
        + (scatter_scratch(items, ntm) if items else []),
        4 * ROWS * 9 * GW * GW * 3,
        tab, grad_two, agg, stats_two, mid_norms[1], totals_two, pre, stats_one, mid_norms[0],
        sigma, ext, blended, kernels, tap_rows, reduce_low, conv_low, expand, windows, later,
        snext, pooled, *early.get("sources", []),
    )

    if fast:
        z_part = sent_d[0].reshape(ntm * z_rows, GW)
        sent_z = lax.psum_scatter(z_part, "tm", scatter_dimension=0, tiled=True)
    small_in = [
        grad_reduce, grad_expand, grad_conv, grad_bias, grad_taps, squares_source, squares_one,
        squares_last,
    ]
    small_out = [
        shaped((R, M)), shaped((R, M)), shaped((9, R, GW)), shaped((1, M)), shaped((9, GW)),
        shaped((8, GW)),
    ]
    unit_rows = 8 * ndp * ntm
    rows = -(-384 // unit_rows) * unit_rows
    small_scratch = [VMEM((rows, GW), F32)] * 2 + all_sums_scratch(ndp, ntm, rows)
    frame_scratch = [VMEM((T, PIX, M), BF16), VMEM((T, PIX, C), BF16), DMA]
    if fast:
        late = scattered(((0, 16, ntm * edge_wide, 1), cubed(grad_w_mta)))
        items, own_items = (late["items"], [(0, 256, M, 2)])

        def early_frame(shape):
            return pl.BlockSpec(shape, lambda i: (jnp.minimum(i, T - 1), 0, 0))

        def late_frame(shape):
            return pl.BlockSpec(shape, lambda i: (jnp.maximum(i - T, 0), 0, 0))

        grad_frames, *rest = pl.pallas_call(
            functools.partial(last_part, ndp, ntm, items, own_items),
            name="last_part",
            grid=(2 * T,),
            in_specs=[
                SCALARS, early_frame((1, PIX, M)), early_frame((1, PIX, M)), pair_mid, pair_mid,
                pair_mid, ANY, fixed((C, M)), order_spec, late_frame((1, PIX, C)),
            ]
            + [fixed(part.shape) for part in small_in]
            + [ANY] * len(items),
            out_specs=[late_frame((1, PIX, C))]
            + [fixed(part.shape) for part in small_out]
            + [fixed((rows_, cols // ntm)) for _, rows_, cols, _ in items + own_items],
            out_shape=[wide_low]
            + small_out
            + [shaped((rows_, cols // ntm)) for _, rows_, cols, _ in items + own_items],
            scratch_shapes=frame_scratch
            + [VMEM((2, 2, 2, C // 8, M), BF16)]
            + small_scratch
            + scatter_scratch(items, ntm)
            + scatter_scratch(own_items, ntm),
            cost_estimate=pl.CostEstimate(flops=1024, bytes_accessed=1024, transcendentals=0),
            compiler_params=pltpu.CompilerParams(
                vmem_limit_bytes=LIMIT, collective_id=14, has_side_effects=True
            ),
        )(
            tab, grad_one, pre, stats_one, mid_norms[0], totals_one, frames, full_in1, order,
            grad_before_one, *small_in, *late["sources"],
        )
        small_sums, sent_f = (rest[:6], rest[6:])
    else:
        grad_w_in1, grad_frames = stage(
            "back_in_one", 14, steps=T, body=back_in_one,
            ins=[
                ins_tab, (grad_one, frame_mid), (pre, frame_mid), (stats_one, pair_mid), mids[0],
                (totals_one, pair_mid), (frames, ANY), (full_in1, fixed((C, M))), order_in,
                (grad_before_one, frame_wide),
            ],
            outs=[(shaped((C, M), BF16), fixed((C, M))), (wide_low, frame_wide)],
            scratch=frame_scratch, cost=4 * ROWS * C * M,
        )
        small_sums = remote_call(
            "final_sums", functools.partial(final_sums, ndp, ntm), 15, [WHOLE] * 8, [WHOLE] * 6,
            small_out, small_scratch, 1 << 26, *small_in,
        )
    totals = (totals_one, totals_two, totals_alpha, totals_beta, totals_three, totals_last)
    if not fast:
        grad_w_mta = jnp.transpose(grad_w_mta, (1, 0, 2)).reshape(GW, 27 * GW)
        delivered = [
            deliver(g)
            for g in (
                grad_w_in1, grad_w_mta, grad_w_out1, grad_w_in2, grad_w_mid2, grad_w_out2,
                grad_w_proj,
            )
        ]
        swap = jnp.broadcast_to(total, (8, GW))
    wrapped = [*small_sums, swap, *totals]
    copied = []
    if fast:
        wrapped += [*sent_f, sent_proj, sent_z]
        copied = [result, grad_frames]
    shards = [
        shaped(shard.shape) for shard in (w_in1, w_mta, w_out1, w_in2, w_mid2, w_out2, w_proj)
    ]
    wrap_out = [
        shaped((4, 2, M)), shaped((3, 2, C)), shaped((3, 3, GW)), shaped((R, M)),
        shaped((9, R, R)), shaped((R, M)), shaped((1, M)), shaped((1, 5)),
    ]
    wrap_out += shards if fast else []
    (
        out_mid, out_wide, out_taps, out_reduce, out_conv, out_expand, out_bias, out_rms, *rest,
    ) = pl.pallas_call(
        functools.partial(wrap, fast),
        name="wrap",
        in_specs=[WHOLE] * len(wrapped) + [ANY] * len(copied),
        out_specs=[WHOLE] * len(wrap_out) + [ANY] * len(copied),
        out_shape=wrap_out + [shaped(part.shape, BF16) for part in copied],
        scratch_shapes=[VMEM(part.shape, BF16) for part in copied]
        + ([DMA((2, 2, T))] if fast else []),
        compiler_params=pltpu.CompilerParams(vmem_limit_bytes=LIMIT),
    )(*wrapped, *copied)
    if fast:
        *delivered, result, grad_frames = rest
    return (
        result.reshape(grad_out.shape),
        grad_frames.reshape(video.shape),
        out_mid,
        out_wide,
        out_taps,
        out_reduce.T,
        out_conv.reshape(3, 3, R, R),
        out_expand,
        out_bias.reshape(M),
        *delivered,
        out_rms.reshape(5),
    )


def solution(mesh):
    clip_spec = P("dp", "tm", None, None, None)
    return jax.shard_map(
        local,
        mesh=mesh,
        in_specs=(clip_spec,) + (P(),) * 8 + (P("dp", "tm"),) * 7 + (clip_spec,),
        out_specs=(clip_spec,) * 2 + (P(),) * 7 + (P("dp", "tm"),) * 7 + (P(),),
        check_vma=False,
    )
```

```python
import functools

import jax
import jax.numpy as jnp
import numpy as np
from jax import lax
from jax.experimental import pallas as pl
from jax.experimental.pallas import tpu as pltpu
from jax.sharding import PartitionSpec as P

C = 2048
M = 512
R = 32
GW = 128
HW = 16
PIX = HW * HW
QUARTER = PIX // 4
CLIPS = 3
SPAN = 2
T = CLIPS * SPAN
ROWS = T * PIX
HALF_ROWS = T * QUARTER
WIDE_TILE = 512
WIDE_STEPS = C // WIDE_TILE

EPSILON = 1e-05
HIGHEST = lax.Precision.HIGHEST
F32 = jnp.float32
BF16 = jnp.bfloat16
MESH = pl.DeviceIdType.MESH
VMEM = pltpu.VMEM
DMA = pltpu.SemaphoreType.DMA
LIMIT = 60 * 1024 * 1024

WHOLE = pl.BlockSpec(memory_space=pltpu.VMEM)
SCALARS = pl.BlockSpec(memory_space=pltpu.SMEM)
ANY = pl.BlockSpec(memory_space=pl.ANY)


def shaped(shape, dtype=F32):
    return jax.ShapeDtypeStruct(shape, dtype)


def fixed(shape):
    return pl.BlockSpec(shape, lambda i: (0,) * len(shape))


def at_first(shape):
    return pl.BlockSpec(shape, lambda i: (i,) + (0,) * (len(shape) - 1))


def at_last(shape):
    return pl.BlockSpec(shape, lambda i: (0,) * (len(shape) - 1) + (i,))


def remote_call(name, body, ident, in_specs, out_specs, out_shape, scratch, cost, *operands):
    return pl.pallas_call(
        body,
        name=name,
        in_specs=in_specs,
        out_specs=out_specs,
        out_shape=out_shape,
        scratch_shapes=scratch,
        cost_estimate=pl.CostEstimate(flops=1024, bytes_accessed=1024, transcendentals=0),
        compiler_params=pltpu.CompilerParams(
            vmem_limit_bytes=LIMIT, collective_id=ident, has_side_effects=True
        ),
    )(*operands)


def sigmoid(z):
    return 0.5 * jnp.tanh(0.5 * z) + 0.5


def nn(left, right):
    return jnp.dot(left, right, preferred_element_type=F32)


def nt(left, right):
    return lax.dot_general(left, right, (((1,), (1,)), ((), ())), preferred_element_type=F32)


def tn(left, right):
    return lax.dot_general(left, right, (((0,), (0,)), ((), ())), preferred_element_type=F32)


def nn_exact(left, right):
    return jnp.dot(left, right, precision=HIGHEST, preferred_element_type=F32)


def nt_exact(left, right):
    return lax.dot_general(
        left, right, (((1,), (1,)), ((), ())), precision=HIGHEST, preferred_element_type=F32
    )


def tn_exact(left, right):
    return lax.dot_general(
        left, right, (((0,), (0,)), ((), ())), precision=HIGHEST, preferred_element_type=F32
    )


def down(values):
    return jnp.sum(values, axis=0, keepdims=True)


def merge(stats, values, tab, i):
    rows = values.shape[0]
    mean = down(values) * (1.0 / rows)
    spread = down(jnp.square(values - mean))
    delta = mean - stats[0:1]
    stats[0:1] += delta * tab[1, i]
    stats[1:2] += spread * tab[0, i] + jnp.square(delta) * (tab[2, i] * rows)


def whole_stats(parts, masks, inv_count):
    mean = sum(down(part) * mask for part, mask in zip(parts, masks)) * inv_count
    spread = sum(down(jnp.square(part - mean)) * mask for part, mask in zip(parts, masks))
    return (mean, spread)


def unit(values, stats):
    return (values - stats[0:1]) * stats[1:2]


def norm_back(grads, centred, stats, pair, totals, mask, inv_count):
    total, cross = (totals[0:1] * inv_count, totals[1:2] * inv_count)
    return (pair[0:1] * stats[1:2]) * (grads - mask * (total + centred * cross))


def peers_of(ndp, ntm):
    d, t = (lax.axis_index("dp"), lax.axis_index("tm"))
    along = [(lax.rem(d + k, ndp), t) for k in range(1, ndp)]
    return along, [(d, lax.rem(t + k, ntm)) for k in range(1, ntm)]


def greet(ndp, ntm):
    along, across = peers_of(ndp, ntm)
    for peer in along + across:
        pl.semaphore_signal(
            pltpu.get_barrier_semaphore(), inc=1, device_id=peer, device_id_type=MESH
        )


def met(ndp, ntm):
    pl.semaphore_wait(pltpu.get_barrier_semaphore(), ndp + ntm - 2)


def sent(source, target, out_sem, in_sem, peer):
    return pltpu.make_async_remote_copy(source, target, out_sem, in_sem, peer, MESH)


def start_all(copies):
    for copy in copies:
        copy.start()


def wait_all(copies):
    for copy in copies:
        copy.wait()


def plain_gather(parts, row, tab):
    return sum(parts[1:], parts[0])


def plain_last(value, tab):
    return value


def spread_gather(scale, parts, row, tab):
    outputs = []
    for k in range(0, parts[0].shape[0], 2):
        means = [part[k : k + 1] for part in parts]
        mean = sum(value * tab[row, s] for s, value in enumerate(means))
        spread = sum(
            part[k + 1 : k + 2] + jnp.square(value - mean) * (tab[row + 1, s] * scale)
            for s, (part, value) in enumerate(zip(parts, means))
        )
        outputs.extend([mean, spread])
    return jnp.concatenate(outputs, axis=0)


def spread_last(scale, value, tab):
    outputs = []
    for k in range(0, value.shape[0], 2):
        outputs.append(value[k : k + 1])
        outputs.append(lax.rsqrt(value[k + 1 : k + 2] * (tab[4, 0] * (1.0 / scale)) + EPSILON))
    return jnp.concatenate(outputs, axis=0)


def swap_scratch(ndp, ntm, shape):
    return [
        VMEM(shape, F32), VMEM((ndp,) + shape, F32), VMEM((ntm,) + shape, F32),
        DMA((4, max(ndp, ntm))),
    ]


def swap_steps(ndp, ntm, scale, tab, out, source, first, second, sems):
    d, t = (lax.axis_index("dp"), lax.axis_index("tm"))
    along, across = peers_of(ndp, ntm)
    if scale is None:
        gather, last = (plain_gather, plain_last)
    else:
        gather = functools.partial(spread_gather, scale)
        last = functools.partial(spread_last, scale)

    def copies(buffer, peers, k):
        return [
            sent(buffer.at[0], buffer.at[j], sems.at[2 * k, j], sems.at[2 * k + 1, j], peer)
            for j, peer in enumerate(peers, 1)
        ]

    one, two = (copies(first, along, 0), copies(second, across, 1))

    def begin():
        first[0] = source[...]
        start_all(one)

    def middle():
        wait_all(one)
        second[0] = gather([first[lax.rem(d - s + ndp, ndp)] for s in range(ndp)], 0, tab)
        start_all(two)

    def end():
        wait_all(two)
        out[...] = last(
            gather([second[lax.rem(t - s + ntm, ntm)] for s in range(ntm)], 2, tab), tab
        )

    return (begin, middle, end)


def all_sums_scratch(ndp, ntm, rows):
    return [
        VMEM((ndp, rows // ndp, GW), F32), VMEM((ntm, rows // ndp // ntm, GW), F32),
        DMA((8, max(ndp, ntm))),
    ]


def all_sums_steps(ndp, ntm, source, out, first, second, sems):
    d, t = (lax.axis_index("dp"), lax.axis_index("tm"))
    large = source.shape[0] // ndp
    small = large // ntm
    along, across = peers_of(ndp, ntm)

    def rows(group, size):
        return pl.ds(pl.multiple_of(group * size, size), size)

    def copies(pieces, peers, k):
        return [
            sent(left, right, sems.at[2 * k, j], sems.at[2 * k + 1, j], peer)
            for j, ((left, right), peer) in enumerate(zip(pieces, peers), 1)
        ]

    own = out.at[pl.ds(pl.multiple_of(d * large + t * small, small), small)]
    block = out.at[rows(d, large)]
    one = copies(
        [(source.at[rows(peer[0], large)], first.at[k]) for k, peer in enumerate(along, 1)],
        along, 0,
    )
    two = copies(
        [(first.at[0, rows(peer[1], small)], second.at[k]) for k, peer in enumerate(across, 1)],
        across, 1,
    )
    three = copies([(own, own)] * (ntm - 1), across, 2)
    four = copies([(block, block)] * (ndp - 1), along, 3)

    def begin():
        start_all(one)

    def second_step():
        wait_all(one)
        first[0] = source[rows(d, large)]
        total = first[lax.rem(d, ndp)]
        for s in range(1, ndp):
            total = total + first[lax.rem(d - s + ndp, ndp)]
        first[0] = total
        start_all(two)

    def third_step():
        wait_all(two)
        second[0] = first[0, rows(t, small)]
        total = second[lax.rem(t, ntm)]
        for s in range(1, ntm):
            total = total + second[lax.rem(t - s + ntm, ntm)]
        own[...] = total
        start_all(three)

    def fourth_step():
        wait_all(three)
        start_all(four)

    def end():
        wait_all(four)

    return [begin, second_step, third_step, fourth_step, end]


def cube(ndp, ntm):
    d, t = (lax.axis_index("dp"), lax.axis_index("tm"))
    core, x, y = (lax.rem(d, 2), lax.rem(d // 2, 2), d // 4)
    peers = ((d + 1 - 2 * core, t), (d + 2 - 4 * x, t), (d + 4 - 8 * y, t))
    return (t, core, x, y, peers)


def lanes(group, width):
    return pl.ds(pl.multiple_of(group * width, GW), width)


def over_z(ntm, low, target, sems):
    d, t = (lax.axis_index("dp"), lax.axis_index("tm"))
    slot = target.at[:, lanes(t, low.shape[1])]
    copies = [pltpu.make_async_copy(low, slot, sems.at[2, 0])]
    for k in range(1, ntm):
        copies.append(sent(low, slot, sems.at[0, k], sems.at[1, k], (d, lax.rem(t + k, ntm))))
    return copies


def gather_steps(ndp, ntm, low, full, rows, z_sems, sems):
    t, core, x, y, (to_core, to_x, to_y) = cube(ndp, ntm)
    own = full.at[2 * y + x, core]
    zs, one, two, three = ([], [], [], [])
    for k, (start, size) in enumerate(rows):
        part = pl.ds(start, size)
        if low.shape[1] == full.shape[3]:
            zs.append([pltpu.make_async_copy(low.at[part], own.at[part], z_sems.at[k, 0, 0])])
        else:
            zs.append(over_z(ntm, low.at[part], own.at[part], z_sems.at[k]))
        first, second = (to_x, to_y) if k % 2 == 0 else (to_y, to_x)
        other = (y, 1 - x) if k % 2 == 0 else (1 - y, x)
        block = full.at[2 * y + x, core, part]
        one.append([sent(block, block, sems.at[0, k, 0], sems.at[0, k, 1], first)])
        pair = []
        for j, (row, col) in enumerate(((y, x), other), 1):
            block = full.at[2 * row + col, core, part]
            pair.append(sent(block, block, sems.at[j, k, 0], sems.at[j, k, 1], second))
        two.append(pair)
        block = full.at[:, core, part]
        three.append([sent(block, block, sems.at[3, k, 0], sems.at[3, k, 1], to_core)])
    count = len(rows)

    def after(waits, starts):
        wait_all(waits)
        start_all(starts)

    return [
        [functools.partial(start_all, zs[k]) for k in range(count)],
        [functools.partial(after, zs[k], one[k]) for k in range(count)],
        [functools.partial(after, one[k], two[k]) for k in range(count)],
        [functools.partial(after, two[k], three[k]) for k in range(count)],
        [functools.partial(after, three[k], []) for k in range(count)],
    ]


def each(start, stop, body):
    def step(k, carry):
        body(k)
        return carry

    lax.fori_loop(start, stop, step, 0)


def rows_at(group, size):
    return pl.ds(pl.multiple_of(group * size, size), size)


def run_steps(steps):
    for step in steps:
        step()


def lane_row(values):
    lane = lax.broadcasted_iota(jnp.int32, (1, GW), 1)
    row = jnp.zeros((1, GW), F32)
    for k, value in enumerate(values):
        row = jnp.where(lane == k, value, row)
    return row


def fill_tables(ndp, ntm, lengths, tab, swap, later):
    d, t = (lax.axis_index("dp"), lax.axis_index("tm"))
    held = [lengths[k] for k in range(ndp * CLIPS)]
    counts = [
        [
            sum(jnp.clip(held[i * CLIPS + c] - j * SPAN, 0, SPAN) for c in range(CLIPS))
            for i in range(ndp)
        ]
        for j in range(ntm)
    ]
    sums = [sum(column) for column in counts]
    total = sum(sums).astype(F32)
    column = [
        sum(jnp.where(t == j, counts[j][i], 0) for j in range(ntm)).astype(F32) for i in range(ndp)
    ]
    mask, after = ([], [])
    for c in range(CLIPS):
        own = lengths[d * CLIPS + c]
        for k in range(SPAN):
            mask.append(jnp.where(t * SPAN + k < own, 1.0, 0.0))
            after.append(jnp.where(t * SPAN + k + 1 < own, 1.0, 0.0))
    before = [sum(mask[:k], jnp.float32(0.0)) for k in range(T)]
    mask_row, before_row = (lane_row(mask), lane_row(before))
    share = 1.0 / jnp.maximum(before_row + mask_row, 1.0)
    tab[...] = jnp.zeros_like(tab)
    tab[0:1] = mask_row
    tab[1:2] = mask_row * share
    tab[2:3] = before_row * mask_row * share
    local = jnp.maximum(sum(mask), 1.0)
    ones = jnp.full((1, GW), 1.0, F32)
    rates = lane_row([1.0 / PIX, 1.0 / QUARTER, 1.0 / PIX, 1.0 / QUARTER, 1.0, 1.0])
    bases = lane_row([local, local, total, total, 1.0, 1.0])
    tab[3:4] = rates / jnp.maximum(bases, ones)
    swap[...] = jnp.zeros_like(swap)
    here = jnp.maximum(sum(column), 1.0)
    swap[0:1] = lane_row(column) / (here * ones)
    swap[1:2] = lane_row(column)
    swap[2:3] = lane_row([value.astype(F32) for value in sums]) / (total * ones)
    swap[3:4] = lane_row([value.astype(F32) for value in sums])
    swap[4:5] = ones / (total * ones)
    swap[5:6] = total * ones
    row = lax.broadcasted_iota(jnp.int32, (8, GW), 0)
    values = jnp.zeros((8, GW), F32)
    for k, value in enumerate(after):
        values = jnp.where(row == k, value, values)
    later[...] = values


def first_gather(
    ndp, ntm, lengths, in_shard, mta_shard, out_shard, mid_shard, proj_shard, last_shard, reduce,
    conv, expand, full_in, full_mta, out_rows, mid_rows, pair, tab, swap, later, reduce_low,
    conv_low, expand_wide,
    low_in, low_mta, low_out, low_mid, z_sems, sems,
):
    greet(ndp, ntm)
    low_in[...] = in_shard[...].astype(BF16)
    low_mta[...] = jnp.zeros_like(low_mta)
    low_mta[:, : mta_shard.shape[1]] = mta_shard[...].astype(BF16)
    low_out[...] = out_shard[...].astype(BF16)
    low_mid[...] = mid_shard[...].astype(BF16)
    chunks = [(k * 128, 128) for k in range(2)]
    one = gather_steps(ndp, ntm, low_in, full_in, chunks, z_sems.at[0], sems.at[0])
    two = gather_steps(ndp, ntm, low_mta, full_mta, ((0, 16),), z_sems.at[1], sems.at[1])
    copies = over_z(ntm, low_out, out_rows, z_sems.at[2, 0])
    copies += over_z(ntm, low_mid, mid_rows, z_sems.at[3, 0])
    met(ndp, ntm)
    run_steps(one[0])
    run_steps(two[0])
    start_all(copies)
    fill_tables(ndp, ntm, lengths, tab, swap, later)
    reduce_low[...] = jnp.zeros_like(reduce_low)
    reduce_low[:, 0:R] = reduce[...].T.astype(BF16)
    conv_low[...] = jnp.zeros_like(conv_low)
    conv_low[:, 0:R, 0:R] = conv[...].astype(BF16).astype(F32)
    expand_wide[...] = jnp.zeros_like(expand_wide)
    expand_wide[0:R] = expand[...]
    pair[0 : C // 8] = proj_shard[...].astype(BF16)
    pair[C // 8 :] = last_shard[...].astype(BF16)
    for k in range(1, 5):
        run_steps(one[k])
        run_steps(two[k])
    wait_all(copies)


def scatter_chunks(items):
    chunks = []
    for item, (base, rows, cols, parts) in enumerate(items):
        size = rows // parts
        for part in range(parts):
            chunks.append((item, base + part * size, part * size, size, cols))
    return chunks


def scatter_scratch(items, ntm):
    chunks = scatter_chunks(items)
    scratch = []
    for _, _, _, rows, cols in chunks:
        scratch += [
            VMEM((2, 2, rows, cols), BF16), VMEM((2, 2, rows, cols), BF16),
            VMEM((2, rows, cols), BF16), VMEM((rows, cols), BF16),
            VMEM((ntm, rows, cols // ntm), BF16),
        ]
    return scratch + [DMA((len(chunks), 7)), DMA((len(chunks), 2, ntm))]


def scatter_steps(ndp, ntm, items, sources, outs, scratch, partial=False):
    t, core, x, y, (to_core, to_x, to_y) = cube(ndp, ntm)
    _, across = peers_of(ndp, ntm)
    chunks = scatter_chunks(items)
    sems, z_sems = scratch[-2:]
    steps = [[], [], [], [], []]
    for i, (item, start, place, size, cols) in enumerate(chunks):
        own, first, second, third, fourth = scratch[5 * i : 5 * i + 5]
        by_x = i % 2 == 0
        part = pl.ds(start, size)
        width = cols // ntm
        source = sources[item]
        one = [
            pltpu.make_async_copy(source.at[:, :, core, part], own, sems.at[i, 0]),
            sent(source.at[:, :, 1 - core, part], first, sems.at[i, 1], sems.at[i, 2], to_core),
        ]
        if by_x:
            two = [sent(own.at[:, 1 - x], second, sems.at[i, 3], sems.at[i, 4], to_x)]
            three = [sent(second.at[1 - y], third, sems.at[i, 5], sems.at[i, 6], to_y)]
        else:
            two = [sent(own.at[1 - y], second, sems.at[i, 3], sems.at[i, 4], to_y)]
            three = [sent(second.at[1 - x], third, sems.at[i, 5], sems.at[i, 6], to_x)]
        four = [
            sent(
                third.at[:, lanes(peer[1], width)], fourth.at[k], z_sems.at[i, 0, k],
                z_sems.at[i, 1, k], peer,
            )
            for k, peer in enumerate(across, 1)
        ]
        four.append(
            pltpu.make_async_copy(third.at[:, lanes(t, width)], fourth.at[0], z_sems.at[i, 0, 0])
        )

        def add_core(one=one, two=two, own=own, first=first):
            wait_all(one)

            def add(k):
                own[k // 2, lax.rem(k, 2)] += first[k // 2, lax.rem(k, 2)]

            each(0, 4, add)
            start_all(two)

        def add_first(two=two, three=three, own=own, second=second, by_x=by_x):
            wait_all(two)

            def add(k):
                second[k] += own[k, x] if by_x else own[y, k]

            each(0, 2, add)
            start_all(three)

        def add_second(
            three=three, four=four, second=second, third=third, by_x=by_x, out=outs[item],
            place=place, size=size,
        ):
            wait_all(three)
            if partial:
                target, base, rows = out
                value = third[...] + second[y if by_x else x]
                tiles = value.shape[1] // ntm // GW
                for k in range(ntm):
                    for j in range(tiles):
                        at, lane = (base + j * rows + place, (k * tiles + j) * GW)
                        target[k, at : at + size] = value[:, lane : lane + GW]
                return
            third[...] += second[y if by_x else x]
            start_all(four)

        def add_last(four=four, fourth=fourth, out=outs[item], place=place, size=size):
            wait_all(four)
            total = fourth[0].astype(F32)
            for k in range(1, ntm):
                total = total + fourth[k].astype(F32)
            out[place : place + size] = total

        steps[0].append(functools.partial(start_all, one))
        adds = (add_core, add_first, add_second) + (() if partial else (add_last,))
        for k, step in enumerate(adds):
            steps[k + 1].append(step)
    return steps


def cubed(grad):
    return grad.reshape((2, 2, 2, grad.shape[0] // 8, grad.shape[1]))


LOCAL = "local"


def staged_kernel(ndp, ntm, steps, body, counts, marks, scale, items, at, *refs):
    n_in, n_source, n_carry, n_out, n_scratch, swaps = counts

    def take(count):
        nonlocal refs
        taken, refs = (refs[:count], refs[count:])
        return taken

    swap_tab = take(swaps)
    ins, sources, shards = (take(n_in), take(n_source), take(n_carry))
    outs = list(take(n_out))
    totals = take(swaps)
    scattered, gathered = (take(len(items)), take(n_carry))
    scratch = take(n_scratch)
    swap_refs = take(4 * swaps)
    lows, carry_sems = (take(n_carry), take(1 if n_carry else 0))
    scatter_refs = refs
    i = pl.program_id(0)
    last = steps - 1
    copies = []
    for k, (low, target) in enumerate(zip(lows, gathered)):
        copies += over_z(ntm, low, target, carry_sems[0].at[k])
    if marks is not None:
        outs.insert(marks, swap_refs[0])

    @pl.when(i == 0)
    def _():
        greet(ndp, ntm)

    tail = body(*ins, *outs, *scratch) or []
    groups = [[], [], [], [], []]
    if items:
        groups = scatter_steps(ndp, ntm, items, sources, scattered, scatter_refs)
    swap = [lambda: None] * 3
    if swaps:
        swap = swap_steps(ndp, ntm, scale, swap_tab[0], totals[0], *swap_refs)

    @pl.when(i == 0)
    def _():
        for shard, low in zip(shards, lows):
            low[...] = shard[...].astype(BF16)
        met(ndp, ntm)
        start_all(copies)
        run_steps(groups[0])

    for k in range(1, 4):
        if items and isinstance(at[k], int) and at[k] < last:

            @pl.when(i == at[k])
            def _(k=k):
                run_steps(groups[k])

    @pl.when(i == last)
    def _():
        for k in range(1, 4):
            if items and at[k] == last:
                run_steps(groups[k])
        for k, name in enumerate("abc"):
            swap[k]()
            if k < len(tail):
                tail[k]()
            for j in range(1, 5):
                if items and at[j] == name:
                    run_steps(groups[j])
        wait_all(copies)


def plain_kernel(steps, body, *refs):
    tail = body(*refs) or []

    @pl.when(pl.program_id(0) == steps - 1)
    def _():
        run_steps(tail)


def staged(
    name, ident, *, ndp, ntm, steps, body, ins, outs, scratch, cost, swap=None, items=(),
    sources=(), at=(0, 1, 2, 3, "c"), carry=(),
):
    arrays, specs = ([], [])
    if swap is not None:
        arrays.append(swap[0])
        specs.append(SCALARS)
    arrays += [array for array, _ in ins] + list(sources) + list(carry)
    specs += [spec for _, spec in ins] + [ANY] * len(sources)
    specs += [fixed(shard.shape) for shard in carry]
    marks = outs.index(LOCAL) if LOCAL in outs else None
    real = [out for out in outs if out is not LOCAL]
    out_shapes, out_specs = ([shape for shape, _ in real], [spec for _, spec in real])
    extra = []
    swaps, scale = (0, None)
    if swap is not None:
        swaps, scale = (1, swap[1])
        out_shapes.append(shaped(swap[2]))
        out_specs.append(fixed(swap[2]))
        extra += swap_scratch(ndp, ntm, swap[2])
    for _, rows, cols, _ in items:
        out_shapes.append(shaped((rows, cols // ntm)))
        out_specs.append(fixed((rows, cols // ntm)))
    for shard in carry:
        out_shapes.append(shaped((shard.shape[0], shard.shape[1] * ntm), BF16))
        out_specs.append(ANY)
        extra.append(VMEM(shard.shape, BF16))
    if carry:
        extra.append(DMA((len(carry), 3, ntm)))
    if items:
        extra += scatter_scratch(items, ntm)
    if not (swaps or items or carry):
        return pl.pallas_call(
            functools.partial(plain_kernel, steps, body),
            name=name,
            grid=(steps,),
            in_specs=specs,
            out_specs=out_specs,
            out_shape=out_shapes,
            scratch_shapes=list(scratch),
            cost_estimate=pl.CostEstimate(flops=1024, bytes_accessed=1024, transcendentals=0),
            compiler_params=pltpu.CompilerParams(vmem_limit_bytes=LIMIT),
        )(*arrays)
    counts = (len(ins), len(sources), len(carry), len(real), len(scratch), swaps)
    return pl.pallas_call(
        functools.partial(
            staged_kernel, ndp, ntm, steps, body, counts, marks, scale, tuple(items), at
        ),
        name=name,
        grid=(steps,),
        in_specs=specs,
        out_specs=out_specs,
        out_shape=out_shapes,
        scratch_shapes=list(scratch) + extra,
        cost_estimate=pl.CostEstimate(flops=1024, bytes_accessed=1024, transcendentals=0),
        compiler_params=pltpu.CompilerParams(
            vmem_limit_bytes=LIMIT, collective_id=ident, has_side_effects=True
        ),
    )(*arrays)


def in_one(tab, video, weight, pre, squares, stats):
    i = pl.program_id(0)

    @pl.when(i == 0)
    def _():
        stats[...] = jnp.zeros_like(stats)
        squares[...] = jnp.zeros_like(squares)

    source = video[0]
    value = nn(source, weight[...]) * tab[0, i]
    pre[0] = value
    merge(stats, value, tab, i)
    squares[...] += down(jnp.square(source.astype(F32))) * tab[0, i]


def column(shape):
    return lax.rem(lax.broadcasted_iota(jnp.int32, shape, 0), HW)


def spread_taps(store, low):
    value = low.astype(F32)
    place = column(value.shape)
    zeros = jnp.zeros((HW, 3 * GW), BF16)
    store[0:HW] = zeros
    store[HW + PIX : PIX + 2 * HW] = zeros
    before = jnp.where(place == 0, 0.0, pltpu.roll(value, 1, 0))
    after = jnp.where(place == HW - 1, 0.0, pltpu.roll(value, PIX - 1, 0))
    store[HW : HW + PIX, 0:GW] = before.astype(BF16)
    store[HW : HW + PIX, GW : 2 * GW] = low
    store[HW : HW + PIX, 2 * GW : 3 * GW] = after.astype(BF16)


def window(store, row):
    return store[row * HW : row * HW + PIX]


def neighbours(ntm):
    d, t = (lax.axis_index("dp"), lax.axis_index("tm"))
    return (t > 0, t < ntm - 1, (d, jnp.maximum(t - 1, 0)), (d, jnp.minimum(t + 1, ntm - 1)))


def rows_of(pieces):
    place = lax.broadcasted_iota(jnp.int32, (8, pieces[0].shape[1]), 0)
    result = jnp.zeros(place.shape, F32)
    for i, piece in enumerate(pieces):
        result = jnp.where(place == i, piece, result)
    return result


def chosen(rows, cols, shift, limit, skip):
    row = lax.broadcasted_iota(jnp.int32, (rows, cols), 0)
    source = lax.broadcasted_iota(jnp.int32, (rows, cols), 1) + shift
    source = jnp.where(source < limit, source, source + skip)
    return jnp.where(row == source, 1.0, 0.0).astype(BF16)


def tile_from_edges(weight, tile, edge, edge_wide):
    start = tile * GW
    block = start // edge
    offset = start - block * edge
    base = offset // GW * GW
    window_lanes = pl.ds(pl.multiple_of(block * edge_wide + base, GW), 2 * GW)
    pick = chosen(2 * GW, GW, offset - base, edge - base, edge_wide - edge)
    return nn(weight[:, window_lanes], pick).astype(BF16)


def edge_from_tiles(tiles, place, edge, edge_wide):
    block = place // (edge_wide // GW)
    start = block * edge + (place - block * (edge_wide // GW)) * GW
    tile = start // GW
    shift = start - tile * GW
    left = nn(tiles[tile], chosen(GW, GW, shift, 2 * GW, 0))
    right = nn(tiles[jnp.minimum(tile + 1, 26)], chosen(GW, GW, shift - GW, 2 * GW, 0))
    return (left + right).astype(BF16)


def mta_forward(
    ndp, ntm, fast, edge, swap_tab, tab, pre, stats, pair, reduce_low, conv_low, expand, bias,
    weight, taps, windows, later, *refs,
):
    carried = 2 if fast else 0
    shards, refs = (refs[:carried], refs[carried:])
    agg, stats_out, ext_out, blended, sigma, snext, pooled, kernels = refs[:8]
    gathered, refs = (refs[8 : 8 + carried], refs[8 + carried :])
    hidden, store, ext, kept, gates, s_own, s_send, s_recv, ssems, rsems = refs[:10]
    swap_refs, refs = (refs[10:14], refs[14:])
    stats_two = swap_refs[0]
    has_prev, has_next, prev, following = neighbours(ntm)
    greet(ndp, ntm)
    dp_steps = [[], [], [], [], []]
    if fast:
        z_sems, dp_sems = refs
        for k, size in enumerate((32, 128)):
            part = gather_steps(
                ndp, ntm, shards[k], gathered[k], ((0, size), (size, size)), z_sems.at[k],
                dp_sems.at[k],
            )
            dp_steps = [steps + more for steps, more in zip(dp_steps, part)]
    swap = swap_steps(ndp, ntm, PIX, swap_tab, stats_out, *swap_refs)

    def assemble(tile):
        if fast:
            value = tile_from_edges(weight, tile, edge, weight.shape[1] // ntm)
        else:
            value = weight[tile]
        row = lax.rem(tile, 9) // 3
        kernels[tile // 9, row, rows_at(lax.rem(tile, 3), GW)] = value

    each(0, 27, assemble)
    met(ndp, ntm)
    run_steps(dp_steps[0])

    def first(f, carry):
        z = unit(pre[f], stats) * pair[0:1] + pair[1:2]
        value = z * sigmoid(z)
        hidden[f] = value
        motion = nn(value.astype(BF16), reduce_low[...]).astype(BF16)
        s_own[f] = nn(windows[...], motion)
        return carry

    lax.fori_loop(0, T, first, 0)
    for clip in range(CLIPS):
        s_send[clip] = s_own[clip * SPAN]
    back = sent(s_send, s_recv, ssems.at[9, 0], rsems.at[9, 0], prev)

    @pl.when(has_prev)
    def _():
        back.start()

    run_steps(dp_steps[1])

    @pl.when(has_prev)
    def _():
        back.wait_send()

    @pl.when(has_next)
    def _():
        back.wait_recv()

    @pl.when(jnp.logical_not(has_next))
    def _():
        s_recv[...] = jnp.zeros_like(s_recv)

    for clip in range(CLIPS):
        snext[clip * SPAN] = s_own[clip * SPAN + 1]
        snext[clip * SPAN + 1] = s_recv[clip]
    total = -rows_of([s_own[f, 4:5] for f in range(T)])
    for tap in range(9):
        rows = rows_of([snext[f, tap : tap + 1] for f in range(T)])
        total = total + nn_exact(rows, conv_low[tap])
    mean = total * (later[...] * (1.0 / PIX))
    pooled[...] = mean
    level = sigmoid(nn_exact(mean, expand[...]) + bias[...])
    sigma[...] = level
    for f in range(T):
        gates[f] = 1.0 + level[f : f + 1]

    @pl.when(jnp.logical_not(has_prev))
    def _():
        for group in range(3):
            ext[group, :, 0] = jnp.zeros((CLIPS, PIX, GW), BF16)

    @pl.when(jnp.logical_not(has_next))
    def _():
        for group in range(3):
            ext[group, :, 3] = jnp.zeros((CLIPS, PIX, GW), BF16)

    def edges(group, clip):
        k = group * CLIPS + clip
        left = sent(ext.at[group, clip, 1], ext.at[group, clip, 3], ssems.at[k, 0], rsems.at[k, 0], prev)
        right = sent(
            ext.at[group, clip, 2], ext.at[group, clip, 0], ssems.at[k, 1], rsems.at[k, 1],
            following,
        )
        return left, right

    def offer(group, clip, first):
        here = lanes(group + 1, GW)

        def piece(step):
            f = clip * SPAN + step
            value = hidden[f, :, here] * gates[f, :, here]
            if not first:
                value = value + agg[f, :, lanes(group, GW)]
            value = value * tab[0, f]
            kept[lax.rem(group, 2), clip, step] = value
            ext[group, clip, step + 1] = value.astype(BF16)

        each(0, SPAN, piece)
        left, right = edges(group, clip)

        @pl.when(has_prev)
        def _():
            left.start()

        @pl.when(has_next)
        def _():
            right.start()

    def taken(group, clip):
        left, right = edges(group, clip)

        @pl.when(has_prev)
        def _():
            left.wait_send()
            right.wait_recv()

        @pl.when(has_next)
        def _():
            right.wait_send()
            left.wait_recv()

    def convolve(group, clip):
        row = [taps[group * 3 + k] for k in range(3)]

        def mix(step):
            f = clip * SPAN + step
            own = [kept[lax.rem(group, 2), clip, k] for k in range(SPAN)]
            line = [ext[group, clip, 0].astype(F32)] + own + [ext[group, clip, 3].astype(F32)]
            here = [jnp.where(step == 0, line[k], line[k + 1]) for k in range(3)]
            mixed = row[0] * here[0] + row[1] * here[1] + row[2] * here[2]
            value = mixed.astype(BF16)
            blended[group, f] = value
            spread_taps(store.at[step], value)
            result = nn(window(store.at[step], 0), kernels[group, 0])
            result += nn(window(store.at[step], 1), kernels[group, 1])
            result += nn(window(store.at[step], 2), kernels[group, 2])
            agg[f, :, lanes(group + 1, GW)] = result

        each(0, SPAN, mix)

    each(0, CLIPS, lambda clip: offer(0, clip, True))

    def base(f):
        agg[f, :, 0:GW] = hidden[f, :, 0:GW] * gates[f, :, 0:GW]

    each(0, T, base)

    def turn(n):
        group, clip = (n // CLIPS, lax.rem(n, CLIPS))
        taken(group, clip)
        convolve(group, clip)

        @pl.when(group < 2)
        def _():
            offer(group + 1, clip, False)

        for k in range(3):

            @pl.when(n == 3 * k + 2)
            def _(k=k):
                run_steps(dp_steps[2 + k])

    each(0, 3 * CLIPS, turn)
    ext_out[...] = ext[...]
    stats_two[...] = jnp.zeros_like(stats_two)
    each(0, T, lambda f: merge(stats_two, agg[f], tab, f))
    run_steps(swap)


def wide_forward(
    ndp, ntm, swap_tab, tab, agg, stats, pair, order, weight_out, video, wide_pair, weight_in,
    hidden_out, out_low, centred, slope, first_out, squares, wide_out, alpha_out,
    hidden, pre, first_sum, wide_stats, *swap_refs,
):
    s = pl.program_id(0)
    h, f = (lax.rem(s, 2 * T) // T, lax.rem(s, T))
    here = lanes(h, C // 2)
    mask = tab[0, f]
    alpha = swap_steps(ndp, ntm, PIX, swap_tab, alpha_out, *swap_refs[4:8])
    sums = swap_refs[4]

    def one(k):
        refs = [ref.at[k] for ref in swap_refs[0:4]]
        return swap_steps(ndp, ntm, PIX, swap_tab, wide_stats.at[k], *refs)

    @pl.when(s == 0)
    def _():
        greet(ndp, ntm)
        swap_refs[0][...] = jnp.zeros_like(swap_refs[0])
        sums[...] = jnp.zeros_like(sums)
        squares[...] = jnp.zeros_like(squares)

    @pl.when(s < T)
    def _():
        z = unit(agg[0], stats) * pair[0:1] + pair[1:2]
        value = nn(order[...], (z * sigmoid(z)).astype(BF16)).astype(BF16)
        hidden[f] = value
        hidden_out[0] = value

    @pl.when(s < 2 * T)
    def _():
        result = nn(hidden[f], weight_out[:, here])
        pre[h, f] = result
        merge(swap_refs[0].at[h], result, tab, f)

    @pl.when(s == 0)
    def _():
        met(ndp, ntm)

    for k in range(2):

        @pl.when(s == 2 * T + k * T)
        def _(k=k):
            one(k)[2]()
            wide_out[:, k * (C // 2) : (k + 1) * (C // 2)] = wide_stats[k]

    @pl.when(s >= 2 * T)
    def _():
        source = nn(order[...], video[0]) * mask
        scaled = unit(pre[h, f], wide_stats[h])
        gains = wide_pair[:, here]
        branch = scaled * gains[0:1] + gains[1:2]
        before = source + branch
        gate = sigmoid(before)
        value = before * gate
        low = value.astype(BF16)
        out_low[0] = low
        centred[0] = scaled.astype(BF16)
        slope[0] = (gate + value * (1.0 - gate)).astype(BF16)
        squares[h, 0:1] += down(jnp.square(branch)) * mask
        squares[h, 1:2] += down(jnp.square(value)) * mask
        part = nn(low, weight_in[rows_at(h, C // 2)])

        @pl.when(h == 0)
        def _():
            first_sum[f] = part

        @pl.when(h == 1)
        def _():
            total = first_sum[f] + part
            first_out[0] = total
            merge(sums, total, tab, f)

    for k in range(2):

        @pl.when(s == (k + 1) * T - 1)
        def _(k=k):
            one(k)[0]()

        @pl.when(s == (k + 1) * T + 3)
        def _(k=k):
            one(k)[1]()

    @pl.when(s == 4 * T - 1)
    def _():
        run_steps(alpha)


def shifted(piece, tap, backward=False):
    rows, cols = (tap // 3 == 0, tap % 3 == 0)
    side = HW // 2
    place = lax.broadcasted_iota(jnp.int32, piece.shape, 0)
    if rows:
        if backward:
            piece = jnp.where(place < QUARTER - side, pltpu.roll(piece, QUARTER - side, 0), 0.0)
        else:
            piece = jnp.where(place >= side, pltpu.roll(piece, side, 0), 0.0)
    if cols:
        col = lax.rem(place, side)
        if backward:
            piece = jnp.where(col < side - 1, pltpu.roll(piece, QUARTER - 1, 0), 0.0)
        else:
            piece = jnp.where(col > 0, pltpu.roll(piece, 1, 0), 0.0)
    return piece


def plane(tap):
    return (0 if tap // 3 == 1 else 2) + (0 if tap % 3 == 1 else 1)


def mid_two(tab, first, stats, pair, weight, taps_out, second, sums, store):
    t = pl.program_id(0)

    @pl.when(t == 0)
    def _():
        def frame(f, carry):
            z = unit(first[f], stats) * pair[0:1] + pair[1:2]
            value = z * sigmoid(z)
            for tap in range(9):
                at = plane(tap) * QUARTER
                piece = shifted(value[at : at + QUARTER], tap)
                store[tap, pl.ds(pl.multiple_of(f * QUARTER, QUARTER), QUARTER)] = piece.astype(BF16)
            return carry

        lax.fori_loop(0, T, frame, 0)

    left = store[t]
    taps_out[0] = left
    part = nn(left, weight[...])

    @pl.when(t == 0)
    def _():
        second[...] = part

    @pl.when(t > 0)
    def _():
        second[...] += part

    @pl.when(t == 8)
    def _():
        parts = [second[f * QUARTER : (f + 1) * QUARTER] for f in range(T)]
        mean, spread = whole_stats(parts, [tab[0, f] for f in range(T)], tab[3, 1])
        sums[0:1] = mean
        sums[1:2] = spread


def middle(
    ndp, ntm, swap_tab, tab, second, stats_mid, pair_mid, joined, even, pairs, cotangent,
    result, grad_weight, grad_projection, grad_even, grad_mid, squares, totals_out, beta_out,
    hidden, thirds, shorts, grads, stats_all, totals_all, hidden_sum,
    mains_all, sides_all, weight_store, projection_store, held, sems, *swap_refs,
):
    s = pl.program_id(0)
    steps = WIDE_STEPS
    j = lax.rem(s, steps)
    sums = swap_refs[8]
    beta = swap_steps(ndp, ntm, None, None, beta_out, *swap_refs[8:12])

    def one(k):
        refs = [ref.at[k] for ref in swap_refs[0:4]]
        return swap_steps(ndp, ntm, QUARTER, swap_tab, stats_all.at[k], *refs)

    def two(k):
        refs = [ref.at[k] for ref in swap_refs[4:8]]
        return swap_steps(ndp, ntm, None, None, totals_all.at[k], *refs)

    def load(k):
        return pltpu.make_async_copy(joined.at[:, k], held.at[k], sems.at[2, k])

    def projection(k):
        return held[k, :, 0 : C // 8].reshape(C, WIDE_TILE)

    def weight(k):
        return held[k, :, C // 8 :].reshape(M, WIDE_TILE)

    @pl.when(s == 0)
    def _():
        greet(ndp, ntm)
        each(0, steps, lambda k: load(k).start())
        z = unit(second[...], stats_mid) * pair_mid[0:1] + pair_mid[1:2]
        hidden[...] = (z * sigmoid(z)).astype(BF16)

    @pl.when(s < steps)
    def _():
        load(j).wait()
        third = nn(hidden[...], weight(j))
        short = nn(even[...].reshape(HALF_ROWS, C), projection(j))
        thirds[j] = third
        shorts[j] = short
        stats = swap_refs[0].at[j]
        stats[...] = jnp.zeros((4, WIDE_TILE), F32)

        def gather_stats(f):
            merge(stats.at[0:2], thirds[j, rows_at(f, QUARTER)], tab, f)
            merge(stats.at[2:4], shorts[j, rows_at(f, QUARTER)], tab, f)

        each(0, T, gather_stats)

    @pl.when(s == 0)
    def _():
        met(ndp, ntm)

    @pl.when(s < steps)
    def _():
        one(j)[0]()

    @pl.when((s >= steps) & (s < 2 * steps))
    def _():
        one(j)[2]()
        stats = stats_all[j]
        sums_two = swap_refs[4].at[j]
        sums_two[...] = jnp.zeros((4, WIDE_TILE), F32)
        squares[...] = jnp.zeros_like(squares)

        def frame(f):
            rows, mask = (rows_at(f, QUARTER), tab[0, f])
            main = unit(thirds[j, rows], stats[0:2])
            side = unit(shorts[j, rows], stats[2:4])
            branch = main * pairs[0:1] + pairs[1:2]
            before = branch + (side * pairs[2:3] + pairs[3:4])
            gate = sigmoid(before)
            value = before * gate
            masked = value * mask
            result[rows] = masked.astype(BF16)
            grad = (gate + value * (1.0 - gate)) * (cotangent[rows].astype(F32) * mask)
            grads[j, rows] = grad
            for k, part in enumerate((grad, grad * main, grad * side)):
                sums_two[k : k + 1] += down(part)
            squares[0:1] += down(jnp.square(branch) * mask)
            squares[1:2] += down(jnp.square(masked))

        each(0, T, frame)
        two(j)[0]()

    @pl.when(s >= 2 * steps)
    def _():
        two(j)[2]()
        totals = totals_all[j]
        totals_out[:, lanes(j, WIDE_TILE)] = totals
        stats = stats_all[j]
        side_totals = jnp.concatenate([totals[0:1], totals[2:3]], axis=0)

        def frame(f):
            rows, mask = (rows_at(f, QUARTER), tab[0, f])
            grad = grads[j, rows]
            main = unit(thirds[j, rows], stats[0:2])
            main = norm_back(grad, main, stats[0:2], pairs[0:2], totals[0:2], mask, tab[3, 3])
            mains_all[j, rows] = main.astype(BF16)
            side = unit(shorts[j, rows], stats[2:4])
            side = norm_back(grad, side, stats[2:4], pairs[2:4], side_totals, mask, tab[3, 3])
            sides_all[j, rows] = side.astype(BF16)

        each(0, T, frame)
        hidden_part = nt(mains_all[j], weight(j))
        even_part = nt(sides_all[j], projection(j))

        @pl.when(j == 0)
        def _():
            hidden_sum[...] = hidden_part
            grad_even[...] = even_part

        @pl.when(j > 0)
        def _():
            hidden_sum[...] += hidden_part
            grad_even[...] += even_part

    @pl.when((s >= 2) & (s < steps + 2))
    def _():
        one(s - 2)[1]()

    @pl.when((s >= steps + 2) & (s < 2 * steps + 2))
    def _():
        two(s - steps - 2)[1]()

    def stores(k):
        here = lanes(k, WIDE_TILE)
        return [
            pltpu.make_async_copy(
                projection_store.at[k], grad_projection.at[:, here], sems.at[0, k]
            ),
            pltpu.make_async_copy(weight_store.at[k], grad_weight.at[:, here], sems.at[1, k]),
        ]

    def product(k):
        source = even[...].reshape(HALF_ROWS, C)
        projection_store[k] = tn(source, sides_all[k]).astype(BF16)
        weight_store[k] = tn(hidden[...], mains_all[k]).astype(BF16)
        start_all(stores(k))

    @pl.when(s == 3 * steps - 1)
    def _():
        centred = unit(second[...], stats_mid)
        z = centred * pair_mid[0:1] + pair_mid[1:2]
        gate = sigmoid(z)
        grad = hidden_sum[...] * (gate + z * gate * (1.0 - gate))
        grad_mid[...] = grad
        sums[0:1] = down(grad)
        sums[1:2] = down(grad * centred)
        beta[0]()
        each(0, steps // 2, product)
        beta[1]()
        each(steps // 2, steps, product)
        beta[2]()
        each(0, steps, lambda k: wait_all(stores(k)))


def back_mid(
    tab, grads, second, stats, pair, totals, taps_in, weight, first, stats_a, pair_a,
    grad_weight, grad_first, sums, low, store, held, sem, partial_sum,
):
    t = pl.program_id(0)
    load = pltpu.make_async_copy(taps_in, held, sem)

    @pl.when(t == 0)
    def _():
        load.start()

        def normal(f):
            rows = rows_at(f, QUARTER)
            centred = unit(second[rows], stats)
            grad = norm_back(grads[rows], centred, stats, pair, totals, tab[0, f], tab[3, 3])
            low[rows] = grad.astype(BF16)

        each(0, T, normal)
        store[...] = jnp.zeros_like(store)

    partial_sum[...] = nt(low[...], weight[...])
    for tap in range(9):

        @pl.when(t == tap)
        def _(tap=tap):
            at = plane(tap) * QUARTER

            def put(f):
                piece = shifted(partial_sum[rows_at(f, QUARTER)], tap, True)
                store[f, at : at + QUARTER] += piece

            each(0, T, put)

    @pl.when(t == 8)
    def _():
        sums[...] = jnp.zeros_like(sums)

        def frame(f, carry):
            centred = unit(first[f], stats_a)
            z = centred * pair_a[0:1] + pair_a[1:2]
            gate = sigmoid(z)
            grad = store[f] * (gate + z * gate * (1.0 - gate))
            grad_first[f] = grad
            sums[0:1] += down(grad)
            sums[1:2] += down(grad * centred)
            return carry

        lax.fori_loop(0, T, frame, 0)

    def products(steps):
        def run():
            if steps[0] == 0:
                load.wait()

            def product(tap):
                grad_weight[:, lanes(tap, M)] = tn(held[tap], low[...]).astype(BF16)

            each(steps[0], steps[-1] + 1, product)

        return run

    return [products(range(5)), products(range(5, 9))]


def back_in_two(
    tab, grads, first, stats, pair, totals, out_low, weight, even, slope, centred,
    grad_weight, grad_before, sums, lows, held, sem,
):
    i = pl.program_id(0)
    load = pltpu.make_async_copy(out_low, held, sem)
    scaled = unit(first[0], stats)
    low = norm_back(grads[0], scaled, stats, pair, totals, tab[0, i], tab[3, 2]).astype(BF16)
    grad = nt(low, weight[...])
    lows[i] = low

    @pl.when(i == 0)
    def _():
        load.start()
        sums[...] = jnp.zeros_like(sums)

    grad = jnp.concatenate([grad[0:QUARTER] + even[...], grad[QUARTER:]], axis=0)
    grad = grad * slope[0].astype(F32)
    grad_before[0] = grad.astype(BF16)
    sums[0:1] += down(grad)
    sums[1:2] += down(grad * centred[0].astype(F32))

    def products(steps):
        def run():
            if steps[0] == 0:
                load.wait()

            def product(k):
                source = held[:, :, lanes(k, WIDE_TILE)].reshape(ROWS, WIDE_TILE)
                value = tn(source, lows[...].reshape(ROWS, M))
                grad_weight[rows_at(k, WIDE_TILE)] = value.astype(BF16)

            each(steps[0], steps[-1] + 1, product)

        return run

    half = WIDE_STEPS // 2
    return [products(range(half)), products(range(half, WIDE_STEPS))]


def back_out_one(
    tab, grads, centred, stats, pair, totals, hidden, weight, order, agg, stats_two, pair_two,
    grad_weight, grad_two, sums, lows, held, sem,
):
    i = pl.program_id(0)
    load = pltpu.make_async_copy(hidden, held, sem)
    low = norm_back(
        grads[0].astype(F32), centred[0].astype(F32), stats, pair, totals, tab[0, i], tab[3, 2]
    ).astype(BF16)
    grad = nt(low, weight[...])
    lows[i] = low

    @pl.when(i == 0)
    def _():
        load.start()
        sums[...] = jnp.zeros_like(sums)

    high = grad.astype(BF16)
    rest = (grad - high.astype(F32)).astype(BF16)
    grad = tn(order[...], high) + tn(order[...], rest)
    scaled = unit(agg[0], stats_two)
    z = scaled * pair_two[0:1] + pair_two[1:2]
    gate = sigmoid(z)
    grad = grad * (gate + z * gate * (1.0 - gate))
    grad_two[0] = grad
    sums[0:1] += down(grad)
    sums[1:2] += down(grad * scaled)

    def products(steps):
        def run():
            if steps[0] == 0:
                load.wait()

            def product(k):
                here = lanes(k, WIDE_TILE)
                source = lows[:, :, here].reshape(ROWS, WIDE_TILE)
                grad_weight[:, here] = tn(held[...].reshape(ROWS, M), source).astype(BF16)

            each(steps[0], steps[-1] + 1, product)

        return run

    half = WIDE_STEPS // 2
    return [products(range(half)), products(range(half, WIDE_STEPS))]


def mta_backward(
    ndp, ntm, items, edge, tab, grads_in, agg_in, stats_two, pair_two, totals, pre_in, stats, pair,
    sigma, ext_in, blended_in, kernels_in, taps, reduce_low, conv_low, expand, windows, later,
    snext, pooled, *refs,
):
    count = len(items)
    sources, refs = (refs[:count], refs[count:])
    grad_one, totals_out, grad_mta, grad_reduce, grad_conv, grad_expand, grad_bias = refs[:7]
    grad_taps, refs = (refs[7], refs[8:])
    outs = []
    if count:
        base = 0
        for _, rows, cols, _ in items:
            outs.append((refs[0], base, rows))
            base += rows * (cols // ntm // GW)
        refs = refs[1:]
    mixed, low_store, store, back, parts, edge_send, edge_recv, mta_sum = refs[:8]
    k_store, k_send, k_recv, gate_sum, ssems, rsems, tiles, tap_sum, spreads, changes = refs[8:18]
    grads, agg, pre, ext, blended, kernels, hiddens, slopes, load_sems = refs[18:27]
    swap_refs, refs = (refs[27:31], refs[31:])
    sums = swap_refs[0]
    loads = [
        pltpu.make_async_copy(source, target, load_sems.at[k])
        for k, (source, target) in enumerate(
            (
                (grads_in, grads), (agg_in, agg), (kernels_in, kernels), (ext_in, ext),
                (blended_in, blended), (pre_in, pre),
            )
        )
    ]
    start_all(loads)
    has_prev, has_next, prev, following = neighbours(ntm)
    greet(ndp, ntm)
    swap = swap_steps(ndp, ntm, None, None, totals_out, *swap_refs)
    steps = [[], [], [], [], []]
    if count:
        steps = scatter_steps(ndp, ntm, items, sources, outs, refs, True)

    def start(group):
        here = slice(group * GW, (group + 1) * GW)

        def frame(f):
            centred = (agg[f, :, here] - stats_two[0:1, here]) * stats_two[1:2, here]
            total, cross = (totals[0:1, here] * tab[3, 2], totals[1:2, here] * tab[3, 2])
            scale = pair_two[0:1, here] * stats_two[1:2, here]
            mixed[f, :, here] = scale * (
                grads[f, :, here] - tab[0, f] * (total + centred * cross)
            )

        each(0, T, frame)

    def activate(f):
        z = unit(pre[f], stats) * pair[0:1] + pair[1:2]
        gate = sigmoid(z)
        value = z * gate
        hiddens[f] = value
        slopes[f] = gate + value * (1.0 - gate)

    met(ndp, ntm)
    run_steps(steps[0])
    wait_all(loads[0:2])
    start(3)
    wait_all(loads[2:5])
    run_steps(steps[1][0:2])

    @pl.when(jnp.logical_not(has_prev))
    def _():
        edge_recv[:, :, 0] = jnp.zeros((3, CLIPS, PIX, GW), BF16)

    @pl.when(jnp.logical_not(has_next))
    def _():
        edge_recv[:, :, 1] = jnp.zeros((3, CLIPS, PIX, GW), BF16)

    tap_sum[...] = jnp.zeros_like(tap_sum)

    def edges(group, clip):
        k = group * CLIPS + clip
        left = sent(
            edge_send.at[group, clip, 0], edge_recv.at[group, clip, 1], ssems.at[k, 0],
            rsems.at[k, 0], prev,
        )
        right = sent(
            edge_send.at[group, clip, 1], edge_recv.at[group, clip, 0], ssems.at[k, 1],
            rsems.at[k, 1], following,
        )
        return left, right

    def convolve(group, clip):
        row = [taps[group * 3 + k] for k in range(3)]
        rest = jnp.where(group < 2, 1.0, 0.0)

        def part(step):
            f = clip * SPAN + step
            value = mixed[f, :, lanes(group + 1, GW)]
            value = value + rest * mixed[f, :, lanes(jnp.minimum(group + 2, 3), GW)]
            value = value.astype(BF16)
            low_store[f] = value
            spread_taps(store.at[step], value)
            result = jnp.zeros((PIX, GW), F32)
            for tap in range(9):
                other = 8 - tap
                patch = store[
                    step,
                    (tap // 3) * HW : (tap // 3) * HW + PIX,
                    (tap % 3) * GW : (tap % 3 + 1) * GW,
                ]
                at = other % 3 * GW
                result += nt(patch, kernels[group, other // 3, at : at + GW])
            for k in range(3):
                source = ext[group, clip, step + k].astype(F32)
                tap_sum[group * 3 + k] += down(result * source)
            parts[step] = result

        each(0, SPAN, part)
        edge_send[group, clip, 0] = (row[0] * parts[0]).astype(BF16)
        edge_send[group, clip, 1] = (row[2] * parts[1]).astype(BF16)
        left, right = edges(group, clip)

        @pl.when(has_prev)
        def _():
            left.start()

        @pl.when(has_next)
        def _():
            right.start()

        back[clip, 0] = row[1] * parts[0] + row[0] * parts[1]
        back[clip, 1] = row[2] * parts[0] + row[1] * parts[1]

    def products(group, clip):
        def product(step):
            f = clip * SPAN + step
            spread_taps(store.at[step], blended[group, f])
            for k in range(3):
                mta_sum[k] += tn(window(store.at[step], k), low_store[f])

        each(0, SPAN, product)

    def collect(group, clip):
        left, right = edges(group, clip)

        @pl.when(has_prev)
        def _():
            left.wait_send()
            right.wait_recv()

        @pl.when(has_next)
        def _():
            right.wait_send()
            left.wait_recv()

        def put(step):
            f = clip * SPAN + step
            total = back[clip, step] + edge_recv[group, clip, step].astype(F32)
            mixed[f, :, lanes(group + 1, GW)] = total * tab[0, f]

        each(0, SPAN, put)

    moments = {
        0: steps[1][2:5], 1: steps[1][5:], 4: steps[2][0:2], 6: steps[2][2:5], 7: steps[2][5:],
    }

    def turn(n):
        group, clip = (2 - n // CLIPS, lax.rem(n, CLIPS))

        @pl.when(n >= CLIPS)
        def _():
            collect(group + 1, clip)

        convolve(group, clip)

        @pl.when(clip == 0)
        def _():
            mta_sum[...] = jnp.zeros_like(mta_sum)

        products(group, clip)

        @pl.when(clip == CLIPS - 1)
        def _():
            for tap in range(9):
                at = tap % 3 * GW
                tiles[group * 9 + tap] = mta_sum[tap // 3, at : at + GW].astype(BF16)

        for k in range(3):

            @pl.when(n == k)
            def _(k=k):
                start(2 - k)

        @pl.when(n == CLIPS)
        def _():
            loads[5].wait()

        @pl.when(n >= CLIPS)
        def _():
            activate(n - CLIPS)

        for k, moment in moments.items():
            if moment:

                @pl.when(n == k)
                def _(moment=moment):
                    run_steps(moment)

    each(0, 3 * CLIPS, turn)
    each(0, CLIPS, lambda clip: collect(0, clip))
    for k in range(9):
        grad_taps[k : k + 1] = tap_sum[k]

    def gates(f):
        gate_sum[f] = down(mixed[f] * hiddens[f])

    each(0, T, gates)
    gate = sigma[...]
    excite = rows_of([gate_sum[f] for f in range(T)]) * gate * (1.0 - gate)
    grad_bias[...] = down(excite)
    grad_expand[...] = tn_exact(pooled[...], excite)
    change = nt_exact(excite, expand[...]) * (later[...] * (1.0 / PIX))
    change_low = change.astype(BF16)
    change_wide = change_low.astype(F32)
    for tap in range(9):
        rows = rows_of([snext[f, tap : tap + 1] for f in range(T)])
        grad_conv[tap] = tn_exact(rows, change_wide)[0:R]
        k_store[tap] = nt(change_low, conv_low[tap].astype(BF16))
    index = lax.broadcasted_iota(jnp.int32, (16, GW), 0)

    def stacked(f):
        result = jnp.zeros((16, GW), F32)
        for tap in range(9):
            result = jnp.where(index == tap, k_store[tap, f : f + 1], result)
        return result

    for clip in range(CLIPS):
        k_send[clip] = stacked(clip * SPAN + 1)
    onward = sent(k_send, k_recv, ssems.at[9, 0], rsems.at[9, 0], following)

    @pl.when(has_next)
    def _():
        onward.start()
        onward.wait_send()

    @pl.when(has_prev)
    def _():
        onward.wait_recv()

    @pl.when(jnp.logical_not(has_prev))
    def _():
        k_recv[...] = jnp.zeros_like(k_recv)

    sums[...] = jnp.zeros_like(sums)
    grad_reduce[...] = jnp.zeros_like(grad_reduce)
    for f in range(T):
        spreads[f] = k_recv[f // SPAN] if f % SPAN == 0 else stacked(f - 1)
        changes[f] = change[f : f + 1]
        gate_sum[f] = 1.0 + gate[f : f + 1]

    def finish_frame(f):
        motion = tn_exact(windows[...].astype(F32), spreads[f]) - changes[f]
        motion_low = motion.astype(BF16)
        grad_reduce[...] += tn(motion_low, hiddens[f].astype(BF16))[0:R]
        grad = mixed[f] * gate_sum[f] + nt(motion_low, reduce_low[...])
        grad = grad * slopes[f]
        grad_one[f] = grad
        sums[0:1] += down(grad)
        sums[1:2] += down(grad * unit(pre[f], stats))

    each(0, T, finish_frame)
    swap[0]()
    if edge:

        def assemble(place):
            grad_mta[:, lanes(place, GW)] = edge_from_tiles(
                tiles, place, edge, grad_mta.shape[1] // ntm
            )

        each(0, grad_mta.shape[1] // GW, assemble)
    else:
        grad_mta[...] = tiles[...]
    swap[1]()
    run_steps(steps[3])
    swap[2]()


def back_in_one(
    tab, grads, pre, stats, pair, totals, video, weight, order, grad_before,
    grad_weight, grad_video, lows, held, sem,
):
    i = pl.program_id(0)
    load = pltpu.make_async_copy(video, held, sem)
    centred = unit(pre[0], stats)
    low = norm_back(grads[0], centred, stats, pair, totals, tab[0, i], tab[3, 2]).astype(BF16)
    lows[i] = low

    @pl.when(i == 0)
    def _():
        load.start()

    grad = nt(low, weight[...]) + tn(order[...], grad_before[0])
    grad_video[0] = (grad * tab[0, i]).astype(BF16)

    def products(steps):
        def run():
            if steps[0] == 0:
                load.wait()

            def product(k):
                source = held[:, :, lanes(k, WIDE_TILE)].reshape(ROWS, WIDE_TILE)
                value = tn(source, lows[...].reshape(ROWS, M))
                grad_weight[rows_at(k, WIDE_TILE)] = value.astype(BF16)

            each(steps[0], steps[-1] + 1, product)

        return run

    half = WIDE_STEPS // 2
    return [products(range(half)), products(range(half, WIDE_STEPS))]


def pack_sums(packed, reduce, expand, conv, bias, taps, source, one, last):
    packed[...] = jnp.zeros_like(packed)
    for k in range(M // GW):
        part = slice(k * GW, (k + 1) * GW)
        packed[k * R : (k + 1) * R] = reduce[:, part]
        packed[128 + k * R : 128 + (k + 1) * R] = expand[0:R, part]
        packed[352 + k : 353 + k] = bias[:, part]
    for group in range(3):
        value = conv[4 * group]
        for k in range(1, min(4, 9 - 4 * group)):
            value = value + pltpu.roll(conv[4 * group + k], k * R, 1)
        packed[256 + group * R : 256 + (group + 1) * R] = value
    packed[360:369] = taps[...]
    lane = lax.broadcasted_iota(jnp.int32, (1, GW), 1)
    row = jnp.zeros((1, GW), F32)
    pieces = (
        source[0:1], one[0, 0:1] + one[1, 0:1], one[0, 1:2] + one[1, 1:2], last[0:1], last[1:2],
    )
    for k, value in enumerate(pieces):
        row = jnp.where(lane == k, jnp.sum(value, axis=1, keepdims=True), row)
    packed[376:377] = row


def unpack_sums(summed, reduce, expand, conv, bias, taps, squares):
    for k in range(M // GW):
        part = slice(k * GW, (k + 1) * GW)
        reduce[:, part] = summed[k * R : (k + 1) * R]
        expand[:, part] = summed[128 + k * R : 128 + (k + 1) * R]
        bias[:, part] = summed[352 + k : 353 + k]
    for tap in range(9):
        group, k = divmod(tap, 4)
        value = summed[256 + group * R : 256 + (group + 1) * R]
        conv[tap] = value if k == 0 else pltpu.roll(value, GW - k * R, 1)
    taps[...] = summed[360:369]
    squares[...] = summed[376:384]


def final_sums(ndp, ntm, *refs):
    ins, outs = (refs[:8], refs[8:14])
    packed, summed, first, second, sems = refs[14:]
    greet(ndp, ntm)
    pack_sums(packed, *ins)
    met(ndp, ntm)
    run_steps(all_sums_steps(ndp, ntm, packed, summed, first, second, sems))
    unpack_sums(summed, *outs)


def last_part(ndp, ntm, items, own_items, *refs):
    tab, grads, pre, stats, pair, totals, video, weight, order, grad_before = refs[:10]
    small_ins, refs = (refs[10:18], refs[18:])
    sources, refs = (refs[: len(items)], refs[len(items) :])
    grad_video, small_outs, refs = (refs[0], refs[1:7], refs[7:])
    outs, refs = (refs[: len(items)], refs[len(items) :])
    own_out, refs = (refs[0], refs[1:])
    lows, held, sem, grad_weight, packed, summed, first, second, sems = refs[:9]
    count = 5 * len(scatter_chunks(items)) + 2
    i = pl.program_id(0)
    load = pltpu.make_async_copy(video, held, sem)
    large = scatter_steps(ndp, ntm, items, sources, outs, refs[9 : 9 + count])
    own = scatter_steps(ndp, ntm, own_items, [grad_weight], [own_out], refs[9 + count :])
    small = all_sums_steps(ndp, ntm, packed, summed, first, second, sems)

    @pl.when(i == 0)
    def _():
        greet(ndp, ntm)
        load.start()
        pack_sums(packed, *small_ins)
        met(ndp, ntm)
        run_steps(large[0])
        small[0]()

    @pl.when(i < T)
    def _():
        centred = unit(pre[0], stats)
        low = norm_back(grads[0], centred, stats, pair, totals, tab[0, i], tab[3, 2])
        lows[i] = low.astype(BF16)

    @pl.when(i == T - 1)
    def _():
        load.wait()
        small[1]()
        run_steps(large[1])

        def product(k):
            source = held[:, :, lanes(k, WIDE_TILE)].reshape(ROWS, WIDE_TILE)
            value = tn(source, lows[...].reshape(ROWS, M)).astype(BF16)
            grad_weight[k // 2, lax.rem(k, 2)] = value.reshape(2, C // 8, M)

        each(0, WIDE_STEPS, product)
        run_steps(own[0])

    @pl.when(i >= T)
    def _():
        grad = nt(lows[i - T], weight[...]) + tn(order[...], grad_before[0])
        grad_video[0] = (grad * tab[0, i - T]).astype(BF16)

    @pl.when(i == T)
    def _():
        small[2]()

    @pl.when(i == T + 2)
    def _():
        run_steps(own[1])

    @pl.when(i == T + 3)
    def _():
        run_steps(large[2])
        small[3]()

    @pl.when(i == 2 * T - 1)
    def _():
        run_steps(large[3])
        run_steps(own[2])
        small[4]()
        unpack_sums(summed, *small_outs)
        run_steps(large[4])
        run_steps(own[3])
        run_steps(own[4])


def wrap(
    fast, reduce, expand, conv, bias, taps, squares, swap, one, two, alpha, beta, three, last, *refs
):
    ins, refs = (refs[:6], refs[6:]) if fast else ((), refs)
    loads, stores = ([], [])
    if fast:
        *targets, held_one, held_two, sems = refs[-5:]
        refs = refs[:-5]
        for k, (source, target, held) in enumerate(
            zip(ins[4:6], targets, (held_one, held_two))
        ):
            size = source.shape[0] // T
            for j in range(T):
                part = pl.ds(j * size, size)
                loads.append(
                    pltpu.make_async_copy(source.at[part], held.at[part], sems.at[k, 0, j])
                )
                stores.append(
                    pltpu.make_async_copy(held.at[part], target.at[part], sems.at[k, 1, j])
                )
    start_all(loads)
    wrap_small(
        fast, reduce, expand, conv, bias, taps, squares, swap, one, two, alpha, beta, three,
        last, ins, refs,
    )
    for load, store in zip(loads, stores):
        load.wait()
        store.start()
    wait_all(stores)


def wrap_small(
    fast, reduce, expand, conv, bias, taps, squares, swap, one, two, alpha, beta, three, last, ins,
    refs,
):
    mid, wide, taps_out, reduce_out, conv_out, expand_out, bias_out, rms = refs[:8]
    for k, totals in enumerate((one, two, alpha, beta)):
        mid[k, 0:1] = totals[1:2]
        mid[k, 1:2] = totals[0:1]
    for k, (gain, shift) in enumerate(((three[1:2], three[0:1]), (last[1:2], last[0:1]))):
        wide[k, 0:1] = gain
        wide[k, 1:2] = shift
    wide[2, 0:1] = last[2:3]
    wide[2, 1:2] = last[0:1]
    for k in range(3):
        taps_out[k] = taps[3 * k : 3 * k + 3]
    reduce_out[...] = reduce[...]
    conv_out[...] = conv[:, :, 0:R]
    expand_out[...] = expand[...]
    bias_out[...] = bias[...]
    lane = lax.broadcasted_iota(jnp.int32, (1, GW), 1)
    total = swap[5:6]
    counts = jnp.where(lane < 3, total * PIX, total * QUARTER) * C
    rms[...] = jnp.sqrt(squares[0:1] / counts)[:, 0:5]
    if fast:
        mta, in1, projection, over = ins[:4]
        in1_out, mta_out, out1_out, in2_out, mid2_out, out2_out, proj_out = refs[8:15]
        in1_out[...] = in1[...]
        mta_out[...] = mta[:, 0 : mta_out.shape[1]]
        proj_out[...] = projection[...].astype(F32)
        at = 0
        for target in (mid2_out, in2_out, out2_out, out1_out):
            rows = target.shape[0]
            for k in range(target.shape[1] // GW):
                target[:, k * GW : (k + 1) * GW] = over[at : at + rows].astype(F32)
                at += rows


def parity_order():
    order = np.zeros((PIX, PIX), np.float32)
    for y in range(HW):
        for x in range(HW):
            row = ((y % 2) * 2 + x % 2) * QUARTER + (y // 2) * (HW // 2) + x // 2
            order[row, y * HW + x] = 1.0
    return order


def window_rows():
    rows = np.zeros((16, PIX), np.float32)
    for tap in range(9):
        for y in range(HW):
            for x in range(HW):
                inside = 0 <= y - (tap // 3 - 1) < HW and 0 <= x - (tap % 3 - 1) < HW
                rows[tap, y * HW + x] = float(inside)
    return rows


def fetch(shard):
    partly = lax.all_gather(shard.astype(BF16), "tm", axis=1, tiled=True)
    return lax.all_gather(partly, "dp", axis=0, tiled=True)


def deliver(gradient):
    partly = lax.psum_scatter(gradient, "dp", scatter_dimension=0, tiled=True)
    return lax.psum_scatter(partly, "tm", scatter_dimension=1, tiled=True).astype(F32)


def padded(values, rows, cols):
    return jnp.pad(values, ((0, rows - values.shape[0]), (0, cols - values.shape[1])))


def tables(lengths, ndp, ntm):
    d, t = (lax.axis_index("dp"), lax.axis_index("tm"))
    grouped = lengths.reshape(ndp, CLIPS)
    starts = jnp.arange(ntm, dtype=jnp.int32) * SPAN
    counts = jnp.sum(jnp.clip(grouped[:, :, None] - starts, 0, SPAN), axis=1).astype(F32)
    own = lax.dynamic_slice_in_dim(lengths, d * CLIPS, CLIPS)
    stamps = t * SPAN + jnp.arange(SPAN, dtype=jnp.int32)
    mask = (stamps[None, :] < own[:, None]).astype(F32).reshape(T)
    later = (stamps[None, :] + 1 < own[:, None]).astype(F32).reshape(T)
    total = jnp.sum(lengths).astype(F32)
    before = jnp.cumsum(mask) - mask
    held = jnp.maximum(before + mask, 1.0)
    local = jnp.maximum(jnp.sum(mask), 1.0)
    full, half = (1.0 / PIX, 1.0 / QUARTER)
    last = jnp.stack([full / local, half / local, full / total, half / total, total, total])
    tab = jnp.stack([mask, mask / held, before * mask / held, last])
    width = max(ndp, ntm)
    column = lax.dynamic_slice_in_dim(counts, t, 1, axis=1)[:, 0]
    sums = jnp.sum(counts, axis=0)

    def row(values):
        return jnp.pad(values, (0, width - values.shape[0]))

    swap = jnp.stack(
        [
            row(column / jnp.maximum(jnp.sum(column), 1.0)),
            row(column),
            row(sums / total),
            row(sums),
            jnp.broadcast_to(1.0 / total, (width,)),
        ]
    )
    return (tab, swap, later, total)


def local(
    video, lengths, mid_norms, wide_norms, taps, me_reduce, me_conv, me_expand, me_bias,
    w_in1, w_mta, w_out1, w_in2, w_mid2, w_out2, w_proj, grad_out,
):
    ndp, ntm = (lax.axis_size("dp"), lax.axis_size("tm"))
    fast = ndp == 8 and ntm == 4
    order = jnp.asarray(parity_order(), BF16)
    windows = jnp.asarray(window_rows(), BF16)
    frames = video.reshape(T, PIX, C)
    cotangent = grad_out.reshape(HALF_ROWS, C)
    bias = me_bias.reshape(1, M)
    tap_rows = taps.reshape(9, 1, GW)
    main_pairs = jnp.concatenate([wide_norms[1], wide_norms[2]], axis=0)
    stage = functools.partial(staged, ndp=ndp, ntm=ntm)

    def gathered(rows):
        return lax.all_gather(rows, "dp", axis=0, tiled=True)

    edge = w_mta.shape[1]
    edge_wide = -(-edge // GW) * GW
    small = (8, GW)
    if fast:
        shard_rows = [w_in1.shape, (w_mta.shape[0], edge_wide), w_out1.shape, w_mid2.shape]
        wide_rows = [(rows, cols * ntm) for rows, cols in shard_rows]
        (
            full_in1, full_mta, rows_out1, rows_mid2, pair, tab, swap, later, reduce_low,
            conv_low, expand,
        ) = remote_call(
            "first_gather", functools.partial(first_gather, ndp, ntm), 1,
            [SCALARS] + [WHOLE] * 9, [WHOLE] * 11,
            [shaped((4, 2) + shape, BF16) for shape in wide_rows[:2]]
            + [shaped(shape, BF16) for shape in wide_rows[2:]]
            + [
                shaped(((C + M) // 8, WIDE_TILE), BF16), shaped(small), shaped(small), shaped(small), shaped((M, GW), BF16),
                shaped((9, GW, GW)), shaped((GW, M)),
            ],
            [VMEM(shape, BF16) for shape in shard_rows] + [DMA((4, 4, 3, ntm)), DMA((2, 4, 4, 2))],
            1 << 24,
            lengths, w_in1, w_mta, w_out1, w_mid2, w_proj, w_out2, me_reduce.T, me_conv.reshape(9, R, R),
            me_expand,
        )
        full_in1 = full_in1.reshape(C, M)
        full_mta = full_mta.reshape(GW, ntm * edge_wide)
        full_mid2 = gathered(rows_mid2)
        joined = lax.all_gather(pair, ("dp", "tm"), axis=0, tiled=True)
    else:
        tab, swap, later, total = tables(lengths, ndp, ntm)
        later = jnp.broadcast_to(jnp.pad(later, (0, 2))[:, None], small)
        reduce_low = padded(me_reduce, M, GW).astype(BF16)
        conv_low = jnp.pad(me_conv.reshape(9, R, R), ((0, 0), (0, GW - R), (0, GW - R)))
        conv_low = conv_low.astype(BF16).astype(F32)
        expand = padded(me_expand, GW, M)
        full_in1, full_mta, full_out1, full_in2, full_mid2, full_out2, full_proj = [
            fetch(shard) for shard in (w_in1, w_mta, w_out1, w_in2, w_mid2, w_out2, w_proj)
        ]
        full_mta = jnp.transpose(full_mta.reshape(GW, 27, GW), (1, 0, 2))
        halves = [
            jnp.transpose(full.reshape(8, -1, WIDE_STEPS, WIDE_TILE), (0, 2, 1, 3))
            for full in (full_proj, full_out2)
        ]
        joined = jnp.concatenate(halves, axis=2)
    joined = joined.reshape(8, WIDE_STEPS, (C + M) // 8, WIDE_TILE)

    frame_wide, frame_mid = (at_first((1, PIX, C)), at_first((1, PIX, M)))
    pair_mid, pair_wide = (fixed((2, M)), fixed((2, C)))
    wide_low, mid_wide = (shaped((T, PIX, C), BF16), shaped((T, PIX, M)))
    even_spec = fixed((T, QUARTER, C))
    order_spec = fixed((PIX, PIX))
    half_mid = fixed((HALF_ROWS, M))
    ins_tab = (tab, SCALARS)
    mids = [(mid_norms[k], pair_mid) for k in range(4)]
    order_in = (order, order_spec)

    pre, squares_source, stats_one, *rows = stage(
        "in_one", 2, steps=T, body=in_one,
        ins=[ins_tab, (frames, frame_wide), (full_in1, fixed((C, M)))],
        outs=[(mid_wide, frame_mid), (shaped((1, C)), fixed((1, C))), LOCAL],
        scratch=[], cost=2 * ROWS * C * M, swap=(swap, PIX, (2, M)),
        carry=(w_in2,) if fast else (),
    )

    frame_low = (T, PIX, GW)
    carried = [rows_out1, *rows] if fast else []
    agg, stats_two, ext, blended, sigma, snext, pooled, kernels, *rows = remote_call(
        "mta_forward", functools.partial(mta_forward, ndp, ntm, fast, edge), 3,
        [SCALARS] * 2 + [WHOLE] * (11 + len(carried)),
        [WHOLE] * (8 + len(carried)),
        [
            mid_wide, shaped((2, M)), shaped((3, CLIPS, 4, PIX, GW), BF16),
            shaped((3,) + frame_low, BF16), shaped((8, M)), shaped((T, 16, GW)), shaped((8, GW)),
            shaped((3, 3, 3 * GW, GW), BF16),
        ]
        + [shaped((4, 2) + part.shape, BF16) for part in carried],
        [
            VMEM((T, PIX, M), F32), VMEM((SPAN, PIX + 2 * HW, 3 * GW), BF16),
            VMEM((3, CLIPS, 4, PIX, GW), BF16), VMEM((2, CLIPS, SPAN, PIX, GW), F32),
            VMEM((T, 1, M), F32), VMEM((T, 16, GW), F32), VMEM((CLIPS, 16, GW), F32),
            VMEM((CLIPS, 16, GW), F32), DMA((10, 2)), DMA((10, 2)),
        ]
        + swap_scratch(ndp, ntm, (2, M))
        + ([DMA((2, 2, 1, 1)), DMA((2, 4, 2, 2))] if fast else []),
        2 * ROWS * 9 * GW * GW * 3,
        swap, tab, pre, stats_one, mid_norms[0], reduce_low, conv_low, expand, bias, full_mta,
        tap_rows, windows, later, *carried,
    )
    if fast:
        full_out1, full_in2 = (rows[0].reshape(M, C), rows[1].reshape(C, M))

    half = C // 2

    def first_frames(i):
        return (jnp.minimum(i, T - 1), 0, 0)

    def half_frames(i):
        late = i >= 2 * T
        return (
            jnp.where(late, lax.rem(i, T), 0), 0, jnp.where(late, lax.rem(i, 2 * T) // T, 0),
        )

    def last_frames(i):
        return (jnp.where(i >= 3 * T, lax.rem(i, T), 0), 0, 0)

    half_wide = pl.BlockSpec((1, PIX, half), half_frames)
    half_sums = [
        VMEM((2, 2, half), F32), VMEM((2, ndp, 2, half), F32), VMEM((2, ntm, 2, half), F32),
        DMA((2, 4, max(ndp, ntm))),
    ]
    (
        hidden_two, out_low, centred_three, slope, first_two, squares_one, stats_three, stats_alpha,
    ) = pl.pallas_call(
        functools.partial(wide_forward, ndp, ntm),
        name="wide_forward",
        grid=(4 * T,),
        in_specs=[
            SCALARS, SCALARS, pl.BlockSpec((1, PIX, M), first_frames), pair_mid, pair_mid,
            order_spec, fixed((M, C)), half_wide, pair_wide, fixed((C, M)),
        ],
        out_specs=[
            pl.BlockSpec((1, PIX, M), first_frames), half_wide, half_wide, half_wide,
            pl.BlockSpec((1, PIX, M), last_frames), fixed((2, 2, half)), pair_wide, pair_mid,
        ],
        out_shape=[
            shaped((T, PIX, M), BF16), wide_low, wide_low, wide_low, mid_wide,
            shaped((2, 2, half)), shaped((2, C)), shaped((2, M)),
        ],
        scratch_shapes=[
            VMEM((T, PIX, M), BF16), VMEM((2, T, PIX, half), F32), VMEM((T, PIX, M), F32),
            VMEM((2, 2, half), F32),
        ]
        + half_sums
        + swap_scratch(ndp, ntm, (2, M)),
        cost_estimate=pl.CostEstimate(flops=1024, bytes_accessed=1024, transcendentals=0),
        compiler_params=pltpu.CompilerParams(
            vmem_limit_bytes=LIMIT, collective_id=4, has_side_effects=True
        ),
    )(
        swap, tab, agg, stats_two, mid_norms[1], order, full_out1, frames, wide_norms[0], full_in2,
    )

    stride_taps, second_two, stats_beta = stage(
        "mid_two", 6, steps=9, body=mid_two,
        ins=[
            ins_tab, (first_two, fixed((T, PIX, M))), (stats_alpha, pair_mid), mids[2],
            (full_mid2, at_last((M, M))),
        ],
        outs=[
            (shaped((9, HALF_ROWS, M), BF16), at_first((1, HALF_ROWS, M))),
            (shaped((HALF_ROWS, M)), half_mid), LOCAL,
        ],
        scratch=[VMEM((9, HALF_ROWS, M), BF16)], cost=2 * HALF_ROWS * 9 * M * M,
        swap=(swap, QUARTER, (2, M)),
    )

    tile = (HALF_ROWS, WIDE_TILE)
    steps = WIDE_STEPS

    def result_at(i):
        return jnp.clip(i - steps, 0, steps - 1)

    def pair_at(i):
        return jnp.where(i < steps, 0, lax.rem(i, steps))

    many = (steps, 4, WIDE_TILE)
    four_sums = [
        VMEM(many, F32), VMEM((steps, ndp, 4, WIDE_TILE), F32),
        VMEM((steps, ntm, 4, WIDE_TILE), F32), DMA((steps, 4, max(ndp, ntm))),
    ]
    result, grad_w_out2, grad_w_proj, grad_even, grad_beta, squares_last, totals_last, totals_beta = (
        pl.pallas_call(
            functools.partial(middle, ndp, ntm),
            name="middle",
            grid=(3 * steps,),
            in_specs=[
                SCALARS, SCALARS, half_mid, pair_mid, pair_mid,
                ANY, even_spec,
                pl.BlockSpec((4, WIDE_TILE), lambda i: (0, pair_at(i))),
                pl.BlockSpec(tile, lambda i: (0, result_at(i))),
            ],
            out_specs=[
                pl.BlockSpec(tile, lambda i: (0, result_at(i))), ANY, ANY, fixed((HALF_ROWS, C)),
                half_mid, pl.BlockSpec((2, WIDE_TILE), lambda i: (0, result_at(i))),
                fixed((4, C)), pair_mid,
            ],
            out_shape=[
                shaped((HALF_ROWS, C), BF16), shaped((M, C), BF16), shaped((C, C), BF16),
                shaped((HALF_ROWS, C)), shaped((HALF_ROWS, M)), shaped((2, C)), shaped((4, C)),
                shaped((2, M)),
            ],
            scratch_shapes=[
                VMEM((HALF_ROWS, M), BF16), VMEM((steps,) + tile, F32), VMEM((steps,) + tile, F32),
                VMEM((steps,) + tile, F32), VMEM(many, F32), VMEM(many, F32),
                VMEM((HALF_ROWS, M), F32), VMEM((steps,) + tile, BF16),
                VMEM((steps,) + tile, BF16), VMEM((steps, M, WIDE_TILE), BF16),
                VMEM((steps, C, WIDE_TILE), BF16), VMEM((steps, 8, (C + M) // 8, WIDE_TILE), BF16),
                DMA((3, steps)),
            ]
            + four_sums * 2
            + swap_scratch(ndp, ntm, (2, M)),
            cost_estimate=pl.CostEstimate(flops=1024, bytes_accessed=1024, transcendentals=0),
            compiler_params=pltpu.CompilerParams(
                vmem_limit_bytes=LIMIT, collective_id=7, has_side_effects=True
            ),
        )(
            swap, tab, second_two, stats_beta, mid_norms[3], joined, out_low, main_pairs, cotangent,
        )
    )
    if fast:
        proj_part = lax.psum_scatter(grad_w_proj, "dp", scatter_dimension=0, tiled=True)
        cube_out2 = cubed(grad_w_out2)

    def scattered(*pairs):
        if not fast:
            return {}
        return {"items": [item for item, _ in pairs], "sources": [source for _, source in pairs]}

    grad_w_mid2, grad_alpha, totals_alpha = stage(
        "back_mid", 10, steps=9, body=back_mid,
        ins=[
            ins_tab, (grad_beta, half_mid), (second_two, half_mid), (stats_beta, pair_mid),
            mids[3], (totals_beta, pair_mid), (stride_taps, ANY), (full_mid2, at_last((M, M))),
            (first_two, fixed((T, PIX, M))), (stats_alpha, pair_mid), mids[2],
        ],
        outs=[
            (shaped((M, 9 * M), BF16), fixed((M, 9 * M))), (mid_wide, fixed((T, PIX, M))), LOCAL,
        ],
        scratch=[
            VMEM((HALF_ROWS, M), BF16), VMEM((T, PIX, M), F32), VMEM((9, HALF_ROWS, M), BF16),
            DMA, VMEM((HALF_ROWS, M), F32),
        ],
        cost=4 * HALF_ROWS * 9 * M * M, swap=(swap, None, (2, M)),
    )
    cube_mid2 = cubed(grad_w_mid2) if fast else None

    grad_w_in2, grad_before_one, totals_three = stage(
        "back_in_two", 11, steps=T, body=back_in_two,
        ins=[
            ins_tab, (grad_alpha, frame_mid), (first_two, frame_mid), (stats_alpha, pair_mid),
            mids[2], (totals_alpha, pair_mid), (out_low, ANY), (full_in2, fixed((C, M))),
            (grad_even, at_first((QUARTER, C))), (slope, frame_wide), (centred_three, frame_wide),
        ],
        outs=[(shaped((C, M), BF16), fixed((C, M))), (wide_low, frame_wide), LOCAL],
        scratch=[VMEM((T, PIX, M), BF16), VMEM((T, PIX, C), BF16), DMA],
        cost=4 * ROWS * C * M, swap=(swap, None, (2, C)),
    )
    cube_in2 = cubed(grad_w_in2) if fast else None

    grad_w_out1, grad_two, totals_two = stage(
        "back_out_one", 12, steps=T, body=back_out_one,
        ins=[
            ins_tab, (grad_before_one, frame_wide), (centred_three, frame_wide),
            (stats_three, pair_wide), (wide_norms[0], pair_wide), (totals_three, pair_wide),
            (hidden_two, ANY), (full_out1, fixed((M, C))), order_in, (agg, frame_mid),
            (stats_two, pair_mid), mids[1],
        ],
        outs=[(shaped((M, C), BF16), fixed((M, C))), (mid_wide, frame_mid), LOCAL],
        scratch=[VMEM((T, PIX, C), BF16), VMEM((T, PIX, M), BF16), DMA],
        cost=4 * ROWS * C * M, swap=(swap, None, (2, M)),
    )
    cube_out1 = cubed(grad_w_out1) if fast else None

    early = {}
    if fast:
        totals_two, proj_part = lax.optimization_barrier((totals_two, proj_part))
        sent_proj = lax.psum_scatter(proj_part, "tm", scatter_dimension=1, tiled=True)
        early = scattered(
            ((0, 64, 9 * M, 2), cube_mid2), ((0, 256, M, 2), cube_in2),
            ((0, 64, C, 2), cube_out2), ((0, 64, C, 2), cube_out1),
        )
    items = early.get("items", [])
    z_rows = sum(rows * (cols // ntm // GW) for _, rows, cols, _ in items)
    mta_shape = (GW, ntm * edge_wide) if fast else (27, GW, GW)
    (
        grad_one, totals_one, grad_w_mta, grad_reduce, grad_conv, grad_expand, grad_bias, grad_taps,
        *sent_d,
    ) = remote_call(
        "mta_backward",
        functools.partial(mta_backward, ndp, ntm, items, edge if fast else None), 13,
        [SCALARS, ANY, ANY, WHOLE, WHOLE, WHOLE, ANY, WHOLE, WHOLE, WHOLE, ANY, ANY, ANY]
        + [WHOLE] * 8
        + [ANY] * len(items),
        [WHOLE] * (9 if items else 8),
        [
            mid_wide, shaped((2, M)), shaped(mta_shape, BF16), shaped((R, M)),
            shaped((9, R, GW)), shaped((GW, M)), shaped((1, M)), shaped((9, GW)),
        ]
        + ([shaped((ntm, z_rows, GW), BF16)] if items else []),
        [
            VMEM((T, PIX, M), F32), VMEM(frame_low, BF16),
            VMEM((SPAN, PIX + 2 * HW, 3 * GW), BF16), VMEM((CLIPS, SPAN, PIX, GW), F32),
            VMEM((SPAN, PIX, GW), F32),
            VMEM((3, CLIPS, 2, PIX, GW), BF16), VMEM((3, CLIPS, 2, PIX, GW), BF16),
            VMEM((3, 3 * GW, GW), F32), VMEM((9, 8, GW), F32), VMEM((CLIPS, 16, GW), F32),
            VMEM((CLIPS, 16, GW), F32), VMEM((T, 1, M), F32), DMA((10, 2)), DMA((10, 2)),
            VMEM((27, GW, GW), BF16), VMEM((9, 1, GW), F32), VMEM((T, 16, GW), F32),
            VMEM((T, 1, GW), F32), VMEM((T, PIX, M), F32), VMEM((T, PIX, M), F32),
            VMEM((T, PIX, M), F32), VMEM((3, CLIPS, 4, PIX, GW), BF16),
            VMEM((3,) + frame_low, BF16), VMEM((3, 3, 3 * GW, GW), BF16),
            VMEM((T, PIX, M), F32), VMEM((T, PIX, M), F32), DMA((6,)),
        ]
        + swap_scratch(ndp, ntm, (2, M))
        + (scatter_scratch(items, ntm) if items else []),
        4 * ROWS * 9 * GW * GW * 3,
        tab, grad_two, agg, stats_two, mid_norms[1], totals_two, pre, stats_one, mid_norms[0],
        sigma, ext, blended, kernels, tap_rows, reduce_low, conv_low, expand, windows, later,
        snext, pooled, *early.get("sources", []),
    )

    if fast:
        z_part = sent_d[0].reshape(ntm * z_rows, GW)
        sent_z = lax.psum_scatter(z_part, "tm", scatter_dimension=0, tiled=True)
    small_in = [
        grad_reduce, grad_expand, grad_conv, grad_bias, grad_taps, squares_source, squares_one,
        squares_last,
    ]
    small_out = [
        shaped((R, M)), shaped((R, M)), shaped((9, R, GW)), shaped((1, M)), shaped((9, GW)),
        shaped((8, GW)),
    ]
    unit_rows = 8 * ndp * ntm
    rows = -(-384 // unit_rows) * unit_rows
    small_scratch = [VMEM((rows, GW), F32)] * 2 + all_sums_scratch(ndp, ntm, rows)
    frame_scratch = [VMEM((T, PIX, M), BF16), VMEM((T, PIX, C), BF16), DMA]
    if fast:
        late = scattered(((0, 16, ntm * edge_wide, 1), cubed(grad_w_mta)))
        items, own_items = (late["items"], [(0, 256, M, 2)])

        def early_frame(shape):
            return pl.BlockSpec(shape, lambda i: (jnp.minimum(i, T - 1), 0, 0))

        def late_frame(shape):
            return pl.BlockSpec(shape, lambda i: (jnp.maximum(i - T, 0), 0, 0))

        grad_frames, *rest = pl.pallas_call(
            functools.partial(last_part, ndp, ntm, items, own_items),
            name="last_part",
            grid=(2 * T,),
            in_specs=[
                SCALARS, early_frame((1, PIX, M)), early_frame((1, PIX, M)), pair_mid, pair_mid,
                pair_mid, ANY, fixed((C, M)), order_spec, late_frame((1, PIX, C)),
            ]
            + [fixed(part.shape) for part in small_in]
            + [ANY] * len(items),
            out_specs=[late_frame((1, PIX, C))]
            + [fixed(part.shape) for part in small_out]
            + [fixed((rows_, cols // ntm)) for _, rows_, cols, _ in items + own_items],
            out_shape=[wide_low]
            + small_out
            + [shaped((rows_, cols // ntm)) for _, rows_, cols, _ in items + own_items],
            scratch_shapes=frame_scratch
            + [VMEM((2, 2, 2, C // 8, M), BF16)]
            + small_scratch
            + scatter_scratch(items, ntm)
            + scatter_scratch(own_items, ntm),
            cost_estimate=pl.CostEstimate(flops=1024, bytes_accessed=1024, transcendentals=0),
            compiler_params=pltpu.CompilerParams(
                vmem_limit_bytes=LIMIT, collective_id=14, has_side_effects=True
            ),
        )(
            tab, grad_one, pre, stats_one, mid_norms[0], totals_one, frames, full_in1, order,
            grad_before_one, *small_in, *late["sources"],
        )
        small_sums, sent_f = (rest[:6], rest[6:])
    else:
        grad_w_in1, grad_frames = stage(
            "back_in_one", 14, steps=T, body=back_in_one,
            ins=[
                ins_tab, (grad_one, frame_mid), (pre, frame_mid), (stats_one, pair_mid), mids[0],
                (totals_one, pair_mid), (frames, ANY), (full_in1, fixed((C, M))), order_in,
                (grad_before_one, frame_wide),
            ],
            outs=[(shaped((C, M), BF16), fixed((C, M))), (wide_low, frame_wide)],
            scratch=frame_scratch, cost=4 * ROWS * C * M,
        )
        small_sums = remote_call(
            "final_sums", functools.partial(final_sums, ndp, ntm), 15, [WHOLE] * 8, [WHOLE] * 6,
            small_out, small_scratch, 1 << 26, *small_in,
        )
    totals = (totals_one, totals_two, totals_alpha, totals_beta, totals_three, totals_last)
    if not fast:
        grad_w_mta = jnp.transpose(grad_w_mta, (1, 0, 2)).reshape(GW, 27 * GW)
        delivered = [
            deliver(g)
            for g in (
                grad_w_in1, grad_w_mta, grad_w_out1, grad_w_in2, grad_w_mid2, grad_w_out2,
                grad_w_proj,
            )
        ]
        swap = jnp.broadcast_to(total, (8, GW))
    wrapped = [*small_sums, swap, *totals]
    copied = []
    if fast:
        wrapped += [*sent_f, sent_proj, sent_z]
        copied = [result, grad_frames]
    shards = [
        shaped(shard.shape) for shard in (w_in1, w_mta, w_out1, w_in2, w_mid2, w_out2, w_proj)
    ]
    wrap_out = [
        shaped((4, 2, M)), shaped((3, 2, C)), shaped((3, 3, GW)), shaped((R, M)),
        shaped((9, R, R)), shaped((R, M)), shaped((1, M)), shaped((1, 5)),
    ]
    wrap_out += shards if fast else []
    (
        out_mid, out_wide, out_taps, out_reduce, out_conv, out_expand, out_bias, out_rms, *rest,
    ) = pl.pallas_call(
        functools.partial(wrap, fast),
        name="wrap",
        in_specs=[WHOLE] * len(wrapped) + [ANY] * len(copied),
        out_specs=[WHOLE] * len(wrap_out) + [ANY] * len(copied),
        out_shape=wrap_out + [shaped(part.shape, BF16) for part in copied],
        scratch_shapes=[VMEM(part.shape, BF16) for part in copied]
        + ([DMA((2, 2, T))] if fast else []),
        compiler_params=pltpu.CompilerParams(vmem_limit_bytes=LIMIT),
    )(*wrapped, *copied)
    if fast:
        *delivered, result, grad_frames = rest
    return (
        result.reshape(grad_out.shape),
        grad_frames.reshape(video.shape),
        out_mid,
        out_wide,
        out_taps,
        out_reduce.T,
        out_conv.reshape(3, 3, R, R),
        out_expand,
        out_bias.reshape(M),
        *delivered,
        out_rms.reshape(5),
    )


def solution(mesh):
    clip_spec = P("dp", "tm", None, None, None)
    return jax.shard_map(
        local,
        mesh=mesh,
        in_specs=(clip_spec,) + (P(),) * 8 + (P("dp", "tm"),) * 7 + (clip_spec,),
        out_specs=(clip_spec,) * 2 + (P(),) * 7 + (P("dp", "tm"),) * 7 + (P(),),
        check_vma=False,
    )
```

```python
import functools

import jax
import jax.numpy as jnp
import numpy as np
from jax import lax
from jax.experimental import pallas as pl
from jax.experimental.pallas import tpu as pltpu
from jax.sharding import PartitionSpec as P

C = 2048
M = 512
R = 32
GW = 128
HW = 16
PIX = HW * HW
QUARTER = PIX // 4
CLIPS = 3
SPAN = 2
T = CLIPS * SPAN
ROWS = T * PIX
HALF_ROWS = T * QUARTER
WIDE_TILE = 512
WIDE_STEPS = C // WIDE_TILE

EPSILON = 1e-05
HIGHEST = lax.Precision.HIGHEST
F32 = jnp.float32
BF16 = jnp.bfloat16
MESH = pl.DeviceIdType.MESH
VMEM = pltpu.VMEM
DMA = pltpu.SemaphoreType.DMA
LIMIT = 60 * 1024 * 1024

WHOLE = pl.BlockSpec(memory_space=pltpu.VMEM)
SCALARS = pl.BlockSpec(memory_space=pltpu.SMEM)
ANY = pl.BlockSpec(memory_space=pl.ANY)


def shaped(shape, dtype=F32):
    return jax.ShapeDtypeStruct(shape, dtype)


def fixed(shape):
    return pl.BlockSpec(shape, lambda i: (0,) * len(shape))


def at_first(shape):
    return pl.BlockSpec(shape, lambda i: (i,) + (0,) * (len(shape) - 1))


def at_last(shape):
    return pl.BlockSpec(shape, lambda i: (0,) * (len(shape) - 1) + (i,))


def remote_call(name, body, ident, in_specs, out_specs, out_shape, scratch, cost, *operands):
    return pl.pallas_call(
        body,
        name=name,
        in_specs=in_specs,
        out_specs=out_specs,
        out_shape=out_shape,
        scratch_shapes=scratch,
        cost_estimate=pl.CostEstimate(flops=1024, bytes_accessed=1024, transcendentals=0),
        compiler_params=pltpu.CompilerParams(
            vmem_limit_bytes=LIMIT, collective_id=ident, has_side_effects=True
        ),
    )(*operands)


def sigmoid(z):
    return 0.5 * jnp.tanh(0.5 * z) + 0.5


def nn(left, right):
    return jnp.dot(left, right, preferred_element_type=F32)


def nt(left, right):
    return lax.dot_general(left, right, (((1,), (1,)), ((), ())), preferred_element_type=F32)


def tn(left, right):
    return lax.dot_general(left, right, (((0,), (0,)), ((), ())), preferred_element_type=F32)


def nn_exact(left, right):
    return jnp.dot(left, right, precision=HIGHEST, preferred_element_type=F32)


def nt_exact(left, right):
    return lax.dot_general(
        left, right, (((1,), (1,)), ((), ())), precision=HIGHEST, preferred_element_type=F32
    )


def tn_exact(left, right):
    return lax.dot_general(
        left, right, (((0,), (0,)), ((), ())), precision=HIGHEST, preferred_element_type=F32
    )


def down(values):
    return jnp.sum(values, axis=0, keepdims=True)


def merge(stats, values, tab, i):
    rows = values.shape[0]
    mean = down(values) * (1.0 / rows)
    spread = down(jnp.square(values - mean))
    delta = mean - stats[0:1]
    stats[0:1] += delta * tab[1, i]
    stats[1:2] += spread * tab[0, i] + jnp.square(delta) * (tab[2, i] * rows)


def whole_stats(parts, masks, inv_count):
    mean = sum(down(part) * mask for part, mask in zip(parts, masks)) * inv_count
    spread = sum(down(jnp.square(part - mean)) * mask for part, mask in zip(parts, masks))
    return (mean, spread)


def unit(values, stats):
    return (values - stats[0:1]) * stats[1:2]


def norm_back(grads, centred, stats, pair, totals, mask, inv_count):
    total, cross = (totals[0:1] * inv_count, totals[1:2] * inv_count)
    return (pair[0:1] * stats[1:2]) * (grads - mask * (total + centred * cross))


def peers_of(ndp, ntm):
    d, t = (lax.axis_index("dp"), lax.axis_index("tm"))
    along = [(lax.rem(d + k, ndp), t) for k in range(1, ndp)]
    return along, [(d, lax.rem(t + k, ntm)) for k in range(1, ntm)]


def greet(ndp, ntm):
    along, across = peers_of(ndp, ntm)
    for peer in along + across:
        pl.semaphore_signal(
            pltpu.get_barrier_semaphore(), inc=1, device_id=peer, device_id_type=MESH
        )


def met(ndp, ntm):
    pl.semaphore_wait(pltpu.get_barrier_semaphore(), ndp + ntm - 2)


def sent(source, target, out_sem, in_sem, peer):
    return pltpu.make_async_remote_copy(source, target, out_sem, in_sem, peer, MESH)


def start_all(copies):
    for copy in copies:
        copy.start()


def wait_all(copies):
    for copy in copies:
        copy.wait()


def plain_gather(parts, row, tab):
    return sum(parts[1:], parts[0])


def plain_last(value, tab):
    return value


def spread_gather(scale, parts, row, tab):
    outputs = []
    for k in range(0, parts[0].shape[0], 2):
        means = [part[k : k + 1] for part in parts]
        mean = sum(value * tab[row, s] for s, value in enumerate(means))
        spread = sum(
            part[k + 1 : k + 2] + jnp.square(value - mean) * (tab[row + 1, s] * scale)
            for s, (part, value) in enumerate(zip(parts, means))
        )
        outputs.extend([mean, spread])
    return jnp.concatenate(outputs, axis=0)


def spread_last(scale, value, tab):
    outputs = []
    for k in range(0, value.shape[0], 2):
        outputs.append(value[k : k + 1])
        outputs.append(lax.rsqrt(value[k + 1 : k + 2] * (tab[4, 0] * (1.0 / scale)) + EPSILON))
    return jnp.concatenate(outputs, axis=0)


def swap_scratch(ndp, ntm, shape):
    return [
        VMEM(shape, F32), VMEM((ndp,) + shape, F32), VMEM((ntm,) + shape, F32),
        DMA((4, max(ndp, ntm))),
    ]


def swap_steps(ndp, ntm, scale, tab, out, source, first, second, sems):
    d, t = (lax.axis_index("dp"), lax.axis_index("tm"))
    along, across = peers_of(ndp, ntm)
    if scale is None:
        gather, last = (plain_gather, plain_last)
    else:
        gather = functools.partial(spread_gather, scale)
        last = functools.partial(spread_last, scale)

    def copies(buffer, peers, k):
        return [
            sent(buffer.at[0], buffer.at[j], sems.at[2 * k, j], sems.at[2 * k + 1, j], peer)
            for j, peer in enumerate(peers, 1)
        ]

    one, two = (copies(first, along, 0), copies(second, across, 1))

    def begin():
        first[0] = source[...]
        start_all(one)

    def middle():
        wait_all(one)
        second[0] = gather([first[lax.rem(d - s + ndp, ndp)] for s in range(ndp)], 0, tab)
        start_all(two)

    def end():
        wait_all(two)
        out[...] = last(
            gather([second[lax.rem(t - s + ntm, ntm)] for s in range(ntm)], 2, tab), tab
        )

    return (begin, middle, end)


def all_sums_scratch(ndp, ntm, rows):
    return [
        VMEM((ndp, rows // ndp, GW), F32), VMEM((ntm, rows // ndp // ntm, GW), F32),
        DMA((8, max(ndp, ntm))),
    ]


def all_sums_steps(ndp, ntm, source, out, first, second, sems):
    d, t = (lax.axis_index("dp"), lax.axis_index("tm"))
    large = source.shape[0] // ndp
    small = large // ntm
    along, across = peers_of(ndp, ntm)

    def rows(group, size):
        return pl.ds(pl.multiple_of(group * size, size), size)

    def copies(pieces, peers, k):
        return [
            sent(left, right, sems.at[2 * k, j], sems.at[2 * k + 1, j], peer)
            for j, ((left, right), peer) in enumerate(zip(pieces, peers), 1)
        ]

    own = out.at[pl.ds(pl.multiple_of(d * large + t * small, small), small)]
    block = out.at[rows(d, large)]
    one = copies(
        [(source.at[rows(peer[0], large)], first.at[k]) for k, peer in enumerate(along, 1)],
        along, 0,
    )
    two = copies(
        [(first.at[0, rows(peer[1], small)], second.at[k]) for k, peer in enumerate(across, 1)],
        across, 1,
    )
    three = copies([(own, own)] * (ntm - 1), across, 2)
    four = copies([(block, block)] * (ndp - 1), along, 3)

    def begin():
        start_all(one)

    def second_step():
        wait_all(one)
        first[0] = source[rows(d, large)]
        total = first[lax.rem(d, ndp)]
        for s in range(1, ndp):
            total = total + first[lax.rem(d - s + ndp, ndp)]
        first[0] = total
        start_all(two)

    def third_step():
        wait_all(two)
        second[0] = first[0, rows(t, small)]
        total = second[lax.rem(t, ntm)]
        for s in range(1, ntm):
            total = total + second[lax.rem(t - s + ntm, ntm)]
        own[...] = total
        start_all(three)

    def fourth_step():
        wait_all(three)
        start_all(four)

    def end():
        wait_all(four)

    return [begin, second_step, third_step, fourth_step, end]


def cube(ndp, ntm):
    d, t = (lax.axis_index("dp"), lax.axis_index("tm"))
    core, x, y = (lax.rem(d, 2), lax.rem(d // 2, 2), d // 4)
    peers = ((d + 1 - 2 * core, t), (d + 2 - 4 * x, t), (d + 4 - 8 * y, t))
    return (t, core, x, y, peers)


def lanes(group, width):
    return pl.ds(pl.multiple_of(group * width, GW), width)


def over_z(ntm, low, target, sems):
    d, t = (lax.axis_index("dp"), lax.axis_index("tm"))
    slot = target.at[:, lanes(t, low.shape[1])]
    copies = [pltpu.make_async_copy(low, slot, sems.at[2, 0])]
    for k in range(1, ntm):
        copies.append(sent(low, slot, sems.at[0, k], sems.at[1, k], (d, lax.rem(t + k, ntm))))
    return copies


def gather_steps(ndp, ntm, low, full, rows, z_sems, sems):
    t, core, x, y, (to_core, to_x, to_y) = cube(ndp, ntm)
    own = full.at[2 * y + x, core]
    zs, one, two, three = ([], [], [], [])
    for k, (start, size) in enumerate(rows):
        part = pl.ds(start, size)
        if low.shape[1] == full.shape[3]:
            zs.append([pltpu.make_async_copy(low.at[part], own.at[part], z_sems.at[k, 0, 0])])
        else:
            zs.append(over_z(ntm, low.at[part], own.at[part], z_sems.at[k]))
        first, second = (to_x, to_y) if k % 2 == 0 else (to_y, to_x)
        other = (y, 1 - x) if k % 2 == 0 else (1 - y, x)
        block = full.at[2 * y + x, core, part]
        one.append([sent(block, block, sems.at[0, k, 0], sems.at[0, k, 1], first)])
        pair = []
        for j, (row, col) in enumerate(((y, x), other), 1):
            block = full.at[2 * row + col, core, part]
            pair.append(sent(block, block, sems.at[j, k, 0], sems.at[j, k, 1], second))
        two.append(pair)
        block = full.at[:, core, part]
        three.append([sent(block, block, sems.at[3, k, 0], sems.at[3, k, 1], to_core)])
    count = len(rows)

    def after(waits, starts):
        wait_all(waits)
        start_all(starts)

    return [
        [functools.partial(start_all, zs[k]) for k in range(count)],
        [functools.partial(after, zs[k], one[k]) for k in range(count)],
        [functools.partial(after, one[k], two[k]) for k in range(count)],
        [functools.partial(after, two[k], three[k]) for k in range(count)],
        [functools.partial(after, three[k], []) for k in range(count)],
    ]


def each(start, stop, body):
    def step(k, carry):
        body(k)
        return carry

    lax.fori_loop(start, stop, step, 0)


def rows_at(group, size):
    return pl.ds(pl.multiple_of(group * size, size), size)


def run_steps(steps):
    for step in steps:
        step()


def lane_row(values):
    lane = lax.broadcasted_iota(jnp.int32, (1, GW), 1)
    row = jnp.zeros((1, GW), F32)
    for k, value in enumerate(values):
        row = jnp.where(lane == k, value, row)
    return row


def fill_tables(ndp, ntm, lengths, tab, swap, later):
    d, t = (lax.axis_index("dp"), lax.axis_index("tm"))
    held = [lengths[k] for k in range(ndp * CLIPS)]
    counts = [
        [
            sum(jnp.clip(held[i * CLIPS + c] - j * SPAN, 0, SPAN) for c in range(CLIPS))
            for i in range(ndp)
        ]
        for j in range(ntm)
    ]
    sums = [sum(column) for column in counts]
    total = sum(sums).astype(F32)
    column = [
        sum(jnp.where(t == j, counts[j][i], 0) for j in range(ntm)).astype(F32) for i in range(ndp)
    ]
    mask, after = ([], [])
    for c in range(CLIPS):
        own = lengths[d * CLIPS + c]
        for k in range(SPAN):
            mask.append(jnp.where(t * SPAN + k < own, 1.0, 0.0))
            after.append(jnp.where(t * SPAN + k + 1 < own, 1.0, 0.0))
    before = [sum(mask[:k], jnp.float32(0.0)) for k in range(T)]
    mask_row, before_row = (lane_row(mask), lane_row(before))
    share = 1.0 / jnp.maximum(before_row + mask_row, 1.0)
    tab[...] = jnp.zeros_like(tab)
    tab[0:1] = mask_row
    tab[1:2] = mask_row * share
    tab[2:3] = before_row * mask_row * share
    local = jnp.maximum(sum(mask), 1.0)
    ones = jnp.full((1, GW), 1.0, F32)
    rates = lane_row([1.0 / PIX, 1.0 / QUARTER, 1.0 / PIX, 1.0 / QUARTER, 1.0, 1.0])
    bases = lane_row([local, local, total, total, 1.0, 1.0])
    tab[3:4] = rates / jnp.maximum(bases, ones)
    swap[...] = jnp.zeros_like(swap)
    here = jnp.maximum(sum(column), 1.0)
    swap[0:1] = lane_row(column) / (here * ones)
    swap[1:2] = lane_row(column)
    swap[2:3] = lane_row([value.astype(F32) for value in sums]) / (total * ones)
    swap[3:4] = lane_row([value.astype(F32) for value in sums])
    swap[4:5] = ones / (total * ones)
    swap[5:6] = total * ones
    row = lax.broadcasted_iota(jnp.int32, (8, GW), 0)
    values = jnp.zeros((8, GW), F32)
    for k, value in enumerate(after):
        values = jnp.where(row == k, value, values)
    later[...] = values


def first_gather(
    ndp, ntm, lengths, in_shard, mta_shard, out_shard, mid_shard, proj_shard, last_shard, reduce,
    conv, expand, full_in, full_mta, out_rows, mid_rows, pair, tab, swap, later, reduce_low,
    conv_low, expand_wide,
    low_in, low_mta, low_out, low_mid, z_sems, sems,
):
    greet(ndp, ntm)
    low_in[...] = in_shard[...].astype(BF16)
    low_mta[...] = jnp.zeros_like(low_mta)
    low_mta[:, : mta_shard.shape[1]] = mta_shard[...].astype(BF16)
    low_out[...] = out_shard[...].astype(BF16)
    low_mid[...] = mid_shard[...].astype(BF16)
    chunks = [(k * 128, 128) for k in range(2)]
    one = gather_steps(ndp, ntm, low_in, full_in, chunks, z_sems.at[0], sems.at[0])
    two = gather_steps(ndp, ntm, low_mta, full_mta, ((0, 16),), z_sems.at[1], sems.at[1])
    copies = over_z(ntm, low_out, out_rows, z_sems.at[2, 0])
    copies += over_z(ntm, low_mid, mid_rows, z_sems.at[3, 0])
    met(ndp, ntm)
    run_steps(one[0])
    run_steps(two[0])
    start_all(copies)
    fill_tables(ndp, ntm, lengths, tab, swap, later)
    reduce_low[...] = jnp.zeros_like(reduce_low)
    reduce_low[:, 0:R] = reduce[...].T.astype(BF16)
    conv_low[...] = jnp.zeros_like(conv_low)
    conv_low[:, 0:R, 0:R] = conv[...].astype(BF16).astype(F32)
    expand_wide[...] = jnp.zeros_like(expand_wide)
    expand_wide[0:R] = expand[...]
    pair[0 : C // 8] = proj_shard[...].astype(BF16)
    pair[C // 8 :] = last_shard[...].astype(BF16)
    for k in range(1, 5):
        run_steps(one[k])
        run_steps(two[k])
    wait_all(copies)


def scatter_chunks(items):
    chunks = []
    for item, (base, rows, cols, parts) in enumerate(items):
        size = rows // parts
        for part in range(parts):
            chunks.append((item, base + part * size, part * size, size, cols))
    return chunks


def scatter_scratch(items, ntm):
    chunks = scatter_chunks(items)
    scratch = []
    for _, _, _, rows, cols in chunks:
        scratch += [
            VMEM((2, 2, rows, cols), BF16), VMEM((2, 2, rows, cols), BF16),
            VMEM((2, rows, cols), BF16), VMEM((rows, cols), BF16),
            VMEM((ntm, rows, cols // ntm), BF16),
        ]
    return scratch + [DMA((len(chunks), 7)), DMA((len(chunks), 2, ntm))]


def scatter_steps(ndp, ntm, items, sources, outs, scratch, partial=False):
    t, core, x, y, (to_core, to_x, to_y) = cube(ndp, ntm)
    _, across = peers_of(ndp, ntm)
    chunks = scatter_chunks(items)
    sems, z_sems = scratch[-2:]
    steps = [[], [], [], [], []]
    for i, (item, start, place, size, cols) in enumerate(chunks):
        own, first, second, third, fourth = scratch[5 * i : 5 * i + 5]
        by_x = i % 2 == 0
        part = pl.ds(start, size)
        width = cols // ntm
        source = sources[item]
        one = [
            pltpu.make_async_copy(source.at[:, :, core, part], own, sems.at[i, 0]),
            sent(source.at[:, :, 1 - core, part], first, sems.at[i, 1], sems.at[i, 2], to_core),
        ]
        if by_x:
            two = [sent(own.at[:, 1 - x], second, sems.at[i, 3], sems.at[i, 4], to_x)]
            three = [sent(second.at[1 - y], third, sems.at[i, 5], sems.at[i, 6], to_y)]
        else:
            two = [sent(own.at[1 - y], second, sems.at[i, 3], sems.at[i, 4], to_y)]
            three = [sent(second.at[1 - x], third, sems.at[i, 5], sems.at[i, 6], to_x)]
        four = [
            sent(
                third.at[:, lanes(peer[1], width)], fourth.at[k], z_sems.at[i, 0, k],
                z_sems.at[i, 1, k], peer,
            )
            for k, peer in enumerate(across, 1)
        ]
        four.append(
            pltpu.make_async_copy(third.at[:, lanes(t, width)], fourth.at[0], z_sems.at[i, 0, 0])
        )

        def add_core(one=one, two=two, own=own, first=first):
            wait_all(one)

            def add(k):
                own[k // 2, lax.rem(k, 2)] += first[k // 2, lax.rem(k, 2)]

            each(0, 4, add)
            start_all(two)

        def add_first(two=two, three=three, own=own, second=second, by_x=by_x):
            wait_all(two)

            def add(k):
                second[k] += own[k, x] if by_x else own[y, k]

            each(0, 2, add)
            start_all(three)

        def add_second(
            three=three, four=four, second=second, third=third, by_x=by_x, out=outs[item],
            place=place, size=size,
        ):
            wait_all(three)
            if partial:
                target, base, rows = out
                value = third[...] + second[y if by_x else x]
                tiles = value.shape[1] // ntm // GW
                for k in range(ntm):
                    for j in range(tiles):
                        at, lane = (base + j * rows + place, (k * tiles + j) * GW)
                        target[k, at : at + size] = value[:, lane : lane + GW]
                return
            third[...] += second[y if by_x else x]
            start_all(four)

        def add_last(four=four, fourth=fourth, out=outs[item], place=place, size=size):
            wait_all(four)
            total = fourth[0].astype(F32)
            for k in range(1, ntm):
                total = total + fourth[k].astype(F32)
            out[place : place + size] = total

        steps[0].append(functools.partial(start_all, one))
        adds = (add_core, add_first, add_second) + (() if partial else (add_last,))
        for k, step in enumerate(adds):
            steps[k + 1].append(step)
    return steps


def cubed(grad):
    return grad.reshape((2, 2, 2, grad.shape[0] // 8, grad.shape[1]))


LOCAL = "local"


def staged_kernel(ndp, ntm, steps, body, counts, marks, scale, items, at, *refs):
    n_in, n_source, n_carry, n_out, n_scratch, swaps = counts

    def take(count):
        nonlocal refs
        taken, refs = (refs[:count], refs[count:])
        return taken

    swap_tab = take(swaps)
    ins, sources, shards = (take(n_in), take(n_source), take(n_carry))
    outs = list(take(n_out))
    totals = take(swaps)
    scattered, gathered = (take(len(items)), take(n_carry))
    scratch = take(n_scratch)
    swap_refs = take(4 * swaps)
    lows, carry_sems = (take(n_carry), take(1 if n_carry else 0))
    scatter_refs = refs
    i = pl.program_id(0)
    last = steps - 1
    copies = []
    for k, (low, target) in enumerate(zip(lows, gathered)):
        copies += over_z(ntm, low, target, carry_sems[0].at[k])
    if marks is not None:
        outs.insert(marks, swap_refs[0])

    @pl.when(i == 0)
    def _():
        greet(ndp, ntm)

    tail = body(*ins, *outs, *scratch) or []
    groups = [[], [], [], [], []]
    if items:
        groups = scatter_steps(ndp, ntm, items, sources, scattered, scatter_refs)
    swap = [lambda: None] * 3
    if swaps:
        swap = swap_steps(ndp, ntm, scale, swap_tab[0], totals[0], *swap_refs)

    @pl.when(i == 0)
    def _():
        for shard, low in zip(shards, lows):
            low[...] = shard[...].astype(BF16)
        met(ndp, ntm)
        start_all(copies)
        run_steps(groups[0])

    for k in range(1, 4):
        if items and isinstance(at[k], int) and at[k] < last:

            @pl.when(i == at[k])
            def _(k=k):
                run_steps(groups[k])

    @pl.when(i == last)
    def _():
        for k in range(1, 4):
            if items and at[k] == last:
                run_steps(groups[k])
        for k, name in enumerate("abc"):
            swap[k]()
            if k < len(tail):
                tail[k]()
            for j in range(1, 5):
                if items and at[j] == name:
                    run_steps(groups[j])
        wait_all(copies)


def plain_kernel(steps, body, *refs):
    tail = body(*refs) or []

    @pl.when(pl.program_id(0) == steps - 1)
    def _():
        run_steps(tail)


def staged(
    name, ident, *, ndp, ntm, steps, body, ins, outs, scratch, cost, swap=None, items=(),
    sources=(), at=(0, 1, 2, 3, "c"), carry=(),
):
    arrays, specs = ([], [])
    if swap is not None:
        arrays.append(swap[0])
        specs.append(SCALARS)
    arrays += [array for array, _ in ins] + list(sources) + list(carry)
    specs += [spec for _, spec in ins] + [ANY] * len(sources)
    specs += [fixed(shard.shape) for shard in carry]
    marks = outs.index(LOCAL) if LOCAL in outs else None
    real = [out for out in outs if out is not LOCAL]
    out_shapes, out_specs = ([shape for shape, _ in real], [spec for _, spec in real])
    extra = []
    swaps, scale = (0, None)
    if swap is not None:
        swaps, scale = (1, swap[1])
        out_shapes.append(shaped(swap[2]))
        out_specs.append(fixed(swap[2]))
        extra += swap_scratch(ndp, ntm, swap[2])
    for _, rows, cols, _ in items:
        out_shapes.append(shaped((rows, cols // ntm)))
        out_specs.append(fixed((rows, cols // ntm)))
    for shard in carry:
        out_shapes.append(shaped((shard.shape[0], shard.shape[1] * ntm), BF16))
        out_specs.append(ANY)
        extra.append(VMEM(shard.shape, BF16))
    if carry:
        extra.append(DMA((len(carry), 3, ntm)))
    if items:
        extra += scatter_scratch(items, ntm)
    if not (swaps or items or carry):
        return pl.pallas_call(
            functools.partial(plain_kernel, steps, body),
            name=name,
            grid=(steps,),
            in_specs=specs,
            out_specs=out_specs,
            out_shape=out_shapes,
            scratch_shapes=list(scratch),
            cost_estimate=pl.CostEstimate(flops=1024, bytes_accessed=1024, transcendentals=0),
            compiler_params=pltpu.CompilerParams(vmem_limit_bytes=LIMIT),
        )(*arrays)
    counts = (len(ins), len(sources), len(carry), len(real), len(scratch), swaps)
    return pl.pallas_call(
        functools.partial(
            staged_kernel, ndp, ntm, steps, body, counts, marks, scale, tuple(items), at
        ),
        name=name,
        grid=(steps,),
        in_specs=specs,
        out_specs=out_specs,
        out_shape=out_shapes,
        scratch_shapes=list(scratch) + extra,
        cost_estimate=pl.CostEstimate(flops=1024, bytes_accessed=1024, transcendentals=0),
        compiler_params=pltpu.CompilerParams(
            vmem_limit_bytes=LIMIT, collective_id=ident, has_side_effects=True
        ),
    )(*arrays)


def in_one(tab, video, weight, pre, squares, stats):
    i = pl.program_id(0)

    @pl.when(i == 0)
    def _():
        stats[...] = jnp.zeros_like(stats)
        squares[...] = jnp.zeros_like(squares)

    source = video[0]
    value = nn(source, weight[...]) * tab[0, i]
    pre[0] = value
    merge(stats, value, tab, i)
    squares[...] += down(jnp.square(source.astype(F32))) * tab[0, i]


def column(shape):
    return lax.rem(lax.broadcasted_iota(jnp.int32, shape, 0), HW)


def spread_taps(store, low):
    value = low.astype(F32)
    place = column(value.shape)
    zeros = jnp.zeros((HW, 3 * GW), BF16)
    store[0:HW] = zeros
    store[HW + PIX : PIX + 2 * HW] = zeros
    before = jnp.where(place == 0, 0.0, pltpu.roll(value, 1, 0))
    after = jnp.where(place == HW - 1, 0.0, pltpu.roll(value, PIX - 1, 0))
    store[HW : HW + PIX, 0:GW] = before.astype(BF16)
    store[HW : HW + PIX, GW : 2 * GW] = low
    store[HW : HW + PIX, 2 * GW : 3 * GW] = after.astype(BF16)


def window(store, row):
    return store[row * HW : row * HW + PIX]


def neighbours(ntm):
    d, t = (lax.axis_index("dp"), lax.axis_index("tm"))
    return (t > 0, t < ntm - 1, (d, jnp.maximum(t - 1, 0)), (d, jnp.minimum(t + 1, ntm - 1)))


def rows_of(pieces):
    place = lax.broadcasted_iota(jnp.int32, (8, pieces[0].shape[1]), 0)
    result = jnp.zeros(place.shape, F32)
    for i, piece in enumerate(pieces):
        result = jnp.where(place == i, piece, result)
    return result


def chosen(rows, cols, shift, limit, skip):
    row = lax.broadcasted_iota(jnp.int32, (rows, cols), 0)
    source = lax.broadcasted_iota(jnp.int32, (rows, cols), 1) + shift
    source = jnp.where(source < limit, source, source + skip)
    return jnp.where(row == source, 1.0, 0.0).astype(BF16)


def tile_from_edges(weight, tile, edge, edge_wide):
    start = tile * GW
    block = start // edge
    offset = start - block * edge
    base = offset // GW * GW
    window_lanes = pl.ds(pl.multiple_of(block * edge_wide + base, GW), 2 * GW)
    pick = chosen(2 * GW, GW, offset - base, edge - base, edge_wide - edge)
    return nn(weight[:, window_lanes], pick).astype(BF16)


def edge_from_tiles(tiles, place, edge, edge_wide):
    block = place // (edge_wide // GW)
    start = block * edge + (place - block * (edge_wide // GW)) * GW
    tile = start // GW
    shift = start - tile * GW
    left = nn(tiles[tile], chosen(GW, GW, shift, 2 * GW, 0))
    right = nn(tiles[jnp.minimum(tile + 1, 26)], chosen(GW, GW, shift - GW, 2 * GW, 0))
    return (left + right).astype(BF16)


def mta_forward(
    ndp, ntm, fast, edge, swap_tab, tab, pre, stats, pair, reduce_low, conv_low, expand, bias,
    weight, taps, windows, later, *refs,
):
    carried = 2 if fast else 0
    shards, refs = (refs[:carried], refs[carried:])
    agg, stats_out, ext_out, blended, sigma, snext, pooled, kernels = refs[:8]
    gathered, refs = (refs[8 : 8 + carried], refs[8 + carried :])
    hidden, store, ext, kept, gates, s_own, s_send, s_recv, ssems, rsems = refs[:10]
    swap_refs, refs = (refs[10:14], refs[14:])
    stats_two = swap_refs[0]
    has_prev, has_next, prev, following = neighbours(ntm)
    greet(ndp, ntm)
    dp_steps = [[], [], [], [], []]
    if fast:
        z_sems, dp_sems = refs
        for k, size in enumerate((32, 128)):
            part = gather_steps(
                ndp, ntm, shards[k], gathered[k], ((0, size), (size, size)), z_sems.at[k],
                dp_sems.at[k],
            )
            dp_steps = [steps + more for steps, more in zip(dp_steps, part)]
    swap = swap_steps(ndp, ntm, PIX, swap_tab, stats_out, *swap_refs)

    def assemble(tile):
        if fast:
            value = tile_from_edges(weight, tile, edge, weight.shape[1] // ntm)
        else:
            value = weight[tile]
        row = lax.rem(tile, 9) // 3
        kernels[tile // 9, row, rows_at(lax.rem(tile, 3), GW)] = value

    each(0, 27, assemble)
    met(ndp, ntm)
    run_steps(dp_steps[0])

    def first(f, carry):
        z = unit(pre[f], stats) * pair[0:1] + pair[1:2]
        value = z * sigmoid(z)
        hidden[f] = value
        motion = nn(value.astype(BF16), reduce_low[...]).astype(BF16)
        s_own[f] = nn(windows[...], motion)
        return carry

    lax.fori_loop(0, T, first, 0)
    for clip in range(CLIPS):
        s_send[clip] = s_own[clip * SPAN]
    back = sent(s_send, s_recv, ssems.at[9, 0], rsems.at[9, 0], prev)

    @pl.when(has_prev)
    def _():
        back.start()

    run_steps(dp_steps[1])

    @pl.when(has_prev)
    def _():
        back.wait_send()

    @pl.when(has_next)
    def _():
        back.wait_recv()

    @pl.when(jnp.logical_not(has_next))
    def _():
        s_recv[...] = jnp.zeros_like(s_recv)

    for clip in range(CLIPS):
        snext[clip * SPAN] = s_own[clip * SPAN + 1]
        snext[clip * SPAN + 1] = s_recv[clip]
    total = -rows_of([s_own[f, 4:5] for f in range(T)])
    for tap in range(9):
        rows = rows_of([snext[f, tap : tap + 1] for f in range(T)])
        total = total + nn_exact(rows, conv_low[tap])
    mean = total * (later[...] * (1.0 / PIX))
    pooled[...] = mean
    level = sigmoid(nn_exact(mean, expand[...]) + bias[...])
    sigma[...] = level
    for f in range(T):
        gates[f] = 1.0 + level[f : f + 1]

    @pl.when(jnp.logical_not(has_prev))
    def _():
        for group in range(3):
            ext[group, :, 0] = jnp.zeros((CLIPS, PIX, GW), BF16)

    @pl.when(jnp.logical_not(has_next))
    def _():
        for group in range(3):
            ext[group, :, 3] = jnp.zeros((CLIPS, PIX, GW), BF16)

    def edges(group, clip):
        k = group * CLIPS + clip
        left = sent(ext.at[group, clip, 1], ext.at[group, clip, 3], ssems.at[k, 0], rsems.at[k, 0], prev)
        right = sent(
            ext.at[group, clip, 2], ext.at[group, clip, 0], ssems.at[k, 1], rsems.at[k, 1],
            following,
        )
        return left, right

    def offer(group, clip, first):
        here = lanes(group + 1, GW)

        def piece(step):
            f = clip * SPAN + step
            value = hidden[f, :, here] * gates[f, :, here]
            if not first:
                value = value + agg[f, :, lanes(group, GW)]
            value = value * tab[0, f]
            kept[lax.rem(group, 2), clip, step] = value
            ext[group, clip, step + 1] = value.astype(BF16)

        each(0, SPAN, piece)
        left, right = edges(group, clip)

        @pl.when(has_prev)
        def _():
            left.start()

        @pl.when(has_next)
        def _():
            right.start()

    def taken(group, clip):
        left, right = edges(group, clip)

        @pl.when(has_prev)
        def _():
            left.wait_send()
            right.wait_recv()

        @pl.when(has_next)
        def _():
            right.wait_send()
            left.wait_recv()

    def convolve(group, clip):
        row = [taps[group * 3 + k] for k in range(3)]

        def mix(step):
            f = clip * SPAN + step
            own = [kept[lax.rem(group, 2), clip, k] for k in range(SPAN)]
            line = [ext[group, clip, 0].astype(F32)] + own + [ext[group, clip, 3].astype(F32)]
            here = [jnp.where(step == 0, line[k], line[k + 1]) for k in range(3)]
            mixed = row[0] * here[0] + row[1] * here[1] + row[2] * here[2]
            value = mixed.astype(BF16)
            blended[group, f] = value
            spread_taps(store.at[step], value)
            result = nn(window(store.at[step], 0), kernels[group, 0])
            result += nn(window(store.at[step], 1), kernels[group, 1])
            result += nn(window(store.at[step], 2), kernels[group, 2])
            agg[f, :, lanes(group + 1, GW)] = result

        each(0, SPAN, mix)

    each(0, CLIPS, lambda clip: offer(0, clip, True))

    def base(f):
        agg[f, :, 0:GW] = hidden[f, :, 0:GW] * gates[f, :, 0:GW]

    each(0, T, base)

    def turn(n):
        group, clip = (n // CLIPS, lax.rem(n, CLIPS))
        taken(group, clip)
        convolve(group, clip)

        @pl.when(group < 2)
        def _():
            offer(group + 1, clip, False)

        for k in range(3):

            @pl.when(n == 3 * k + 2)
            def _(k=k):
                run_steps(dp_steps[2 + k])

    each(0, 3 * CLIPS, turn)
    ext_out[...] = ext[...]
    stats_two[...] = jnp.zeros_like(stats_two)
    each(0, T, lambda f: merge(stats_two, agg[f], tab, f))
    run_steps(swap)


def wide_forward(
    ndp, ntm, swap_tab, tab, agg, stats, pair, order, weight_out, video, wide_pair, weight_in,
    hidden_out, out_low, centred, slope, first_out, squares, wide_out, alpha_out,
    hidden, pre, first_sum, wide_stats, *swap_refs,
):
    s = pl.program_id(0)
    h, f = (lax.rem(s, 2 * T) // T, lax.rem(s, T))
    here = lanes(h, C // 2)
    mask = tab[0, f]
    alpha = swap_steps(ndp, ntm, PIX, swap_tab, alpha_out, *swap_refs[4:8])
    sums = swap_refs[4]

    def one(k):
        refs = [ref.at[k] for ref in swap_refs[0:4]]
        return swap_steps(ndp, ntm, PIX, swap_tab, wide_stats.at[k], *refs)

    @pl.when(s == 0)
    def _():
        greet(ndp, ntm)
        swap_refs[0][...] = jnp.zeros_like(swap_refs[0])
        sums[...] = jnp.zeros_like(sums)
        squares[...] = jnp.zeros_like(squares)

    @pl.when(s < T)
    def _():
        z = unit(agg[0], stats) * pair[0:1] + pair[1:2]
        value = nn(order[...], (z * sigmoid(z)).astype(BF16)).astype(BF16)
        hidden[f] = value
        hidden_out[0] = value

    @pl.when(s < 2 * T)
    def _():
        result = nn(hidden[f], weight_out[:, here])
        pre[h, f] = result
        merge(swap_refs[0].at[h], result, tab, f)

    @pl.when(s == 0)
    def _():
        met(ndp, ntm)

    for k in range(2):

        @pl.when(s == 2 * T + k * T)
        def _(k=k):
            one(k)[2]()
            wide_out[:, k * (C // 2) : (k + 1) * (C // 2)] = wide_stats[k]

    @pl.when(s >= 2 * T)
    def _():
        source = nn(order[...], video[0]) * mask
        scaled = unit(pre[h, f], wide_stats[h])
        gains = wide_pair[:, here]
        branch = scaled * gains[0:1] + gains[1:2]
        before = source + branch
        gate = sigmoid(before)
        value = before * gate
        low = value.astype(BF16)
        out_low[0] = low
        centred[0] = scaled.astype(BF16)
        slope[0] = (gate + value * (1.0 - gate)).astype(BF16)
        squares[h, 0:1] += down(jnp.square(branch)) * mask
        squares[h, 1:2] += down(jnp.square(value)) * mask
        part = nn(low, weight_in[rows_at(h, C // 2)])

        @pl.when(h == 0)
        def _():
            first_sum[f] = part

        @pl.when(h == 1)
        def _():
            total = first_sum[f] + part
            first_out[0] = total
            merge(sums, total, tab, f)

    for k in range(2):

        @pl.when(s == (k + 1) * T - 1)
        def _(k=k):
            one(k)[0]()

        @pl.when(s == (k + 1) * T + 3)
        def _(k=k):
            one(k)[1]()

    @pl.when(s == 4 * T - 1)
    def _():
        run_steps(alpha)


def shifted(piece, tap, backward=False):
    rows, cols = (tap // 3 == 0, tap % 3 == 0)
    side = HW // 2
    place = lax.broadcasted_iota(jnp.int32, piece.shape, 0)
    if rows:
        if backward:
            piece = jnp.where(place < QUARTER - side, pltpu.roll(piece, QUARTER - side, 0), 0.0)
        else:
            piece = jnp.where(place >= side, pltpu.roll(piece, side, 0), 0.0)
    if cols:
        col = lax.rem(place, side)
        if backward:
            piece = jnp.where(col < side - 1, pltpu.roll(piece, QUARTER - 1, 0), 0.0)
        else:
            piece = jnp.where(col > 0, pltpu.roll(piece, 1, 0), 0.0)
    return piece


def plane(tap):
    return (0 if tap // 3 == 1 else 2) + (0 if tap % 3 == 1 else 1)


def mid_two(tab, first, stats, pair, weight, taps_out, second, sums, store):
    t = pl.program_id(0)

    @pl.when(t == 0)
    def _():
        def frame(f, carry):
            z = unit(first[f], stats) * pair[0:1] + pair[1:2]
            value = z * sigmoid(z)
            for tap in range(9):
                at = plane(tap) * QUARTER
                piece = shifted(value[at : at + QUARTER], tap)
                store[tap, pl.ds(pl.multiple_of(f * QUARTER, QUARTER), QUARTER)] = piece.astype(BF16)
            return carry

        lax.fori_loop(0, T, frame, 0)

    left = store[t]
    taps_out[0] = left
    part = nn(left, weight[...])

    @pl.when(t == 0)
    def _():
        second[...] = part

    @pl.when(t > 0)
    def _():
        second[...] += part

    @pl.when(t == 8)
    def _():
        parts = [second[f * QUARTER : (f + 1) * QUARTER] for f in range(T)]
        mean, spread = whole_stats(parts, [tab[0, f] for f in range(T)], tab[3, 1])
        sums[0:1] = mean
        sums[1:2] = spread


def middle(
    ndp, ntm, swap_tab, tab, second, stats_mid, pair_mid, joined, even, pairs, cotangent,
    result, grad_weight, grad_projection, grad_even, grad_mid, squares, totals_out, beta_out,
    hidden, thirds, shorts, grads, stats_all, totals_all, hidden_sum,
    mains_all, sides_all, weight_store, projection_store, held, sems, *swap_refs,
):
    s = pl.program_id(0)
    steps = WIDE_STEPS
    j = lax.rem(s, steps)
    sums = swap_refs[8]
    beta = swap_steps(ndp, ntm, None, None, beta_out, *swap_refs[8:12])

    def one(k):
        refs = [ref.at[k] for ref in swap_refs[0:4]]
        return swap_steps(ndp, ntm, QUARTER, swap_tab, stats_all.at[k], *refs)

    def two(k):
        refs = [ref.at[k] for ref in swap_refs[4:8]]
        return swap_steps(ndp, ntm, None, None, totals_all.at[k], *refs)

    def load(k):
        return pltpu.make_async_copy(joined.at[:, k], held.at[k], sems.at[2, k])

    def projection(k):
        return held[k, :, 0 : C // 8].reshape(C, WIDE_TILE)

    def weight(k):
        return held[k, :, C // 8 :].reshape(M, WIDE_TILE)

    @pl.when(s == 0)
    def _():
        greet(ndp, ntm)
        each(0, steps, lambda k: load(k).start())
        z = unit(second[...], stats_mid) * pair_mid[0:1] + pair_mid[1:2]
        hidden[...] = (z * sigmoid(z)).astype(BF16)

    @pl.when(s < steps)
    def _():
        load(j).wait()
        third = nn(hidden[...], weight(j))
        short = nn(even[...].reshape(HALF_ROWS, C), projection(j))
        thirds[j] = third
        shorts[j] = short
        stats = swap_refs[0].at[j]
        stats[...] = jnp.zeros((4, WIDE_TILE), F32)

        def gather_stats(f):
            merge(stats.at[0:2], thirds[j, rows_at(f, QUARTER)], tab, f)
            merge(stats.at[2:4], shorts[j, rows_at(f, QUARTER)], tab, f)

        each(0, T, gather_stats)

    @pl.when(s == 0)
    def _():
        met(ndp, ntm)

    @pl.when(s < steps)
    def _():
        one(j)[0]()

    @pl.when((s >= steps) & (s < 2 * steps))
    def _():
        one(j)[2]()
        stats = stats_all[j]
        sums_two = swap_refs[4].at[j]
        sums_two[...] = jnp.zeros((4, WIDE_TILE), F32)
        squares[...] = jnp.zeros_like(squares)

        def frame(f):
            rows, mask = (rows_at(f, QUARTER), tab[0, f])
            main = unit(thirds[j, rows], stats[0:2])
            side = unit(shorts[j, rows], stats[2:4])
            branch = main * pairs[0:1] + pairs[1:2]
            before = branch + (side * pairs[2:3] + pairs[3:4])
            gate = sigmoid(before)
            value = before * gate
            masked = value * mask
            result[rows] = masked.astype(BF16)
            grad = (gate + value * (1.0 - gate)) * (cotangent[rows].astype(F32) * mask)
            grads[j, rows] = grad
            for k, part in enumerate((grad, grad * main, grad * side)):
                sums_two[k : k + 1] += down(part)
            squares[0:1] += down(jnp.square(branch) * mask)
            squares[1:2] += down(jnp.square(masked))

        each(0, T, frame)
        two(j)[0]()

    @pl.when(s >= 2 * steps)
    def _():
        two(j)[2]()
        totals = totals_all[j]
        totals_out[:, lanes(j, WIDE_TILE)] = totals
        stats = stats_all[j]
        side_totals = jnp.concatenate([totals[0:1], totals[2:3]], axis=0)

        def frame(f):
            rows, mask = (rows_at(f, QUARTER), tab[0, f])
            grad = grads[j, rows]
            main = unit(thirds[j, rows], stats[0:2])
            main = norm_back(grad, main, stats[0:2], pairs[0:2], totals[0:2], mask, tab[3, 3])
            mains_all[j, rows] = main.astype(BF16)
            side = unit(shorts[j, rows], stats[2:4])
            side = norm_back(grad, side, stats[2:4], pairs[2:4], side_totals, mask, tab[3, 3])
            sides_all[j, rows] = side.astype(BF16)

        each(0, T, frame)
        hidden_part = nt(mains_all[j], weight(j))
        even_part = nt(sides_all[j], projection(j))

        @pl.when(j == 0)
        def _():
            hidden_sum[...] = hidden_part
            grad_even[...] = even_part

        @pl.when(j > 0)
        def _():
            hidden_sum[...] += hidden_part
            grad_even[...] += even_part

    @pl.when((s >= 2) & (s < steps + 2))
    def _():
        one(s - 2)[1]()

    @pl.when((s >= steps + 2) & (s < 2 * steps + 2))
    def _():
        two(s - steps - 2)[1]()

    def stores(k):
        here = lanes(k, WIDE_TILE)
        return [
            pltpu.make_async_copy(
                projection_store.at[k], grad_projection.at[:, here], sems.at[0, k]
            ),
            pltpu.make_async_copy(weight_store.at[k], grad_weight.at[:, here], sems.at[1, k]),
        ]

    def product(k):
        source = even[...].reshape(HALF_ROWS, C)
        projection_store[k] = tn(source, sides_all[k]).astype(BF16)
        weight_store[k] = tn(hidden[...], mains_all[k]).astype(BF16)
        start_all(stores(k))

    @pl.when(s == 3 * steps - 1)
    def _():
        centred = unit(second[...], stats_mid)
        z = centred * pair_mid[0:1] + pair_mid[1:2]
        gate = sigmoid(z)
        grad = hidden_sum[...] * (gate + z * gate * (1.0 - gate))
        grad_mid[...] = grad
        sums[0:1] = down(grad)
        sums[1:2] = down(grad * centred)
        beta[0]()
        each(0, steps // 2, product)
        beta[1]()
        each(steps // 2, steps, product)
        beta[2]()
        each(0, steps, lambda k: wait_all(stores(k)))


def back_mid(
    tab, grads, second, stats, pair, totals, taps_in, weight, first, stats_a, pair_a,
    grad_weight, grad_first, sums, low, store, held, sem, partial_sum,
):
    t = pl.program_id(0)
    load = pltpu.make_async_copy(taps_in, held, sem)

    @pl.when(t == 0)
    def _():
        load.start()

        def normal(f):
            rows = rows_at(f, QUARTER)
            centred = unit(second[rows], stats)
            grad = norm_back(grads[rows], centred, stats, pair, totals, tab[0, f], tab[3, 3])
            low[rows] = grad.astype(BF16)

        each(0, T, normal)
        store[...] = jnp.zeros_like(store)

    partial_sum[...] = nt(low[...], weight[...])
    for tap in range(9):

        @pl.when(t == tap)
        def _(tap=tap):
            at = plane(tap) * QUARTER

            def put(f):
                piece = shifted(partial_sum[rows_at(f, QUARTER)], tap, True)
                store[f, at : at + QUARTER] += piece

            each(0, T, put)

    @pl.when(t == 8)
    def _():
        sums[...] = jnp.zeros_like(sums)

        def frame(f, carry):
            centred = unit(first[f], stats_a)
            z = centred * pair_a[0:1] + pair_a[1:2]
            gate = sigmoid(z)
            grad = store[f] * (gate + z * gate * (1.0 - gate))
            grad_first[f] = grad
            sums[0:1] += down(grad)
            sums[1:2] += down(grad * centred)
            return carry

        lax.fori_loop(0, T, frame, 0)

    def products(steps):
        def run():
            if steps[0] == 0:
                load.wait()

            def product(tap):
                grad_weight[:, lanes(tap, M)] = tn(held[tap], low[...]).astype(BF16)

            each(steps[0], steps[-1] + 1, product)

        return run

    return [products(range(5)), products(range(5, 9))]


def back_in_two(
    tab, grads, first, stats, pair, totals, out_low, weight, even, slope, centred,
    grad_weight, grad_before, sums, lows, held, sem,
):
    i = pl.program_id(0)
    load = pltpu.make_async_copy(out_low, held, sem)
    scaled = unit(first[0], stats)
    low = norm_back(grads[0], scaled, stats, pair, totals, tab[0, i], tab[3, 2]).astype(BF16)
    grad = nt(low, weight[...])
    lows[i] = low

    @pl.when(i == 0)
    def _():
        load.start()
        sums[...] = jnp.zeros_like(sums)

    grad = jnp.concatenate([grad[0:QUARTER] + even[...], grad[QUARTER:]], axis=0)
    grad = grad * slope[0].astype(F32)
    grad_before[0] = grad.astype(BF16)
    sums[0:1] += down(grad)
    sums[1:2] += down(grad * centred[0].astype(F32))

    def products(steps):
        def run():
            if steps[0] == 0:
                load.wait()

            def product(k):
                source = held[:, :, lanes(k, WIDE_TILE)].reshape(ROWS, WIDE_TILE)
                value = tn(source, lows[...].reshape(ROWS, M))
                grad_weight[rows_at(k, WIDE_TILE)] = value.astype(BF16)

            each(steps[0], steps[-1] + 1, product)

        return run

    half = WIDE_STEPS // 2
    return [products(range(half)), products(range(half, WIDE_STEPS))]


def back_out_one(
    tab, grads, centred, stats, pair, totals, hidden, weight, order, agg, stats_two, pair_two,
    grad_weight, grad_two, sums, lows, held, sem,
):
    i = pl.program_id(0)
    load = pltpu.make_async_copy(hidden, held, sem)
    low = norm_back(
        grads[0].astype(F32), centred[0].astype(F32), stats, pair, totals, tab[0, i], tab[3, 2]
    ).astype(BF16)
    grad = nt(low, weight[...])
    lows[i] = low

    @pl.when(i == 0)
    def _():
        load.start()
        sums[...] = jnp.zeros_like(sums)

    high = grad.astype(BF16)
    rest = (grad - high.astype(F32)).astype(BF16)
    grad = tn(order[...], high) + tn(order[...], rest)
    scaled = unit(agg[0], stats_two)
    z = scaled * pair_two[0:1] + pair_two[1:2]
    gate = sigmoid(z)
    grad = grad * (gate + z * gate * (1.0 - gate))
    grad_two[0] = grad
    sums[0:1] += down(grad)
    sums[1:2] += down(grad * scaled)

    def products(steps):
        def run():
            if steps[0] == 0:
                load.wait()

            def product(k):
                here = lanes(k, WIDE_TILE)
                source = lows[:, :, here].reshape(ROWS, WIDE_TILE)
                grad_weight[:, here] = tn(held[...].reshape(ROWS, M), source).astype(BF16)

            each(steps[0], steps[-1] + 1, product)

        return run

    half = WIDE_STEPS // 2
    return [products(range(half)), products(range(half, WIDE_STEPS))]


def mta_backward(
    ndp, ntm, items, edge, tab, grads_in, agg_in, stats_two, pair_two, totals, pre_in, stats, pair,
    sigma, ext_in, blended_in, kernels_in, taps, reduce_low, conv_low, expand, windows, later,
    snext, pooled, *refs,
):
    count = len(items)
    sources, refs = (refs[:count], refs[count:])
    grad_one, totals_out, grad_mta, grad_reduce, grad_conv, grad_expand, grad_bias = refs[:7]
    grad_taps, refs = (refs[7], refs[8:])
    outs = []
    if count:
        base = 0
        for _, rows, cols, _ in items:
            outs.append((refs[0], base, rows))
            base += rows * (cols // ntm // GW)
        refs = refs[1:]
    mixed, low_store, store, back, parts, edge_send, edge_recv, mta_sum = refs[:8]
    k_store, k_send, k_recv, gate_sum, ssems, rsems, tiles, tap_sum, spreads, changes = refs[8:18]
    grads, agg, pre, ext, blended, kernels, hiddens, slopes, load_sems = refs[18:27]
    swap_refs, refs = (refs[27:31], refs[31:])
    sums = swap_refs[0]
    loads = [
        pltpu.make_async_copy(source, target, load_sems.at[k])
        for k, (source, target) in enumerate(
            (
                (grads_in, grads), (agg_in, agg), (kernels_in, kernels), (ext_in, ext),
                (blended_in, blended), (pre_in, pre),
            )
        )
    ]
    start_all(loads)
    has_prev, has_next, prev, following = neighbours(ntm)
    greet(ndp, ntm)
    swap = swap_steps(ndp, ntm, None, None, totals_out, *swap_refs)
    steps = [[], [], [], [], []]
    if count:
        steps = scatter_steps(ndp, ntm, items, sources, outs, refs, True)

    def start(group):
        here = slice(group * GW, (group + 1) * GW)

        def frame(f):
            centred = (agg[f, :, here] - stats_two[0:1, here]) * stats_two[1:2, here]
            total, cross = (totals[0:1, here] * tab[3, 2], totals[1:2, here] * tab[3, 2])
            scale = pair_two[0:1, here] * stats_two[1:2, here]
            mixed[f, :, here] = scale * (
                grads[f, :, here] - tab[0, f] * (total + centred * cross)
            )

        each(0, T, frame)

    def activate(f):
        z = unit(pre[f], stats) * pair[0:1] + pair[1:2]
        gate = sigmoid(z)
        value = z * gate
        hiddens[f] = value
        slopes[f] = gate + value * (1.0 - gate)

    met(ndp, ntm)
    run_steps(steps[0])
    wait_all(loads[0:2])
    start(3)
    wait_all(loads[2:5])
    run_steps(steps[1][0:2])

    @pl.when(jnp.logical_not(has_prev))
    def _():
        edge_recv[:, :, 0] = jnp.zeros((3, CLIPS, PIX, GW), BF16)

    @pl.when(jnp.logical_not(has_next))
    def _():
        edge_recv[:, :, 1] = jnp.zeros((3, CLIPS, PIX, GW), BF16)

    tap_sum[...] = jnp.zeros_like(tap_sum)

    def edges(group, clip):
        k = group * CLIPS + clip
        left = sent(
            edge_send.at[group, clip, 0], edge_recv.at[group, clip, 1], ssems.at[k, 0],
            rsems.at[k, 0], prev,
        )
        right = sent(
            edge_send.at[group, clip, 1], edge_recv.at[group, clip, 0], ssems.at[k, 1],
            rsems.at[k, 1], following,
        )
        return left, right

    def convolve(group, clip):
        row = [taps[group * 3 + k] for k in range(3)]
        rest = jnp.where(group < 2, 1.0, 0.0)

        def part(step):
            f = clip * SPAN + step
            value = mixed[f, :, lanes(group + 1, GW)]
            value = value + rest * mixed[f, :, lanes(jnp.minimum(group + 2, 3), GW)]
            value = value.astype(BF16)
            low_store[f] = value
            spread_taps(store.at[step], value)
            result = jnp.zeros((PIX, GW), F32)
            for tap in range(9):
                other = 8 - tap
                patch = store[
                    step,
                    (tap // 3) * HW : (tap // 3) * HW + PIX,
                    (tap % 3) * GW : (tap % 3 + 1) * GW,
                ]
                at = other % 3 * GW
                result += nt(patch, kernels[group, other // 3, at : at + GW])
            for k in range(3):
                source = ext[group, clip, step + k].astype(F32)
                tap_sum[group * 3 + k] += down(result * source)
            parts[step] = result

        each(0, SPAN, part)
        edge_send[group, clip, 0] = (row[0] * parts[0]).astype(BF16)
        edge_send[group, clip, 1] = (row[2] * parts[1]).astype(BF16)
        left, right = edges(group, clip)

        @pl.when(has_prev)
        def _():
            left.start()

        @pl.when(has_next)
        def _():
            right.start()

        back[clip, 0] = row[1] * parts[0] + row[0] * parts[1]
        back[clip, 1] = row[2] * parts[0] + row[1] * parts[1]

    def products(group, clip):
        def product(step):
            f = clip * SPAN + step
            spread_taps(store.at[step], blended[group, f])
            for k in range(3):
                mta_sum[k] += tn(window(store.at[step], k), low_store[f])

        each(0, SPAN, product)

    def collect(group, clip):
        left, right = edges(group, clip)

        @pl.when(has_prev)
        def _():
            left.wait_send()
            right.wait_recv()

        @pl.when(has_next)
        def _():
            right.wait_send()
            left.wait_recv()

        def put(step):
            f = clip * SPAN + step
            total = back[clip, step] + edge_recv[group, clip, step].astype(F32)
            mixed[f, :, lanes(group + 1, GW)] = total * tab[0, f]

        each(0, SPAN, put)

    moments = {
        0: steps[1][2:5], 1: steps[1][5:], 5: steps[2][0:2], 8: steps[2][2:4],
    }

    def turn(n):
        group, clip = (2 - n // CLIPS, lax.rem(n, CLIPS))

        @pl.when(n >= CLIPS)
        def _():
            collect(group + 1, clip)

        convolve(group, clip)

        @pl.when(clip == 0)
        def _():
            mta_sum[...] = jnp.zeros_like(mta_sum)

        products(group, clip)

        @pl.when(clip == CLIPS - 1)
        def _():
            for tap in range(9):
                at = tap % 3 * GW
                tiles[group * 9 + tap] = mta_sum[tap // 3, at : at + GW].astype(BF16)

        for k in range(3):

            @pl.when(n == k)
            def _(k=k):
                start(2 - k)

        @pl.when(n == CLIPS)
        def _():
            loads[5].wait()

        @pl.when(n >= CLIPS)
        def _():
            activate(n - CLIPS)

        for k, moment in moments.items():
            if moment:

                @pl.when(n == k)
                def _(moment=moment):
                    run_steps(moment)

    each(0, 3 * CLIPS, turn)
    each(0, CLIPS, lambda clip: collect(0, clip))
    for k in range(9):
        grad_taps[k : k + 1] = tap_sum[k]

    def gates(f):
        gate_sum[f] = down(mixed[f] * hiddens[f])

    each(0, T, gates)
    run_steps(steps[2][4:6])
    gate = sigma[...]
    excite = rows_of([gate_sum[f] for f in range(T)]) * gate * (1.0 - gate)
    grad_bias[...] = down(excite)
    grad_expand[...] = tn_exact(pooled[...], excite)
    change = nt_exact(excite, expand[...]) * (later[...] * (1.0 / PIX))
    change_low = change.astype(BF16)
    change_wide = change_low.astype(F32)
    for tap in range(9):
        rows = rows_of([snext[f, tap : tap + 1] for f in range(T)])
        grad_conv[tap] = tn_exact(rows, change_wide)[0:R]
        k_store[tap] = nt(change_low, conv_low[tap].astype(BF16))
    index = lax.broadcasted_iota(jnp.int32, (16, GW), 0)

    def stacked(f):
        result = jnp.zeros((16, GW), F32)
        for tap in range(9):
            result = jnp.where(index == tap, k_store[tap, f : f + 1], result)
        return result

    for clip in range(CLIPS):
        k_send[clip] = stacked(clip * SPAN + 1)
    onward = sent(k_send, k_recv, ssems.at[9, 0], rsems.at[9, 0], following)

    @pl.when(has_next)
    def _():
        onward.start()
        onward.wait_send()

    @pl.when(has_prev)
    def _():
        onward.wait_recv()

    @pl.when(jnp.logical_not(has_prev))
    def _():
        k_recv[...] = jnp.zeros_like(k_recv)

    sums[...] = jnp.zeros_like(sums)
    grad_reduce[...] = jnp.zeros_like(grad_reduce)
    for f in range(T):
        spreads[f] = k_recv[f // SPAN] if f % SPAN == 0 else stacked(f - 1)
        changes[f] = change[f : f + 1]
        gate_sum[f] = 1.0 + gate[f : f + 1]

    def finish_frame(f):
        motion = tn_exact(windows[...].astype(F32), spreads[f]) - changes[f]
        motion_low = motion.astype(BF16)
        grad_reduce[...] += tn(motion_low, hiddens[f].astype(BF16))[0:R]
        grad = mixed[f] * gate_sum[f] + nt(motion_low, reduce_low[...])
        grad = grad * slopes[f]
        grad_one[f] = grad
        sums[0:1] += down(grad)
        sums[1:2] += down(grad * unit(pre[f], stats))

    each(0, T, finish_frame)
    run_steps(steps[2][6:])
    swap[0]()
    if edge:

        def assemble(place):
            grad_mta[:, lanes(place, GW)] = edge_from_tiles(
                tiles, place, edge, grad_mta.shape[1] // ntm
            )

        each(0, grad_mta.shape[1] // GW, assemble)
    else:
        grad_mta[...] = tiles[...]
    swap[1]()
    run_steps(steps[3])
    swap[2]()


def back_in_one(
    tab, grads, pre, stats, pair, totals, video, weight, order, grad_before,
    grad_weight, grad_video, lows, held, sem,
):
    i = pl.program_id(0)
    load = pltpu.make_async_copy(video, held, sem)
    centred = unit(pre[0], stats)
    low = norm_back(grads[0], centred, stats, pair, totals, tab[0, i], tab[3, 2]).astype(BF16)
    lows[i] = low

    @pl.when(i == 0)
    def _():
        load.start()

    grad = nt(low, weight[...]) + tn(order[...], grad_before[0])
    grad_video[0] = (grad * tab[0, i]).astype(BF16)

    def products(steps):
        def run():
            if steps[0] == 0:
                load.wait()

            def product(k):
                source = held[:, :, lanes(k, WIDE_TILE)].reshape(ROWS, WIDE_TILE)
                value = tn(source, lows[...].reshape(ROWS, M))
                grad_weight[rows_at(k, WIDE_TILE)] = value.astype(BF16)

            each(steps[0], steps[-1] + 1, product)

        return run

    half = WIDE_STEPS // 2
    return [products(range(half)), products(range(half, WIDE_STEPS))]


def pack_sums(packed, reduce, expand, conv, bias, taps, source, one, last):
    packed[...] = jnp.zeros_like(packed)
    for k in range(M // GW):
        part = slice(k * GW, (k + 1) * GW)
        packed[k * R : (k + 1) * R] = reduce[:, part]
        packed[128 + k * R : 128 + (k + 1) * R] = expand[0:R, part]
        packed[352 + k : 353 + k] = bias[:, part]
    for group in range(3):
        value = conv[4 * group]
        for k in range(1, min(4, 9 - 4 * group)):
            value = value + pltpu.roll(conv[4 * group + k], k * R, 1)
        packed[256 + group * R : 256 + (group + 1) * R] = value
    packed[360:369] = taps[...]
    lane = lax.broadcasted_iota(jnp.int32, (1, GW), 1)
    row = jnp.zeros((1, GW), F32)
    pieces = (
        source[0:1], one[0, 0:1] + one[1, 0:1], one[0, 1:2] + one[1, 1:2], last[0:1], last[1:2],
    )
    for k, value in enumerate(pieces):
        row = jnp.where(lane == k, jnp.sum(value, axis=1, keepdims=True), row)
    packed[376:377] = row


def unpack_sums(summed, reduce, expand, conv, bias, taps, squares):
    for k in range(M // GW):
        part = slice(k * GW, (k + 1) * GW)
        reduce[:, part] = summed[k * R : (k + 1) * R]
        expand[:, part] = summed[128 + k * R : 128 + (k + 1) * R]
        bias[:, part] = summed[352 + k : 353 + k]
    for tap in range(9):
        group, k = divmod(tap, 4)
        value = summed[256 + group * R : 256 + (group + 1) * R]
        conv[tap] = value if k == 0 else pltpu.roll(value, GW - k * R, 1)
    taps[...] = summed[360:369]
    squares[...] = summed[376:384]


def final_sums(ndp, ntm, *refs):
    ins, outs = (refs[:8], refs[8:14])
    packed, summed, first, second, sems = refs[14:]
    greet(ndp, ntm)
    pack_sums(packed, *ins)
    met(ndp, ntm)
    run_steps(all_sums_steps(ndp, ntm, packed, summed, first, second, sems))
    unpack_sums(summed, *outs)


def last_part(ndp, ntm, items, own_items, *refs):
    tab, grads, pre, stats, pair, totals, video, weight, order, grad_before = refs[:10]
    small_ins, refs = (refs[10:18], refs[18:])
    sources, refs = (refs[: len(items)], refs[len(items) :])
    grad_video, small_outs, refs = (refs[0], refs[1:7], refs[7:])
    outs, refs = (refs[: len(items)], refs[len(items) :])
    own_out, refs = (refs[0], refs[1:])
    lows, held, sem, grad_weight, packed, summed, first, second, sems = refs[:9]
    count = 5 * len(scatter_chunks(items)) + 2
    i = pl.program_id(0)
    load = pltpu.make_async_copy(video, held, sem)
    large = scatter_steps(ndp, ntm, items, sources, outs, refs[9 : 9 + count])
    own = scatter_steps(ndp, ntm, own_items, [grad_weight], [own_out], refs[9 + count :])
    small = all_sums_steps(ndp, ntm, packed, summed, first, second, sems)

    @pl.when(i == 0)
    def _():
        greet(ndp, ntm)
        load.start()
        pack_sums(packed, *small_ins)
        met(ndp, ntm)
        run_steps(large[0])
        small[0]()

    @pl.when(i < T)
    def _():
        centred = unit(pre[0], stats)
        low = norm_back(grads[0], centred, stats, pair, totals, tab[0, i], tab[3, 2])
        lows[i] = low.astype(BF16)

    @pl.when(i == T - 1)
    def _():
        load.wait()
        small[1]()
        run_steps(large[1])

        def product(k):
            source = held[:, :, lanes(k, WIDE_TILE)].reshape(ROWS, WIDE_TILE)
            value = tn(source, lows[...].reshape(ROWS, M)).astype(BF16)
            grad_weight[k // 2, lax.rem(k, 2)] = value.reshape(2, C // 8, M)

        each(0, WIDE_STEPS, product)
        run_steps(own[0])

    @pl.when(i >= T)
    def _():
        grad = nt(lows[i - T], weight[...]) + tn(order[...], grad_before[0])
        grad_video[0] = (grad * tab[0, i - T]).astype(BF16)

    @pl.when(i == T)
    def _():
        small[2]()

    @pl.when(i == T + 2)
    def _():
        run_steps(own[1])

    @pl.when(i == T + 3)
    def _():
        run_steps(large[2])
        small[3]()

    @pl.when(i == 2 * T - 1)
    def _():
        run_steps(large[3])
        run_steps(own[2])
        small[4]()
        unpack_sums(summed, *small_outs)
        run_steps(large[4])
        run_steps(own[3])
        run_steps(own[4])


def wrap(
    fast, reduce, expand, conv, bias, taps, squares, swap, one, two, alpha, beta, three, last, *refs
):
    ins, refs = (refs[:6], refs[6:]) if fast else ((), refs)
    loads, stores = ([], [])
    if fast:
        *targets, held_one, held_two, sems = refs[-5:]
        refs = refs[:-5]
        for k, (source, target, held) in enumerate(
            zip(ins[4:6], targets, (held_one, held_two))
        ):
            size = source.shape[0] // T
            for j in range(T):
                part = pl.ds(j * size, size)
                loads.append(
                    pltpu.make_async_copy(source.at[part], held.at[part], sems.at[k, 0, j])
                )
                stores.append(
                    pltpu.make_async_copy(held.at[part], target.at[part], sems.at[k, 1, j])
                )
    start_all(loads)
    wrap_small(
        fast, reduce, expand, conv, bias, taps, squares, swap, one, two, alpha, beta, three,
        last, ins, refs,
    )
    for load, store in zip(loads, stores):
        load.wait()
        store.start()
    wait_all(stores)


def wrap_small(
    fast, reduce, expand, conv, bias, taps, squares, swap, one, two, alpha, beta, three, last, ins,
    refs,
):
    mid, wide, taps_out, reduce_out, conv_out, expand_out, bias_out, rms = refs[:8]
    for k, totals in enumerate((one, two, alpha, beta)):
        mid[k, 0:1] = totals[1:2]
        mid[k, 1:2] = totals[0:1]
    for k, (gain, shift) in enumerate(((three[1:2], three[0:1]), (last[1:2], last[0:1]))):
        wide[k, 0:1] = gain
        wide[k, 1:2] = shift
    wide[2, 0:1] = last[2:3]
    wide[2, 1:2] = last[0:1]
    for k in range(3):
        taps_out[k] = taps[3 * k : 3 * k + 3]
    reduce_out[...] = reduce[...]
    conv_out[...] = conv[:, :, 0:R]
    expand_out[...] = expand[...]
    bias_out[...] = bias[...]
    lane = lax.broadcasted_iota(jnp.int32, (1, GW), 1)
    total = swap[5:6]
    counts = jnp.where(lane < 3, total * PIX, total * QUARTER) * C
    rms[...] = jnp.sqrt(squares[0:1] / counts)[:, 0:5]
    if fast:
        mta, in1, projection, over = ins[:4]
        in1_out, mta_out, out1_out, in2_out, mid2_out, out2_out, proj_out = refs[8:15]
        in1_out[...] = in1[...]
        mta_out[...] = mta[:, 0 : mta_out.shape[1]]
        proj_out[...] = projection[...].astype(F32)
        at = 0
        for target in (mid2_out, in2_out, out2_out, out1_out):
            rows = target.shape[0]
            for k in range(target.shape[1] // GW):
                target[:, k * GW : (k + 1) * GW] = over[at : at + rows].astype(F32)
                at += rows


def parity_order():
    order = np.zeros((PIX, PIX), np.float32)
    for y in range(HW):
        for x in range(HW):
            row = ((y % 2) * 2 + x % 2) * QUARTER + (y // 2) * (HW // 2) + x // 2
            order[row, y * HW + x] = 1.0
    return order


def window_rows():
    rows = np.zeros((16, PIX), np.float32)
    for tap in range(9):
        for y in range(HW):
            for x in range(HW):
                inside = 0 <= y - (tap // 3 - 1) < HW and 0 <= x - (tap % 3 - 1) < HW
                rows[tap, y * HW + x] = float(inside)
    return rows


def fetch(shard):
    partly = lax.all_gather(shard.astype(BF16), "tm", axis=1, tiled=True)
    return lax.all_gather(partly, "dp", axis=0, tiled=True)


def deliver(gradient):
    partly = lax.psum_scatter(gradient, "dp", scatter_dimension=0, tiled=True)
    return lax.psum_scatter(partly, "tm", scatter_dimension=1, tiled=True).astype(F32)


def padded(values, rows, cols):
    return jnp.pad(values, ((0, rows - values.shape[0]), (0, cols - values.shape[1])))


def tables(lengths, ndp, ntm):
    d, t = (lax.axis_index("dp"), lax.axis_index("tm"))
    grouped = lengths.reshape(ndp, CLIPS)
    starts = jnp.arange(ntm, dtype=jnp.int32) * SPAN
    counts = jnp.sum(jnp.clip(grouped[:, :, None] - starts, 0, SPAN), axis=1).astype(F32)
    own = lax.dynamic_slice_in_dim(lengths, d * CLIPS, CLIPS)
    stamps = t * SPAN + jnp.arange(SPAN, dtype=jnp.int32)
    mask = (stamps[None, :] < own[:, None]).astype(F32).reshape(T)
    later = (stamps[None, :] + 1 < own[:, None]).astype(F32).reshape(T)
    total = jnp.sum(lengths).astype(F32)
    before = jnp.cumsum(mask) - mask
    held = jnp.maximum(before + mask, 1.0)
    local = jnp.maximum(jnp.sum(mask), 1.0)
    full, half = (1.0 / PIX, 1.0 / QUARTER)
    last = jnp.stack([full / local, half / local, full / total, half / total, total, total])
    tab = jnp.stack([mask, mask / held, before * mask / held, last])
    width = max(ndp, ntm)
    column = lax.dynamic_slice_in_dim(counts, t, 1, axis=1)[:, 0]
    sums = jnp.sum(counts, axis=0)

    def row(values):
        return jnp.pad(values, (0, width - values.shape[0]))

    swap = jnp.stack(
        [
            row(column / jnp.maximum(jnp.sum(column), 1.0)),
            row(column),
            row(sums / total),
            row(sums),
            jnp.broadcast_to(1.0 / total, (width,)),
        ]
    )
    return (tab, swap, later, total)


def local(
    video, lengths, mid_norms, wide_norms, taps, me_reduce, me_conv, me_expand, me_bias,
    w_in1, w_mta, w_out1, w_in2, w_mid2, w_out2, w_proj, grad_out,
):
    ndp, ntm = (lax.axis_size("dp"), lax.axis_size("tm"))
    fast = ndp == 8 and ntm == 4
    order = jnp.asarray(parity_order(), BF16)
    windows = jnp.asarray(window_rows(), BF16)
    frames = video.reshape(T, PIX, C)
    cotangent = grad_out.reshape(HALF_ROWS, C)
    bias = me_bias.reshape(1, M)
    tap_rows = taps.reshape(9, 1, GW)
    main_pairs = jnp.concatenate([wide_norms[1], wide_norms[2]], axis=0)
    stage = functools.partial(staged, ndp=ndp, ntm=ntm)

    def gathered(rows):
        return lax.all_gather(rows, "dp", axis=0, tiled=True)

    edge = w_mta.shape[1]
    edge_wide = -(-edge // GW) * GW
    small = (8, GW)
    if fast:
        shard_rows = [w_in1.shape, (w_mta.shape[0], edge_wide), w_out1.shape, w_mid2.shape]
        wide_rows = [(rows, cols * ntm) for rows, cols in shard_rows]
        (
            full_in1, full_mta, rows_out1, rows_mid2, pair, tab, swap, later, reduce_low,
            conv_low, expand,
        ) = remote_call(
            "first_gather", functools.partial(first_gather, ndp, ntm), 1,
            [SCALARS] + [WHOLE] * 9, [WHOLE] * 11,
            [shaped((4, 2) + shape, BF16) for shape in wide_rows[:2]]
            + [shaped(shape, BF16) for shape in wide_rows[2:]]
            + [
                shaped(((C + M) // 8, WIDE_TILE), BF16), shaped(small), shaped(small), shaped(small), shaped((M, GW), BF16),
                shaped((9, GW, GW)), shaped((GW, M)),
            ],
            [VMEM(shape, BF16) for shape in shard_rows] + [DMA((4, 4, 3, ntm)), DMA((2, 4, 4, 2))],
            1 << 24,
            lengths, w_in1, w_mta, w_out1, w_mid2, w_proj, w_out2, me_reduce.T, me_conv.reshape(9, R, R),
            me_expand,
        )
        full_in1 = full_in1.reshape(C, M)
        full_mta = full_mta.reshape(GW, ntm * edge_wide)
        full_mid2 = gathered(rows_mid2)
        joined = lax.all_gather(pair, ("dp", "tm"), axis=0, tiled=True)
    else:
        tab, swap, later, total = tables(lengths, ndp, ntm)
        later = jnp.broadcast_to(jnp.pad(later, (0, 2))[:, None], small)
        reduce_low = padded(me_reduce, M, GW).astype(BF16)
        conv_low = jnp.pad(me_conv.reshape(9, R, R), ((0, 0), (0, GW - R), (0, GW - R)))
        conv_low = conv_low.astype(BF16).astype(F32)
        expand = padded(me_expand, GW, M)
        full_in1, full_mta, full_out1, full_in2, full_mid2, full_out2, full_proj = [
            fetch(shard) for shard in (w_in1, w_mta, w_out1, w_in2, w_mid2, w_out2, w_proj)
        ]
        full_mta = jnp.transpose(full_mta.reshape(GW, 27, GW), (1, 0, 2))
        halves = [
            jnp.transpose(full.reshape(8, -1, WIDE_STEPS, WIDE_TILE), (0, 2, 1, 3))
            for full in (full_proj, full_out2)
        ]
        joined = jnp.concatenate(halves, axis=2)
    joined = joined.reshape(8, WIDE_STEPS, (C + M) // 8, WIDE_TILE)

    frame_wide, frame_mid = (at_first((1, PIX, C)), at_first((1, PIX, M)))
    pair_mid, pair_wide = (fixed((2, M)), fixed((2, C)))
    wide_low, mid_wide = (shaped((T, PIX, C), BF16), shaped((T, PIX, M)))
    even_spec = fixed((T, QUARTER, C))
    order_spec = fixed((PIX, PIX))
    half_mid = fixed((HALF_ROWS, M))
    ins_tab = (tab, SCALARS)
    mids = [(mid_norms[k], pair_mid) for k in range(4)]
    order_in = (order, order_spec)

    pre, squares_source, stats_one, *rows = stage(
        "in_one", 2, steps=T, body=in_one,
        ins=[ins_tab, (frames, frame_wide), (full_in1, fixed((C, M)))],
        outs=[(mid_wide, frame_mid), (shaped((1, C)), fixed((1, C))), LOCAL],
        scratch=[], cost=2 * ROWS * C * M, swap=(swap, PIX, (2, M)),
        carry=(w_in2,) if fast else (),
    )

    frame_low = (T, PIX, GW)
    carried = [rows_out1, *rows] if fast else []
    agg, stats_two, ext, blended, sigma, snext, pooled, kernels, *rows = remote_call(
        "mta_forward", functools.partial(mta_forward, ndp, ntm, fast, edge), 3,
        [SCALARS] * 2 + [WHOLE] * (11 + len(carried)),
        [WHOLE] * (8 + len(carried)),
        [
            mid_wide, shaped((2, M)), shaped((3, CLIPS, 4, PIX, GW), BF16),
            shaped((3,) + frame_low, BF16), shaped((8, M)), shaped((T, 16, GW)), shaped((8, GW)),
            shaped((3, 3, 3 * GW, GW), BF16),
        ]
        + [shaped((4, 2) + part.shape, BF16) for part in carried],
        [
            VMEM((T, PIX, M), F32), VMEM((SPAN, PIX + 2 * HW, 3 * GW), BF16),
            VMEM((3, CLIPS, 4, PIX, GW), BF16), VMEM((2, CLIPS, SPAN, PIX, GW), F32),
            VMEM((T, 1, M), F32), VMEM((T, 16, GW), F32), VMEM((CLIPS, 16, GW), F32),
            VMEM((CLIPS, 16, GW), F32), DMA((10, 2)), DMA((10, 2)),
        ]
        + swap_scratch(ndp, ntm, (2, M))
        + ([DMA((2, 2, 1, 1)), DMA((2, 4, 2, 2))] if fast else []),
        2 * ROWS * 9 * GW * GW * 3,
        swap, tab, pre, stats_one, mid_norms[0], reduce_low, conv_low, expand, bias, full_mta,
        tap_rows, windows, later, *carried,
    )
    if fast:
        full_out1, full_in2 = (rows[0].reshape(M, C), rows[1].reshape(C, M))

    half = C // 2

    def first_frames(i):
        return (jnp.minimum(i, T - 1), 0, 0)

    def half_frames(i):
        late = i >= 2 * T
        return (
            jnp.where(late, lax.rem(i, T), 0), 0, jnp.where(late, lax.rem(i, 2 * T) // T, 0),
        )

    def last_frames(i):
        return (jnp.where(i >= 3 * T, lax.rem(i, T), 0), 0, 0)

    half_wide = pl.BlockSpec((1, PIX, half), half_frames)
    half_sums = [
        VMEM((2, 2, half), F32), VMEM((2, ndp, 2, half), F32), VMEM((2, ntm, 2, half), F32),
        DMA((2, 4, max(ndp, ntm))),
    ]
    (
        hidden_two, out_low, centred_three, slope, first_two, squares_one, stats_three, stats_alpha,
    ) = pl.pallas_call(
        functools.partial(wide_forward, ndp, ntm),
        name="wide_forward",
        grid=(4 * T,),
        in_specs=[
            SCALARS, SCALARS, pl.BlockSpec((1, PIX, M), first_frames), pair_mid, pair_mid,
            order_spec, fixed((M, C)), half_wide, pair_wide, fixed((C, M)),
        ],
        out_specs=[
            pl.BlockSpec((1, PIX, M), first_frames), half_wide, half_wide, half_wide,
            pl.BlockSpec((1, PIX, M), last_frames), fixed((2, 2, half)), pair_wide, pair_mid,
        ],
        out_shape=[
            shaped((T, PIX, M), BF16), wide_low, wide_low, wide_low, mid_wide,
            shaped((2, 2, half)), shaped((2, C)), shaped((2, M)),
        ],
        scratch_shapes=[
            VMEM((T, PIX, M), BF16), VMEM((2, T, PIX, half), F32), VMEM((T, PIX, M), F32),
            VMEM((2, 2, half), F32),
        ]
        + half_sums
        + swap_scratch(ndp, ntm, (2, M)),
        cost_estimate=pl.CostEstimate(flops=1024, bytes_accessed=1024, transcendentals=0),
        compiler_params=pltpu.CompilerParams(
            vmem_limit_bytes=LIMIT, collective_id=4, has_side_effects=True
        ),
    )(
        swap, tab, agg, stats_two, mid_norms[1], order, full_out1, frames, wide_norms[0], full_in2,
    )

    stride_taps, second_two, stats_beta = stage(
        "mid_two", 6, steps=9, body=mid_two,
        ins=[
            ins_tab, (first_two, fixed((T, PIX, M))), (stats_alpha, pair_mid), mids[2],
            (full_mid2, at_last((M, M))),
        ],
        outs=[
            (shaped((9, HALF_ROWS, M), BF16), at_first((1, HALF_ROWS, M))),
            (shaped((HALF_ROWS, M)), half_mid), LOCAL,
        ],
        scratch=[VMEM((9, HALF_ROWS, M), BF16)], cost=2 * HALF_ROWS * 9 * M * M,
        swap=(swap, QUARTER, (2, M)),
    )

    tile = (HALF_ROWS, WIDE_TILE)
    steps = WIDE_STEPS

    def result_at(i):
        return jnp.clip(i - steps, 0, steps - 1)

    def pair_at(i):
        return jnp.where(i < steps, 0, lax.rem(i, steps))

    many = (steps, 4, WIDE_TILE)
    four_sums = [
        VMEM(many, F32), VMEM((steps, ndp, 4, WIDE_TILE), F32),
        VMEM((steps, ntm, 4, WIDE_TILE), F32), DMA((steps, 4, max(ndp, ntm))),
    ]
    result, grad_w_out2, grad_w_proj, grad_even, grad_beta, squares_last, totals_last, totals_beta = (
        pl.pallas_call(
            functools.partial(middle, ndp, ntm),
            name="middle",
            grid=(3 * steps,),
            in_specs=[
                SCALARS, SCALARS, half_mid, pair_mid, pair_mid,
                ANY, even_spec,
                pl.BlockSpec((4, WIDE_TILE), lambda i: (0, pair_at(i))),
                pl.BlockSpec(tile, lambda i: (0, result_at(i))),
            ],
            out_specs=[
                pl.BlockSpec(tile, lambda i: (0, result_at(i))), ANY, ANY, fixed((HALF_ROWS, C)),
                half_mid, pl.BlockSpec((2, WIDE_TILE), lambda i: (0, result_at(i))),
                fixed((4, C)), pair_mid,
            ],
            out_shape=[
                shaped((HALF_ROWS, C), BF16), shaped((M, C), BF16), shaped((C, C), BF16),
                shaped((HALF_ROWS, C)), shaped((HALF_ROWS, M)), shaped((2, C)), shaped((4, C)),
                shaped((2, M)),
            ],
            scratch_shapes=[
                VMEM((HALF_ROWS, M), BF16), VMEM((steps,) + tile, F32), VMEM((steps,) + tile, F32),
                VMEM((steps,) + tile, F32), VMEM(many, F32), VMEM(many, F32),
                VMEM((HALF_ROWS, M), F32), VMEM((steps,) + tile, BF16),
                VMEM((steps,) + tile, BF16), VMEM((steps, M, WIDE_TILE), BF16),
                VMEM((steps, C, WIDE_TILE), BF16), VMEM((steps, 8, (C + M) // 8, WIDE_TILE), BF16),
                DMA((3, steps)),
            ]
            + four_sums * 2
            + swap_scratch(ndp, ntm, (2, M)),
            cost_estimate=pl.CostEstimate(flops=1024, bytes_accessed=1024, transcendentals=0),
            compiler_params=pltpu.CompilerParams(
                vmem_limit_bytes=LIMIT, collective_id=7, has_side_effects=True
            ),
        )(
            swap, tab, second_two, stats_beta, mid_norms[3], joined, out_low, main_pairs, cotangent,
        )
    )
    if fast:
        proj_part = lax.psum_scatter(grad_w_proj, "dp", scatter_dimension=0, tiled=True)
        cube_out2 = cubed(grad_w_out2)

    def scattered(*pairs):
        if not fast:
            return {}
        return {"items": [item for item, _ in pairs], "sources": [source for _, source in pairs]}

    grad_w_mid2, grad_alpha, totals_alpha = stage(
        "back_mid", 10, steps=9, body=back_mid,
        ins=[
            ins_tab, (grad_beta, half_mid), (second_two, half_mid), (stats_beta, pair_mid),
            mids[3], (totals_beta, pair_mid), (stride_taps, ANY), (full_mid2, at_last((M, M))),
            (first_two, fixed((T, PIX, M))), (stats_alpha, pair_mid), mids[2],
        ],
        outs=[
            (shaped((M, 9 * M), BF16), fixed((M, 9 * M))), (mid_wide, fixed((T, PIX, M))), LOCAL,
        ],
        scratch=[
            VMEM((HALF_ROWS, M), BF16), VMEM((T, PIX, M), F32), VMEM((9, HALF_ROWS, M), BF16),
            DMA, VMEM((HALF_ROWS, M), F32),
        ],
        cost=4 * HALF_ROWS * 9 * M * M, swap=(swap, None, (2, M)),
    )
    cube_mid2 = cubed(grad_w_mid2) if fast else None

    grad_w_in2, grad_before_one, totals_three = stage(
        "back_in_two", 11, steps=T, body=back_in_two,
        ins=[
            ins_tab, (grad_alpha, frame_mid), (first_two, frame_mid), (stats_alpha, pair_mid),
            mids[2], (totals_alpha, pair_mid), (out_low, ANY), (full_in2, fixed((C, M))),
            (grad_even, at_first((QUARTER, C))), (slope, frame_wide), (centred_three, frame_wide),
        ],
        outs=[(shaped((C, M), BF16), fixed((C, M))), (wide_low, frame_wide), LOCAL],
        scratch=[VMEM((T, PIX, M), BF16), VMEM((T, PIX, C), BF16), DMA],
        cost=4 * ROWS * C * M, swap=(swap, None, (2, C)),
    )
    cube_in2 = cubed(grad_w_in2) if fast else None

    grad_w_out1, grad_two, totals_two = stage(
        "back_out_one", 12, steps=T, body=back_out_one,
        ins=[
            ins_tab, (grad_before_one, frame_wide), (centred_three, frame_wide),
            (stats_three, pair_wide), (wide_norms[0], pair_wide), (totals_three, pair_wide),
            (hidden_two, ANY), (full_out1, fixed((M, C))), order_in, (agg, frame_mid),
            (stats_two, pair_mid), mids[1],
        ],
        outs=[(shaped((M, C), BF16), fixed((M, C))), (mid_wide, frame_mid), LOCAL],
        scratch=[VMEM((T, PIX, C), BF16), VMEM((T, PIX, M), BF16), DMA],
        cost=4 * ROWS * C * M, swap=(swap, None, (2, M)),
    )
    cube_out1 = cubed(grad_w_out1) if fast else None

    early = {}
    if fast:
        totals_two, proj_part = lax.optimization_barrier((totals_two, proj_part))
        sent_proj = lax.psum_scatter(proj_part, "tm", scatter_dimension=1, tiled=True)
        early = scattered(
            ((0, 64, 9 * M, 2), cube_mid2), ((0, 256, M, 2), cube_in2),
            ((0, 64, C, 2), cube_out2), ((0, 64, C, 2), cube_out1),
        )
    items = early.get("items", [])
    z_rows = sum(rows * (cols // ntm // GW) for _, rows, cols, _ in items)
    mta_shape = (GW, ntm * edge_wide) if fast else (27, GW, GW)
    (
        grad_one, totals_one, grad_w_mta, grad_reduce, grad_conv, grad_expand, grad_bias, grad_taps,
        *sent_d,
    ) = remote_call(
        "mta_backward",
        functools.partial(mta_backward, ndp, ntm, items, edge if fast else None), 13,
        [SCALARS, ANY, ANY, WHOLE, WHOLE, WHOLE, ANY, WHOLE, WHOLE, WHOLE, ANY, ANY, ANY]
        + [WHOLE] * 8
        + [ANY] * len(items),
        [WHOLE] * (9 if items else 8),
        [
            mid_wide, shaped((2, M)), shaped(mta_shape, BF16), shaped((R, M)),
            shaped((9, R, GW)), shaped((GW, M)), shaped((1, M)), shaped((9, GW)),
        ]
        + ([shaped((ntm, z_rows, GW), BF16)] if items else []),
        [
            VMEM((T, PIX, M), F32), VMEM(frame_low, BF16),
            VMEM((SPAN, PIX + 2 * HW, 3 * GW), BF16), VMEM((CLIPS, SPAN, PIX, GW), F32),
            VMEM((SPAN, PIX, GW), F32),
            VMEM((3, CLIPS, 2, PIX, GW), BF16), VMEM((3, CLIPS, 2, PIX, GW), BF16),
            VMEM((3, 3 * GW, GW), F32), VMEM((9, 8, GW), F32), VMEM((CLIPS, 16, GW), F32),
            VMEM((CLIPS, 16, GW), F32), VMEM((T, 1, M), F32), DMA((10, 2)), DMA((10, 2)),
            VMEM((27, GW, GW), BF16), VMEM((9, 1, GW), F32), VMEM((T, 16, GW), F32),
            VMEM((T, 1, GW), F32), VMEM((T, PIX, M), F32), VMEM((T, PIX, M), F32),
            VMEM((T, PIX, M), F32), VMEM((3, CLIPS, 4, PIX, GW), BF16),
            VMEM((3,) + frame_low, BF16), VMEM((3, 3, 3 * GW, GW), BF16),
            VMEM((T, PIX, M), F32), VMEM((T, PIX, M), F32), DMA((6,)),
        ]
        + swap_scratch(ndp, ntm, (2, M))
        + (scatter_scratch(items, ntm) if items else []),
        4 * ROWS * 9 * GW * GW * 3,
        tab, grad_two, agg, stats_two, mid_norms[1], totals_two, pre, stats_one, mid_norms[0],
        sigma, ext, blended, kernels, tap_rows, reduce_low, conv_low, expand, windows, later,
        snext, pooled, *early.get("sources", []),
    )

    if fast:
        z_part = sent_d[0].reshape(ntm * z_rows, GW)
        sent_z = lax.psum_scatter(z_part, "tm", scatter_dimension=0, tiled=True)
    small_in = [
        grad_reduce, grad_expand, grad_conv, grad_bias, grad_taps, squares_source, squares_one,
        squares_last,
    ]
    small_out = [
        shaped((R, M)), shaped((R, M)), shaped((9, R, GW)), shaped((1, M)), shaped((9, GW)),
        shaped((8, GW)),
    ]
    unit_rows = 8 * ndp * ntm
    rows = -(-384 // unit_rows) * unit_rows
    small_scratch = [VMEM((rows, GW), F32)] * 2 + all_sums_scratch(ndp, ntm, rows)
    frame_scratch = [VMEM((T, PIX, M), BF16), VMEM((T, PIX, C), BF16), DMA]
    if fast:
        late = scattered(((0, 16, ntm * edge_wide, 1), cubed(grad_w_mta)))
        items, own_items = (late["items"], [(0, 256, M, 2)])

        def early_frame(shape):
            return pl.BlockSpec(shape, lambda i: (jnp.minimum(i, T - 1), 0, 0))

        def late_frame(shape):
            return pl.BlockSpec(shape, lambda i: (jnp.maximum(i - T, 0), 0, 0))

        grad_frames, *rest = pl.pallas_call(
            functools.partial(last_part, ndp, ntm, items, own_items),
            name="last_part",
            grid=(2 * T,),
            in_specs=[
                SCALARS, early_frame((1, PIX, M)), early_frame((1, PIX, M)), pair_mid, pair_mid,
                pair_mid, ANY, fixed((C, M)), order_spec, late_frame((1, PIX, C)),
            ]
            + [fixed(part.shape) for part in small_in]
            + [ANY] * len(items),
            out_specs=[late_frame((1, PIX, C))]
            + [fixed(part.shape) for part in small_out]
            + [fixed((rows_, cols // ntm)) for _, rows_, cols, _ in items + own_items],
            out_shape=[wide_low]
            + small_out
            + [shaped((rows_, cols // ntm)) for _, rows_, cols, _ in items + own_items],
            scratch_shapes=frame_scratch
            + [VMEM((2, 2, 2, C // 8, M), BF16)]
            + small_scratch
            + scatter_scratch(items, ntm)
            + scatter_scratch(own_items, ntm),
            cost_estimate=pl.CostEstimate(flops=1024, bytes_accessed=1024, transcendentals=0),
            compiler_params=pltpu.CompilerParams(
                vmem_limit_bytes=LIMIT, collective_id=14, has_side_effects=True
            ),
        )(
            tab, grad_one, pre, stats_one, mid_norms[0], totals_one, frames, full_in1, order,
            grad_before_one, *small_in, *late["sources"],
        )
        small_sums, sent_f = (rest[:6], rest[6:])
    else:
        grad_w_in1, grad_frames = stage(
            "back_in_one", 14, steps=T, body=back_in_one,
            ins=[
                ins_tab, (grad_one, frame_mid), (pre, frame_mid), (stats_one, pair_mid), mids[0],
                (totals_one, pair_mid), (frames, ANY), (full_in1, fixed((C, M))), order_in,
                (grad_before_one, frame_wide),
            ],
            outs=[(shaped((C, M), BF16), fixed((C, M))), (wide_low, frame_wide)],
            scratch=frame_scratch, cost=4 * ROWS * C * M,
        )
        small_sums = remote_call(
            "final_sums", functools.partial(final_sums, ndp, ntm), 15, [WHOLE] * 8, [WHOLE] * 6,
            small_out, small_scratch, 1 << 26, *small_in,
        )
    totals = (totals_one, totals_two, totals_alpha, totals_beta, totals_three, totals_last)
    if not fast:
        grad_w_mta = jnp.transpose(grad_w_mta, (1, 0, 2)).reshape(GW, 27 * GW)
        delivered = [
            deliver(g)
            for g in (
                grad_w_in1, grad_w_mta, grad_w_out1, grad_w_in2, grad_w_mid2, grad_w_out2,
                grad_w_proj,
            )
        ]
        swap = jnp.broadcast_to(total, (8, GW))
    wrapped = [*small_sums, swap, *totals]
    copied = []
    if fast:
        wrapped += [*sent_f, sent_proj, sent_z]
        copied = [result, grad_frames]
    shards = [
        shaped(shard.shape) for shard in (w_in1, w_mta, w_out1, w_in2, w_mid2, w_out2, w_proj)
    ]
    wrap_out = [
        shaped((4, 2, M)), shaped((3, 2, C)), shaped((3, 3, GW)), shaped((R, M)),
        shaped((9, R, R)), shaped((R, M)), shaped((1, M)), shaped((1, 5)),
    ]
    wrap_out += shards if fast else []
    (
        out_mid, out_wide, out_taps, out_reduce, out_conv, out_expand, out_bias, out_rms, *rest,
    ) = pl.pallas_call(
        functools.partial(wrap, fast),
        name="wrap",
        in_specs=[WHOLE] * len(wrapped) + [ANY] * len(copied),
        out_specs=[WHOLE] * len(wrap_out) + [ANY] * len(copied),
        out_shape=wrap_out + [shaped(part.shape, BF16) for part in copied],
        scratch_shapes=[VMEM(part.shape, BF16) for part in copied]
        + ([DMA((2, 2, T))] if fast else []),
        compiler_params=pltpu.CompilerParams(vmem_limit_bytes=LIMIT),
    )(*wrapped, *copied)
    if fast:
        *delivered, result, grad_frames = rest
    return (
        result.reshape(grad_out.shape),
        grad_frames.reshape(video.shape),
        out_mid,
        out_wide,
        out_taps,
        out_reduce.T,
        out_conv.reshape(3, 3, R, R),
        out_expand,
        out_bias.reshape(M),
        *delivered,
        out_rms.reshape(5),
    )


def solution(mesh):
    clip_spec = P("dp", "tm", None, None, None)
    return jax.shard_map(
        local,
        mesh=mesh,
        in_specs=(clip_spec,) + (P(),) * 8 + (P("dp", "tm"),) * 7 + (clip_spec,),
        out_specs=(clip_spec,) * 2 + (P(),) * 7 + (P("dp", "tm"),) * 7 + (P(),),
        check_vma=False,
    )
```
